32 devices in a mesh: seq: 4 (over z), exp: 8 (over y, x, core).
Axes of the slice: x: 2, y: 2, z: 4, core: 2. Of those that a mesh axis runs over, the one named last changes fastest.
Arguments:
- tokens: bfloat16 [8192, 4096], P(('seq', 'exp')), may hold values from -3 to 3
- cotangent: bfloat16 [8192, 4096], P(('seq', 'exp')), may hold values from -2 to 2
- router: bfloat16 [4096, 8], replicated, may hold values from -0.09375 to 0.09375
- threshold: float32 [8], replicated, may hold values from -1 to 1
- w_gate: bfloat16 [8, 4096, 1536], P('exp', None, 'seq'), may hold values from -0.09375 to 0.09375
- w_up: bfloat16 [8, 4096, 1536], P('exp', None, 'seq'), may hold values from -0.09375 to 0.09375
- w_down: bfloat16 [8, 1536, 4096], P('exp', 'seq'), may hold values from -0.15625 to 0.15625
- hid_scale: float32 [8, 1536], P('exp', 'seq'), may hold values from 0.5 to 2
- picks: int32 [32, 8, 4], P(('seq', 'exp')), may hold values from 0 to 255, as said below
- counts: int32 [32, 8], P(('seq', 'exp')), may hold values from 1 to 4, as said below
Outputs:
- mixture: bfloat16 [8192, 4096], P(('seq', 'exp'))
- token_grad: bfloat16 [8192, 4096], P(('seq', 'exp'))
- router_grad: float32 [4096, 8], P(('seq', 'exp'))
- threshold_grad: float32 [8], replicated
- gate_grad: float32 [8, 4096, 1536], P('exp', None, 'seq')
- up_grad: float32 [8, 4096, 1536], P('exp', None, 'seq')
- down_grad: float32 [8, 1536, 4096], P('exp', 'seq')
The draws below stay inside these ranges and needn't reach their ends.
Inputs may be any that keep to these rules, and one draw needn't show every extreme that they name: Each list picks[p, e] holds 4 distinct local rows of owner p. `counts`: for every expert some owner fills all 4 slots.
All inputs are finite; a program needn't handle non-finite values.
Results may differ from the reference program's by a relative error of at most 0.018.
Values may be sent and summed in bfloat16 or wider, within the bound.
No kernel may reach another device: no remote copies, remote signals or barrier semaphores. Data moves between devices by JAX's collectives and lax.ppermute only.
A program may use at most 128 MiB of HBM per device.

```python
import math
import jax
import jax.numpy as jnp
from jax import lax

D = 4096
HID = 1536
TOK_DEV = 256
SLOT = 4
EXPERTS = 8
OWNERS = 32
TOKENS = 8192
N_SEQ = 4


def draw_picks(key, part):
    noise = jax.random.randint(jax.random.fold_in(key, 11), (OWNERS, EXPERTS, TOK_DEV), 0, 2 ** 20)
    order = noise * TOK_DEV + jnp.arange(TOK_DEV, dtype=jnp.int32)[None, None, :]
    ranked = jnp.argsort(order, axis=-1)
    return ranked[:, :, :SLOT].astype(jnp.int32)


def draw_counts(key, part):
    filled = jax.random.randint(jax.random.fold_in(key, 21), (OWNERS, EXPERTS), 1, SLOT + 1)
    fullest = jax.random.randint(jax.random.fold_in(key, 22), (EXPERTS,), 0, OWNERS)
    owner_ids = jnp.arange(OWNERS, dtype=jnp.int32)[:, None]
    return jnp.where(owner_ids == fullest[None, :], SLOT, filled).astype(jnp.int32)


def shard_levels(own_key, extent, cuts, least, high):
    level = 1.0
    for position, blocks in cuts:
        steps = jax.random.uniform(jax.random.fold_in(jax.random.fold_in(own_key, 6), position), (blocks,), jnp.float32, least / len(cuts), high / len(cuts))
        level = level * jnp.repeat(jnp.exp(steps), extent[position] // blocks).reshape((-1,) + (1,) * (len(extent) - 1 - position))
    return level


def centred(stream_key, extent, spread, bound, pieces=(), held_as=jnp.bfloat16):
    gain = shard_levels(stream_key, extent, pieces, -0.22, 0.18) if pieces else 1.0
    entries = jax.random.normal(stream_key, extent, jnp.float32) * spread * gain
    return jnp.minimum(jnp.maximum(entries, -bound), bound).astype(held_as)


def setup_inputs(seed: int = 0) -> dict:
    seeds = jax.random.split(jax.random.key(seed), 11)
    tokens = centred(seeds[0], (TOKENS, D), 1.0, 3.0, ((0, 32),))
    cotangent = centred(seeds[1], (TOKENS, D), 0.5, 2.0, ((0, 32),))
    router = centred(seeds[2], (D, EXPERTS), D ** -0.5, 0.09375)
    threshold = jnp.clip(jax.random.uniform(seeds[3], (EXPERTS,), jnp.float32, -1.0, 1.0), -1.0, 1.0)
    w_gate = centred(seeds[4], (EXPERTS, D, HID), D ** -0.5, 0.09375, ((0, 8), (2, 4)))
    w_up = centred(seeds[5], (EXPERTS, D, HID), D ** -0.5, 0.09375, ((0, 8), (2, 4)))
    w_down = centred(seeds[6], (EXPERTS, HID, D), HID ** -0.5, 0.15625, ((0, 8), (1, 4)))
    hid_scale = jnp.clip(jnp.exp(math.log(2.0) - 1.3862944 * jax.random.uniform(seeds[7], (EXPERTS, HID), jnp.float32) ** shard_levels(seeds[7], (EXPERTS, HID), ((0, 8), (1, 4)), -0.2, 0.2)), 0.5, 2.0)
    picks = draw_picks(jax.random.fold_in(seeds[10], 71), 0)
    counts = draw_counts(jax.random.fold_in(seeds[10], 71), 0)
    return dict(tokens=tokens, cotangent=cotangent, router=router, threshold=threshold, w_gate=w_gate, w_up=w_up, w_down=w_down, hid_scale=hid_scale, picks=picks, counts=counts)


def group_sum(left, right):
    group_size = left.shape[1] // N_SEQ
    left_parts = left.astype(jnp.float32).reshape(left.shape[0], N_SEQ, group_size)
    right_parts = right.astype(jnp.float32).reshape(N_SEQ, group_size, right.shape[1])
    parts = jnp.einsum("rsh,shd->rsd", left_parts, right_parts, precision=lax.Precision.HIGHEST)
    return jnp.sum(parts.astype(jnp.bfloat16).astype(jnp.float32), axis=1).astype(jnp.bfloat16)


def group_back(gate_delta, up_delta, gate_mat, up_mat):
    group_size = gate_delta.shape[1] // N_SEQ
    row_total = gate_delta.shape[0]
    gate_parts = gate_delta.astype(jnp.float32).reshape(row_total, N_SEQ, group_size)
    up_parts = up_delta.astype(jnp.float32).reshape(row_total, N_SEQ, group_size)
    gate_w = gate_mat.astype(jnp.float32).reshape(gate_mat.shape[0], N_SEQ, group_size)
    up_w = up_mat.astype(jnp.float32).reshape(up_mat.shape[0], N_SEQ, group_size)
    parts = jnp.einsum("rsh,dsh->rsd", gate_parts, gate_w, precision=lax.Precision.HIGHEST)
    parts = parts + jnp.einsum("rsh,dsh->rsd", up_parts, up_w, precision=lax.Precision.HIGHEST)
    return jnp.sum(parts.astype(jnp.bfloat16).astype(jnp.float32), axis=1).astype(jnp.bfloat16)


def reference(tokens, cotangent, router, threshold, w_gate, w_up, w_down, hid_scale, picks, counts):
    scores = jnp.dot(tokens, router, preferred_element_type=jnp.float32)
    gates = jax.nn.sigmoid(scores - threshold[None, :])
    owner_count = picks.shape[0]
    slot_count = picks.shape[2]
    expert_count = router.shape[1]
    owner_base = jnp.arange(owner_count, dtype=jnp.int32)[:, None] * TOK_DEV
    mixture = jnp.zeros(tokens.shape, jnp.float32)
    returned_sum = jnp.zeros(tokens.shape, jnp.float32)
    score_grad = jnp.zeros((tokens.shape[0], expert_count), jnp.float32)
    gate_list = []
    up_list = []
    down_list = []
    for expert in range(expert_count):
        row_index = (owner_base + picks[:, expert, :]).astype(jnp.int32).reshape(-1)
        active = (jnp.arange(slot_count, dtype=jnp.int32)[None, :] < counts[:, expert][:, None]).astype(jnp.float32).reshape(-1)
        exp_rows = tokens[row_index]
        raw_gate = gates[row_index, expert]
        gate_value = raw_gate * active
        cot_rows = cotangent[row_index].astype(jnp.float32)
        scaled_cot = (cot_rows * gate_value[:, None]).astype(jnp.bfloat16)
        pre_gate = jnp.dot(exp_rows, w_gate[expert], preferred_element_type=jnp.float32)
        pre_up = jnp.dot(exp_rows, w_up[expert], preferred_element_type=jnp.float32)
        sigmoid_val = jax.nn.sigmoid(pre_gate)
        activated = pre_gate * sigmoid_val
        hidden = (activated * pre_up * hid_scale[expert][None, :]).astype(jnp.bfloat16)
        expert_out = group_sum(hidden, w_down[expert])
        out_wide = expert_out.astype(jnp.float32)
        mixture = mixture.at[row_index].add(gate_value[:, None] * out_wide)
        hidden_grad = jnp.dot(scaled_cot, w_down[expert].T, preferred_element_type=jnp.float32)
        scaled_grad = hidden_grad * hid_scale[expert][None, :]
        gate_delta = (scaled_grad * pre_up * sigmoid_val * (1.0 + pre_gate * (1.0 - sigmoid_val))).astype(jnp.bfloat16)
        up_delta = (scaled_grad * activated).astype(jnp.bfloat16)
        down_list.append(jnp.dot(hidden.T, scaled_cot, preferred_element_type=jnp.float32))
        gate_list.append(jnp.dot(exp_rows.T, gate_delta, preferred_element_type=jnp.float32))
        up_list.append(jnp.dot(exp_rows.T, up_delta, preferred_element_type=jnp.float32))
        row_grad = group_back(gate_delta, up_delta, w_gate[expert], w_up[expert])
        returned_sum = returned_sum.at[row_index].add(row_grad.astype(jnp.float32))
        gate_pull = active * jnp.sum(cot_rows * out_wide, axis=-1)
        score_grad = score_grad.at[row_index, expert].add(gate_pull * raw_gate * (1.0 - raw_gate))
    token_grad = returned_sum + jnp.dot(score_grad, router.astype(jnp.float32).T, precision=lax.Precision.HIGHEST)
    router_grad = jnp.dot(tokens.astype(jnp.float32).T, score_grad, precision=lax.Precision.HIGHEST)
    threshold_grad = -jnp.sum(score_grad, axis=0)
    return (mixture.astype(jnp.bfloat16), token_grad.astype(jnp.bfloat16), router_grad, threshold_grad,
            jnp.stack(gate_list), jnp.stack(up_list), jnp.stack(down_list))
```

```python
import jax
import jax.numpy as jnp
from jax import lax
from jax.sharding import PartitionSpec as P

BOTH = ("seq", "exp")
F32 = jnp.float32
BF16 = jnp.bfloat16


def mm(a, b, dims=((1,), (0,))):
    return lax.dot_general(a, b, (dims, ((), ())), preferred_element_type=F32)


def split3(v):
    hi = lax.reduce_precision(v, 8, 7)
    rest = v - hi
    mid = lax.reduce_precision(rest, 8, 7)
    low = rest - mid
    return [part.astype(BF16) for part in (hi, mid, low)]


def on_device(tokens, cotangent, router, threshold, w_gate, w_up, w_down, hid_scale, picks, counts):
    experts, slots = picks.shape[1:]
    own, features = tokens.shape
    seq_n = lax.axis_size("seq")
    everyone = seq_n * lax.axis_size("exp")
    expert = lax.axis_index("exp")

    live = jnp.arange(slots, dtype=jnp.int32)[None, :] < counts[0][:, None]
    flat = picks[0].reshape(-1)
    hit = flat[:, None] == jnp.arange(own, dtype=jnp.int32)[None, :]
    hit_live = (hit & live.reshape(-1)[:, None]).astype(BF16)
    hit = hit.astype(BF16)

    def dispatch(chooser, rows):
        many = jnp.tile(chooser, (seq_n, 1))
        sent = mm(many, rows).astype(BF16).reshape(everyone, slots, features)
        return lax.all_to_all(sent, BOTH, split_axis=0, concat_axis=0, tiled=True).reshape(-1, features)

    def bring_back(rows):
        sent = rows.reshape(everyone, slots, features)
        back = lax.all_to_all(sent, BOTH, split_axis=0, concat_axis=0, tiled=True).reshape(-1, features)
        return mm(jnp.tile(hit_live, (seq_n, 1)), back, ((0,), (0,))).astype(BF16)

    rows = dispatch(hit, tokens)
    cots = dispatch(hit_live, cotangent)

    gate_mat, up_mat, down_mat = w_gate[0], w_up[0], w_down[0]
    scale = hid_scale[0][None, :]
    column = lax.dynamic_slice_in_dim(router, expert, 1, axis=1)
    gates = jax.nn.sigmoid(mm(rows, column) - lax.dynamic_slice_in_dim(threshold, expert, 1)[None, :])
    pre_gate = mm(rows, gate_mat)
    pre_up = mm(rows, up_mat)
    sig = jax.nn.sigmoid(pre_gate)
    act = pre_gate * sig
    hidden = (act * pre_up * scale).astype(BF16)
    out = mm(hidden, down_mat)
    mixture = bring_back((out * gates).astype(BF16))

    cots_wide = cots.astype(F32)
    scaled = (cots_wide * gates).astype(BF16)
    grad = mm(scaled, down_mat, ((1,), (1,))) * scale
    gate_delta = (grad * pre_up * sig * (1.0 + pre_gate * (1.0 - sig))).astype(BF16)
    up_delta = (grad * act).astype(BF16)
    score = jnp.sum(cots_wide * out, axis=1, keepdims=True) * gates * (1.0 - gates)
    back = mm(gate_delta, gate_mat, ((1,), (1,))) + mm(up_delta, up_mat, ((1,), (1,)))
    back = back + score * column.astype(F32).reshape(1, -1)
    token_grad = bring_back(back.astype(BF16))

    parts = jnp.concatenate(split3(score), axis=1)
    router_part = jnp.sum(mm(parts, rows, ((0,), (0,))), axis=0)
    message = jnp.concatenate(
        [router_part.reshape(everyone, -1), jnp.broadcast_to(-jnp.sum(score), (everyone, 1))], axis=1
    )
    told = lax.all_to_all(message, BOTH, split_axis=0, concat_axis=0, tiled=True)
    told = jnp.sum(told.reshape(seq_n, experts, -1), axis=0)
    router_grad = told[:, :-1].T
    threshold_grad = told[:, -1]

    gate_grad = mm(rows, gate_delta, ((0,), (0,)))
    up_grad = mm(rows, up_delta, ((0,), (0,)))
    down_grad = mm(hidden, scaled, ((0,), (0,)))
    return (
        mixture,
        token_grad,
        router_grad,
        threshold_grad,
        gate_grad[None],
        up_grad[None],
        down_grad[None],
    )


def solution(mesh):
    by_owner = P(BOTH, None)
    columns = P("exp", None, "seq")
    down = P("exp", "seq", None)
    return jax.shard_map(
        on_device,
        mesh=mesh,
        in_specs=(
            by_owner,
            by_owner,
            P(),
            P(),
            columns,
            columns,
            down,
            P("exp", "seq"),
            P(BOTH, None, None),
            by_owner,
        ),
        out_specs=(by_owner, by_owner, by_owner, P(), columns, columns, down),
        check_vma=False,
    )
```

```python
import functools

import jax
import jax.numpy as jnp
from jax import lax
from jax.experimental import pallas as pl
from jax.experimental.pallas import tpu as pltpu
from jax.sharding import PartitionSpec as P

BOTH = ("seq", "exp")
F32 = jnp.float32
BF16 = jnp.bfloat16
ROWS = ((0,), (0,))
LAST = ((1,), (1,))
STEPS = 4
PARAMS = pltpu.CompilerParams(vmem_limit_bytes=40 * 2**20)


def mm(a, b, dims=((1,), (0,))):
    return lax.dot_general(a, b, (dims, ((), ())), preferred_element_type=F32)


def spec(block, index):
    return pl.BlockSpec(block, index)


def whole(shape):
    return pl.BlockSpec(shape, lambda *_: (0,) * len(shape))


def in_smem():
    return pl.BlockSpec(memory_space=pltpu.SMEM)


def choosers(picks_ref, counts_ref, own, pack, only_live):
    slots, experts = picks_ref.shape
    shape = (experts * pack * slots, own)
    row = lax.broadcasted_iota(jnp.int32, shape, 0)
    token = lax.broadcasted_iota(jnp.int32, shape, 1)
    expert = row // (pack * slots)
    slot = row % slots
    part = (row // slots) % pack
    want = jnp.full(shape, -1, jnp.int32)
    for e in range(experts):
        for k in range(slots):
            pick = picks_ref[k, e]
            if only_live:
                pick = jnp.where(k < counts_ref[0, e], pick, -1)
            want = jnp.where((expert == e) & (slot == k), pick, want)
    return [jnp.where((want == token) & (part == h), 1.0, 0.0).astype(BF16) for h in range(pack)]


def choose_rows(rows, picks, counts, pack, only_live):
    own, features = rows.shape
    slots, experts = picks.shape
    count = experts * pack * slots
    width = features // pack // STEPS

    def body(picks_ref, counts_ref, *refs):
        parts, out_ref, one_hot = refs[:pack], refs[pack], refs[pack + 1]

        @pl.when(pl.program_id(0) == 0)
        def _():
            for h, chooser in enumerate(choosers(picks_ref, counts_ref, own, pack, only_live)):
                one_hot[h] = chooser

        out_ref[...] = sum(mm(one_hot[h], parts[h][...]) for h in range(pack)).astype(BF16)

    return pl.pallas_call(
        body,
        grid=(STEPS,),
        in_specs=[in_smem(), in_smem()]
        + [spec((own, width), lambda i, h=h: (0, h * STEPS + i)) for h in range(pack)],
        out_specs=spec((count, width), lambda i: (0, i)),
        out_shape=jax.ShapeDtypeStruct((count, features // pack), BF16),
        scratch_shapes=[pltpu.VMEM((pack, count, own), BF16)],
        compiler_params=PARAMS,
        cost_estimate=pl.CostEstimate(
            flops=2 * count * own * features, bytes_accessed=2 * features * own, transcendentals=0
        ),
    )(picks, counts, *([rows] * pack))


def scatter_rows(back, picks, counts, own, pack):
    count, part_width = back.shape
    width = part_width // STEPS

    def body(picks_ref, counts_ref, back_ref, out_ref, one_hot):
        @pl.when((pl.program_id(0) == 0) & (pl.program_id(1) == 0))
        def _():
            for h, chooser in enumerate(choosers(picks_ref, counts_ref, own, pack, True)):
                one_hot[h] = chooser

        out_ref[...] = mm(one_hot[pl.program_id(0)], back_ref[...], ROWS).astype(BF16)

    return pl.pallas_call(
        body,
        grid=(pack, STEPS),
        in_specs=[in_smem(), in_smem(), spec((count, width), lambda h, i: (0, i))],
        out_specs=spec((own, width), lambda h, i: (0, h * STEPS + i)),
        out_shape=jax.ShapeDtypeStruct((own, part_width * pack), BF16),
        scratch_shapes=[pltpu.VMEM((pack, count, own), BF16)],
        compiler_params=PARAMS,
        cost_estimate=pl.CostEstimate(
            flops=2 * count * own * part_width * pack,
            bytes_accessed=2 * part_width * pack * own,
            transcendentals=0,
        ),
    )(picks, counts, back)


def first_part(rows, pack, slots):
    row = lax.broadcasted_iota(jnp.int32, (rows, 1), 0)
    return (row // slots) % pack == 0


def fold(parts, slots):
    rows = parts[0].shape[0]
    total = parts[0]
    for h in range(1, len(parts)):
        total = total + pltpu.roll(parts[h], rows - h * slots, 0)
    return total


def spread(value, pack, slots):
    return [value if h == 0 else pltpu.roll(value, h * slots, 0) for h in range(pack)]


def arrange(refs):
    near = len(refs) // 2
    blocks = [refs[0][...]]
    for k in range(1, near + 1):
        blocks.append(refs[k][...] + refs[2 * near + 1 - k][...])
    return jnp.concatenate(blocks, axis=0)


def expert_forward(blocks, seq_n, slots, pack, router, threshold, w_gate, w_up, w_down, hid_scale):
    block_rows, part_width = blocks[0].shape
    rows = block_rows * seq_n
    hidden_n = w_gate.shape[2]
    experts = router.shape[1]
    width = part_width // STEPS
    ready = STEPS - 1

    def first(i):
        return jnp.minimum(i, ready)

    def second(i):
        return jnp.maximum(i - STEPS, 0)

    n_blocks = len(blocks)

    def body(*refs):
        refs = list(refs)
        block_refs = [refs.pop(0) for _ in range(n_blocks)]
        router_refs = [refs.pop(0) for _ in range(pack)]
        gate_refs = [refs.pop(0) for _ in range(pack)]
        up_refs = [refs.pop(0) for _ in range(pack)]
        down_refs = [refs.pop(0) for _ in range(pack)]
        threshold_ref, scale_ref = refs.pop(0), refs.pop(0)
        x_ref, gate_ref, up_ref, g_ref, hidden_ref = [refs.pop(0) for _ in range(5)]
        out_refs = [refs.pop(0) for _ in range(seq_n)]
        acc_gate, acc_up, acc_score = refs
        i = pl.program_id(0)

        @pl.when(i == 0)
        def _():
            acc_gate[...] = jnp.zeros_like(acc_gate)
            acc_up[...] = jnp.zeros_like(acc_up)
            acc_score[...] = jnp.zeros_like(acc_score)

        @pl.when(i < STEPS)
        def _():
            x = arrange(block_refs)
            x_ref[...] = x
            for h in range(pack):
                acc_score[h] += mm(x, router_refs[h][...])
                acc_gate[h] += mm(x, gate_refs[h][...])
                acc_up[h] += mm(x, up_refs[h][...])

        @pl.when(i == ready)
        def _():
            mine = lax.broadcasted_iota(jnp.int32, (rows, experts), 1) == lax.axis_index("exp")
            score = fold([acc_score[h] for h in range(pack)], slots) - threshold_ref[...]
            g = jax.nn.sigmoid(jnp.sum(jnp.where(mine, score, 0.0), axis=1, keepdims=True))
            g_ref[...] = jnp.broadcast_to(g, g_ref.shape)
            gate = fold([acc_gate[h] for h in range(pack)], slots)
            up = fold([acc_up[h] for h in range(pack)], slots)
            gate_ref[...] = gate
            up_ref[...] = up
            hidden = gate * jax.nn.sigmoid(gate) * up * scale_ref[...] * g
            hidden = jnp.where(first_part(rows, pack, slots), hidden, 0.0)
            for h, value in enumerate(spread(hidden, pack, slots)):
                hidden_ref[h] = value.astype(BF16)

        @pl.when(i >= STEPS)
        def _():
            out = sum(mm(hidden_ref[h], down_refs[h][...]) for h in range(pack)).astype(BF16)
            for k in range(seq_n):
                out_refs[k][...] = out[k * block_rows : (k + 1) * block_rows]

    in_specs = (
        [spec((block_rows, width), lambda i: (0, first(i))) for _ in blocks]
        + [spec((width, experts), lambda i, h=h: (h * STEPS + first(i), 0)) for h in range(pack)]
        + [spec((None, width, hidden_n), lambda i, h=h: (0, h * STEPS + first(i), 0)) for h in range(pack)] * 2
        + [spec((None, hidden_n, width), lambda i, h=h: (0, 0, h * STEPS + second(i))) for h in range(pack)]
        + [whole((1, experts)), whole((1, hidden_n))]
    )
    out_specs = [
        spec((rows, width), lambda i: (0, first(i))),
        whole((rows, hidden_n)),
        whole((rows, hidden_n)),
        whole((rows, 128)),
        whole((pack, rows, hidden_n)),
    ] + [spec((block_rows, width), lambda i: (0, second(i)))] * seq_n
    out_shape = [
        jax.ShapeDtypeStruct((rows, part_width), BF16),
        jax.ShapeDtypeStruct((rows, hidden_n), F32),
        jax.ShapeDtypeStruct((rows, hidden_n), F32),
        jax.ShapeDtypeStruct((rows, 128), F32),
        jax.ShapeDtypeStruct((pack, rows, hidden_n), BF16),
    ] + [jax.ShapeDtypeStruct((block_rows, part_width), BF16)] * seq_n
    return pl.pallas_call(
        body,
        grid=(2 * STEPS,),
        in_specs=in_specs,
        out_specs=out_specs,
        out_shape=out_shape,
        scratch_shapes=[
            pltpu.VMEM((pack, rows, hidden_n), F32),
            pltpu.VMEM((pack, rows, hidden_n), F32),
            pltpu.VMEM((pack, rows, experts), F32),
        ],
        compiler_params=PARAMS,
        cost_estimate=pl.CostEstimate(
            flops=6 * rows * part_width * pack * hidden_n,
            bytes_accessed=6 * part_width * pack * hidden_n,
            transcendentals=0,
        ),
    )(
        *blocks,
        *([router] * pack),
        *([w_gate] * pack),
        *([w_up] * pack),
        *([w_down] * pack),
        threshold.reshape(1, -1),
        hid_scale,
    )


def split3(v):
    hi = v.astype(BF16)
    rest = v - hi.astype(F32)
    mid = rest.astype(BF16)
    return hi, mid, (rest - mid.astype(F32)).astype(BF16)


def expert_backward(blocks, seq_n, slots, pack, x, pre_gate, pre_up, gates, router, w_gate, w_up, w_down, hid_scale):
    block_rows, part_width = blocks[0].shape
    rows = block_rows * seq_n
    hidden_n = w_gate.shape[2]
    experts = router.shape[1]
    width = part_width // STEPS
    ready = STEPS - 1

    def first(i):
        return jnp.minimum(i, ready)

    def second(i):
        return jnp.maximum(i - STEPS, 0)

    n_blocks = len(blocks)

    def body(*refs):
        refs = list(refs)
        block_refs = [refs.pop(0) for _ in range(n_blocks)]
        router_refs = [refs.pop(0) for _ in range(pack)]
        gate_refs = [refs.pop(0) for _ in range(pack)]
        up_refs = [refs.pop(0) for _ in range(pack)]
        down_refs = [refs.pop(0) for _ in range(pack)]
        scale_ref, x_ref, pre_gate_ref, pre_up_ref, g_ref = [refs.pop(0) for _ in range(5)]
        c_ref, gate_delta, up_delta, router_ref, total_ref = [refs.pop(0) for _ in range(5)]
        out_refs = [refs.pop(0) for _ in range(seq_n)]
        acc, columns = refs
        i = pl.program_id(0)

        @pl.when(i == 0)
        def _():
            acc[...] = jnp.zeros_like(acc)

        @pl.when(i < STEPS)
        def _():
            c = arrange(block_refs)
            c_ref[...] = c
            for h in range(pack):
                acc[h] += mm(c, down_refs[h][...], LAST)

        @pl.when(i == ready)
        def _():
            keep = first_part(rows, pack, slots)
            raw = fold([acc[h] for h in range(pack)], slots) * scale_ref[...]
            raw = jnp.where(keep, raw, 0.0)
            g = g_ref[:, :1]
            gate = pre_gate_ref[...]
            up = pre_up_ref[...]
            sig = jax.nn.sigmoid(gate)
            act = gate * sig
            score = jnp.sum(act * up * raw, axis=1, keepdims=True) * g * (1.0 - g)
            grad = raw * g
            to_gate = grad * up * sig * (1.0 + gate * (1.0 - sig))
            to_up = grad * act
            mine = lax.broadcasted_iota(jnp.int32, (rows, experts), 1) == lax.axis_index("exp")
            for h, value in enumerate(spread(to_gate, pack, slots)):
                gate_delta[h] = value.astype(BF16)
            for h, value in enumerate(spread(to_up, pack, slots)):
                up_delta[h] = value.astype(BF16)
            column = jnp.where(mine, score, 0.0)
            for h, value in enumerate(spread(column, pack, slots)):
                for n, piece in enumerate(split3(value)):
                    columns[h, n] = piece
            total_ref[...] = jnp.broadcast_to(-jnp.sum(score, axis=0, keepdims=True), total_ref.shape)

        @pl.when(i >= STEPS)
        def _():
            out = jnp.zeros((rows, width), F32)
            x_now = x_ref[...]
            for h in range(pack):
                out = out + mm(gate_delta[h], gate_refs[h][...], LAST)
                out = out + mm(up_delta[h], up_refs[h][...], LAST)
                out = out + mm(columns[h, 0], router_refs[h][...], LAST)
                out = out + mm(columns[h, 1], router_refs[h][...], LAST)
                part = sum(mm(columns[h, n], x_now, ROWS) for n in range(3))
                router_ref[h : h + 1, :] = jnp.sum(part, axis=0, keepdims=True)
            out = out.astype(BF16)
            for k in range(seq_n):
                out_refs[k][...] = out[k * block_rows : (k + 1) * block_rows]

    in_specs = (
        [spec((block_rows, width), lambda i: (0, first(i))) for _ in blocks]
        + [spec((width, experts), lambda i, h=h: (h * STEPS + second(i), 0)) for h in range(pack)]
        + [spec((None, width, hidden_n), lambda i, h=h: (0, h * STEPS + second(i), 0)) for h in range(pack)] * 2
        + [spec((None, hidden_n, width), lambda i, h=h: (0, 0, h * STEPS + first(i))) for h in range(pack)]
        + [
            whole((1, hidden_n)),
            spec((rows, width), lambda i: (0, second(i))),
            whole((rows, hidden_n)),
            whole((rows, hidden_n)),
            whole((rows, 128)),
        ]
    )
    out_specs = [
        spec((rows, width), lambda i: (0, first(i))),
        whole((pack, rows, hidden_n)),
        whole((pack, rows, hidden_n)),
        spec((pack, width), lambda i: (0, second(i))),
        whole((1, 128)),
    ] + [spec((block_rows, width), lambda i: (0, second(i)))] * seq_n
    out_shape = [
        jax.ShapeDtypeStruct((rows, part_width), BF16),
        jax.ShapeDtypeStruct((pack, rows, hidden_n), BF16),
        jax.ShapeDtypeStruct((pack, rows, hidden_n), BF16),
        jax.ShapeDtypeStruct((pack, part_width), F32),
        jax.ShapeDtypeStruct((1, 128), F32),
    ] + [jax.ShapeDtypeStruct((block_rows, part_width), BF16)] * seq_n
    return pl.pallas_call(
        body,
        grid=(2 * STEPS,),
        in_specs=in_specs,
        out_specs=out_specs,
        out_shape=out_shape,
        scratch_shapes=[
            pltpu.VMEM((pack, rows, hidden_n), F32),
            pltpu.VMEM((pack, 3, rows, experts), BF16),
        ],
        compiler_params=PARAMS,
        cost_estimate=pl.CostEstimate(
            flops=6 * rows * part_width * pack * hidden_n,
            bytes_accessed=6 * part_width * pack * hidden_n,
            transcendentals=0,
        ),
    )(
        *blocks,
        *([router] * pack),
        *([w_gate] * pack),
        *([w_up] * pack),
        *([w_down] * pack),
        hid_scale,
        x,
        pre_gate,
        pre_up,
        gates,
    )


def weight_grads(x, c, hidden, gate_delta, up_delta):
    rows, part_width = x.shape
    pack, _, hidden_n = hidden.shape
    width = part_width // STEPS

    def body(x_ref, c_ref, hidden_ref, gate_ref, up_ref, gate_out, up_out, down_out):
        x_now = x_ref[...]
        gate_out[...] = mm(x_now, gate_ref[...], ROWS)
        up_out[...] = mm(x_now, up_ref[...], ROWS)
        down_out[...] = mm(hidden_ref[...], c_ref[...], ROWS)

    part = spec((None, rows, hidden_n), lambda h, i: (h, 0, 0))
    tall = spec((None, width, hidden_n), lambda h, i: (0, h * STEPS + i, 0))
    return pl.pallas_call(
        body,
        grid=(pack, STEPS),
        in_specs=[spec((rows, width), lambda h, i: (0, i))] * 2 + [part] * 3,
        out_specs=[tall, tall, spec((None, hidden_n, width), lambda h, i: (0, 0, h * STEPS + i))],
        out_shape=[
            jax.ShapeDtypeStruct((1, part_width * pack, hidden_n), F32),
            jax.ShapeDtypeStruct((1, part_width * pack, hidden_n), F32),
            jax.ShapeDtypeStruct((1, hidden_n, part_width * pack), F32),
        ],
        compiler_params=PARAMS,
        cost_estimate=pl.CostEstimate(
            flops=6 * rows * part_width * pack * hidden_n,
            bytes_accessed=12 * part_width * pack * hidden_n,
            transcendentals=0,
        ),
    )(x, c, hidden, gate_delta, up_delta)


def line_gather(block, n):
    rights, lefts = [], []
    right = left = block
    for j in range(1, n):
        right = lax.ppermute(right, "seq", [(s, s + 1) for s in range(j - 1, n - 1)])
        left = lax.ppermute(left, "seq", [(s, s - 1) for s in range(1, n - j + 1)])
        rights.append(right)
        lefts.append(left)
    return [block] + rights + lefts


def add(*parts):
    return sum(part.astype(F32) for part in parts).astype(BF16)


def line_sum(parts, n):
    right, left = parts[1], parts[n - 1]
    for j in range(1, n):
        if j > 1:
            right, left = add(parts[j], right), add(parts[n - j], left)
        right = lax.ppermute(right, "seq", [(s, s + 1) for s in range(j)])
        left = lax.ppermute(left, "seq", [(s, s - 1) for s in range(n - j, n)])
    return add(parts[0], right, left)


def on_device(tokens, cotangent, router, threshold, w_gate, w_up, w_down, hid_scale, picks, counts):
    experts, slots = picks.shape[1:]
    own, features = tokens.shape
    seq_n = lax.axis_size("seq")
    everyone = seq_n * lax.axis_size("exp")
    pack = max(1, 8 // slots)
    chosen = picks[0].T

    def to_experts(block):
        block = block.reshape(experts, -1, block.shape[1])
        return lax.all_to_all(block, "exp", split_axis=0, concat_axis=0, tiled=True).reshape(-1, block.shape[2])

    x_blocks = line_gather(to_experts(choose_rows(tokens, chosen, counts, pack, False)), seq_n)
    c_blocks = line_gather(to_experts(choose_rows(cotangent, chosen, counts, pack, True)), seq_n)

    x, pre_gate, pre_up, gates, hidden, *out = expert_forward(
        x_blocks, seq_n, slots, pack, router, threshold, w_gate, w_up, w_down, hid_scale
    )
    mixture = scatter_rows(to_experts(line_sum(out, seq_n)), chosen, counts, own, pack)

    c, gate_delta, up_delta, router_part, total, *back = expert_backward(
        c_blocks, seq_n, slots, pack, x, pre_gate, pre_up, gates, router, w_gate, w_up, w_down, hid_scale
    )
    token_grad = scatter_rows(to_experts(line_sum(back, seq_n)), chosen, counts, own, pack)

    message = jnp.concatenate(
        [router_part.reshape(everyone, -1), jnp.broadcast_to(total[:, :1], (everyone, 1))], axis=1
    )
    told = lax.all_to_all(message, BOTH, split_axis=0, concat_axis=0, tiled=True)
    told = jnp.sum(told.reshape(seq_n, experts, -1), axis=0)

    gate_grad, up_grad, down_grad = weight_grads(x, c, hidden, gate_delta, up_delta)
    return mixture, token_grad, told[:, :-1].T, told[:, -1], gate_grad, up_grad, down_grad


def solution(mesh):
    by_owner = P(BOTH, None)
    columns = P("exp", None, "seq")
    down = P("exp", "seq", None)
    return jax.shard_map(
        on_device,
        mesh=mesh,
        in_specs=(
            by_owner,
            by_owner,
            P(),
            P(),
            columns,
            columns,
            down,
            P("exp", "seq"),
            P(BOTH, None, None),
            by_owner,
        ),
        out_specs=(by_owner, by_owner, by_owner, P(), columns, columns, down),
        check_vma=False,
    )
```

```python
import jax
import jax.numpy as jnp
from jax import lax
from jax.experimental import pallas as pl
from jax.experimental.pallas import tpu as pltpu
from jax.sharding import PartitionSpec as P

BOTH = ("seq", "exp")
F32 = jnp.float32
BF16 = jnp.bfloat16
ROWS = ((0,), (0,))
LAST = ((1,), (1,))
STEPS = 4
LANES = 128


def mm(a, b, dims=((1,), (0,))):
    return lax.dot_general(a, b, (dims, ((), ())), preferred_element_type=F32)


def limit(mib):
    return pltpu.CompilerParams(vmem_limit_bytes=mib * 2**20)


def cost(flops, moved):
    return pl.CostEstimate(flops=flops, bytes_accessed=moved, transcendentals=0)


def shape(dims, dtype=BF16):
    return jax.ShapeDtypeStruct(dims, dtype)


IN_HBM = pl.BlockSpec(memory_space=pltpu.HBM)
ANYWHERE = pl.BlockSpec(memory_space=pl.ANY)
IN_VMEM = pl.BlockSpec(memory_space=pltpu.VMEM)


def choose_rows(rows, picks, counts, pack, only_live):
    own, features = rows.shape
    slots, experts = picks.shape
    count = experts * pack * slots
    part = features // pack
    width = part // STEPS

    def body(picks_ref, counts_ref, rows_ref, out_ref, hot_ref, picks_s, counts_s, rows_v, sems):
        small = [
            pltpu.make_async_copy(picks_ref, picks_s, sems.at[STEPS]),
            pltpu.make_async_copy(counts_ref, counts_s, sems.at[STEPS + 1]),
        ]
        large = [
            pltpu.make_async_copy(rows_ref.at[:, pl.ds(j * pack * width, pack * width)],
                                  rows_v.at[:, pl.ds(j * pack * width, pack * width)], sems.at[j])
            for j in range(STEPS)
        ]
        for copy in small + large:
            copy.start()
        for copy in small:
            copy.wait()
        dims = (count, own)
        row = lax.broadcasted_iota(jnp.int32, dims, 0)
        token = lax.broadcasted_iota(jnp.int32, dims, 1)
        place = row // (pack * slots) * slots + row % slots
        part_of = (row // slots) % pack
        want = jnp.full(dims, -1, jnp.int32)
        for e in range(experts):
            for k in range(slots):
                pick = picks_s[k, e]
                if only_live:
                    pick = jnp.where(k < counts_s[0, e], pick, -1)
                want = jnp.where(place == e * slots + k, pick, want)
        for h in range(pack):
            hot_ref[h] = jnp.where((want == token) & (part_of == h), 1.0, 0.0).astype(BF16)
        for copy in large:
            copy.wait()
        for j in range(STEPS):
            out_ref[:, j * width : (j + 1) * width] = sum(
                mm(hot_ref[h], rows_v[:, h * part + j * width : h * part + (j + 1) * width]) for h in range(pack)
            ).astype(BF16)

    return pl.pallas_call(
        body,
        in_specs=[IN_HBM] * 3,
        out_specs=[IN_VMEM] * 2,
        out_shape=[shape((count, part)), shape((pack, count, own))],
        scratch_shapes=[
            pltpu.SMEM(picks.shape, jnp.int32),
            pltpu.SMEM(counts.shape, jnp.int32),
            pltpu.VMEM(rows.shape, BF16),
            pltpu.SemaphoreType.DMA((STEPS + 2,)),
        ],
        compiler_params=limit(8),
        cost_estimate=cost(2 * count * own * features, 2 * features * own),
    )(picks, counts, rows)


def scatter_rows(back, hot):
    count, part = back.shape
    pack, _, own = hot.shape
    width = part // 2

    def body(hot_ref, back_ref, out_ref):
        out_ref[...] = mm(hot_ref[...], back_ref[...], ROWS).astype(BF16)

    return pl.pallas_call(
        body,
        grid=(pack, 2),
        in_specs=[
            pl.BlockSpec((None, count, own), lambda h, i: (h, 0, 0)),
            pl.BlockSpec((count, width), lambda h, i: (0, i)),
        ],
        out_specs=pl.BlockSpec((own, width), lambda h, i: (0, h * 2 + i)),
        out_shape=shape((own, part * pack)),
        compiler_params=limit(8),
        cost_estimate=cost(2 * count * own * part * pack, 2 * part * pack * own),
    )(hot, back)


def first_part(rows, pack, slots):
    return (lax.broadcasted_iota(jnp.int32, (rows, 1), 0) // slots) % pack == 0


def fold(parts, slots):
    rows = parts[0].shape[0]
    total = parts[0]
    for h in range(1, len(parts)):
        total = total + pltpu.roll(parts[h], rows - h * slots, 0)
    return total


def spread(value, pack, slots):
    return [value if h == 0 else pltpu.roll(value, h * slots, 0) for h in range(pack)]


class Arrivals:
    def __init__(self, blocks, plan):
        self.blocks, self.plan = blocks, plan

    def start(self, refs, target, sems):
        rows = refs[0].shape[0]
        here = lax.axis_index("seq")
        for k, (a, b, t) in enumerate(self.plan):
            place = target.at[pl.ds(k * rows, rows), :]
            if a == b:
                pltpu.make_async_copy(refs[a], place, sems.at[k]).start()
            else:

                @pl.when(here >= t)
                def _():
                    pltpu.make_async_copy(refs[a], place, sems.at[k]).start()

                @pl.when(here < t)
                def _():
                    pltpu.make_async_copy(refs[b], place, sems.at[k]).start()

    def wait(self, refs, target, sems):
        rows = refs[0].shape[0]
        for k, (a, _, _) in enumerate(self.plan):
            pltpu.make_async_copy(refs[a], target.at[pl.ds(k * rows, rows), :], sems.at[k]).wait()


def side_copies(gate_ref, up_ref, router_ref, side, sems, pack, j, width):
    part = side.shape[0]
    hidden_n = gate_ref.shape[2]
    rows = pl.ds(j * width, width)
    copies = []
    for h in range(pack):
        for n, ref in enumerate((gate_ref, up_ref)):
            columns = pl.ds((2 * h + n) * hidden_n, hidden_n)
            copies.append((ref.at[0, pl.ds(h * part + j * width, width), :], side.at[rows, columns]))
    columns = pl.ds(2 * pack * hidden_n, LANES)
    copies.append((router_ref.at[rows, :], side.at[rows, columns]))
    return [pltpu.make_async_copy(a, b, sems.at[j, n]) for n, (a, b) in enumerate(copies)]


def down_copies(down_ref, stack, sems, pack):
    hidden_n = down_ref.shape[1]
    part = stack.shape[1]
    return [
        pltpu.make_async_copy(
            down_ref.at[0, :, pl.ds(h * part, part)], stack.at[pl.ds(h * hidden_n, hidden_n), :], sems.at[h]
        )
        for h in range(pack)
    ]


def send_blocks(out, out_refs, seq_n, columns):
    rows = out.shape[0] // seq_n
    for k in range(seq_n):
        out_refs[k][:, columns] = out[k * rows : (k + 1) * rows]
    if len(out_refs) > seq_n:
        here = lax.axis_index("seq")

        @pl.when(here == 0)
        def _():
            out_refs[seq_n][:, columns] = out[rows : 2 * rows]

        @pl.when(here > 0)
        def _():
            out_refs[seq_n][:, columns] = out[(seq_n - 1) * rows :]


def sends(seq_n):
    return seq_n + 1 if seq_n == 4 else seq_n


def expert_forward(arrivals, seq_n, slots, experts, pack, router_side, threshold, w_gate, w_up, w_down, hid_scale):
    block_rows, part = arrivals.blocks[0].shape
    rows = block_rows * seq_n
    hidden_n = w_gate.shape[2]
    width = part // STEPS
    total = 2 * pack * hidden_n + LANES
    n_blocks = len(arrivals.blocks)
    n_sends = sends(seq_n)

    def body(*refs):
        blocks = refs[:n_blocks]
        router_ref, gate_ref, up_ref, down_ref, threshold_ref, scale_ref = refs[n_blocks : n_blocks + 6]
        x_ref, pre_ref, hidden_ref = refs[n_blocks + 6 : n_blocks + 9]
        out_refs = refs[n_blocks + 9 : n_blocks + 9 + n_sends]
        side, stack, x_sems, side_sems, stack_sems = refs[n_blocks + 9 + n_sends :]
        arrivals.start(blocks, x_ref, x_sems)
        chunks = [side_copies(gate_ref, up_ref, router_ref, side, side_sems, pack, j, width) for j in range(STEPS)]
        downs = down_copies(down_ref, stack, stack_sems, pack)
        for chunk in chunks:
            for copy in chunk:
                copy.start()
        for copy in downs:
            copy.start()
        arrivals.wait(blocks, x_ref, x_sems)
        for j, chunk in enumerate(chunks):
            for copy in chunk:
                copy.wait()
            y = mm(x_ref[:, j * width : (j + 1) * width], side[j * width : (j + 1) * width, :])
            if j == 0:
                acc = y
            else:
                acc = acc + y
        columns = [acc[:, n * hidden_n : (n + 1) * hidden_n] for n in range(2 * pack)]
        gate = fold(columns[0::2], slots)
        up = fold(columns[1::2], slots)
        scores = acc[:, 2 * pack * hidden_n :]
        lane = lax.broadcasted_iota(jnp.int32, scores.shape, 1)
        expert = lax.axis_index("exp")
        score = fold([jnp.where(lane == h * experts + expert, scores, 0.0) for h in range(pack)], slots)
        lane = lax.broadcasted_iota(jnp.int32, threshold_ref.shape, 1)
        score = score - jnp.where(lane == expert, threshold_ref[...], 0.0)
        g = jax.nn.sigmoid(jnp.sum(score, axis=1, keepdims=True))
        pre_ref[:, :hidden_n] = gate
        pre_ref[:, hidden_n : 2 * hidden_n] = up
        pre_ref[:, 2 * hidden_n :] = jnp.broadcast_to(g, (rows, LANES))
        hidden = gate * jax.nn.sigmoid(gate) * up * scale_ref[...] * g
        hidden = jnp.where(first_part(rows, pack, slots), hidden, 0.0)
        for h, value in enumerate(spread(hidden, pack, slots)):
            hidden_ref[:, h * hidden_n : (h + 1) * hidden_n] = value.astype(BF16)
        for copy in downs:
            copy.wait()
        for j in range(STEPS):
            now = slice(j * width, (j + 1) * width)
            send_blocks(mm(hidden_ref[...], stack[:, now]).astype(BF16), out_refs, seq_n, now)

    padded = jnp.zeros((1, LANES), F32).at[:, :experts].set(threshold[None, :])
    return pl.pallas_call(
        body,
        in_specs=[ANYWHERE] * n_blocks + [IN_HBM] * 4 + [IN_VMEM] * 2,
        out_specs=[IN_VMEM] * (3 + n_sends),
        out_shape=[
            shape((rows, part)),
            shape((rows, 2 * hidden_n + LANES), F32),
            shape((rows, pack * hidden_n)),
        ]
        + [shape((block_rows, part))] * n_sends,
        scratch_shapes=[
            pltpu.VMEM((part, total), BF16),
            pltpu.VMEM((pack * hidden_n, part), BF16),
            pltpu.SemaphoreType.DMA((seq_n,)),
            pltpu.SemaphoreType.DMA((STEPS, 2 * pack + 1)),
            pltpu.SemaphoreType.DMA((pack,)),
        ],
        compiler_params=limit(28),
        cost_estimate=cost(6 * rows * part * pack * hidden_n, 6 * part * pack * hidden_n),
    )(*arrivals.blocks, router_side, w_gate, w_up, w_down, padded, hid_scale)


def split3(v):
    hi = v.astype(BF16)
    rest = v - hi.astype(F32)
    mid = rest.astype(BF16)
    return hi, mid, (rest - mid.astype(F32)).astype(BF16)


def expert_backward(arrivals, seq_n, slots, experts, pack, x, pre, router_side, w_gate, w_up, w_down, hid_scale):
    block_rows, part = arrivals.blocks[0].shape
    rows = block_rows * seq_n
    hidden_n = w_gate.shape[2]
    width = part // STEPS
    total = 2 * pack * hidden_n + LANES
    n_blocks = len(arrivals.blocks)
    n_sends = sends(seq_n)

    def body(*refs):
        blocks = refs[:n_blocks]
        router_ref, gate_ref, up_ref, down_ref, scale_ref, x_ref, pre_ref = refs[n_blocks : n_blocks + 7]
        c_ref, delta_ref, router_out, total_ref = refs[n_blocks + 7 : n_blocks + 11]
        out_refs = refs[n_blocks + 11 : n_blocks + 11 + n_sends]
        side, stack, columns, x_sems, side_sems, stack_sems = refs[n_blocks + 11 + n_sends :]
        arrivals.start(blocks, c_ref, x_sems)
        chunks = [side_copies(gate_ref, up_ref, router_ref, side, side_sems, pack, j, width) for j in range(STEPS)]
        downs = down_copies(down_ref, stack, stack_sems, pack)
        for copy in downs:
            copy.start()
        for chunk in chunks:
            for copy in chunk:
                copy.start()
        arrivals.wait(blocks, c_ref, x_sems)
        parts = []
        for h, copy in enumerate(downs):
            copy.wait()
            parts.append(mm(c_ref[...], stack[h * hidden_n : (h + 1) * hidden_n, :], LAST))
        raw = jnp.where(first_part(rows, pack, slots), fold(parts, slots) * scale_ref[...], 0.0)
        gate = pre_ref[:, :hidden_n]
        up = pre_ref[:, hidden_n : 2 * hidden_n]
        g = pre_ref[:, 2 * hidden_n : 2 * hidden_n + 1]
        sig = jax.nn.sigmoid(gate)
        act = gate * sig
        score = jnp.sum(act * up * raw, axis=1, keepdims=True) * g * (1.0 - g)
        grad = raw * g
        to_gate = spread(grad * up * sig * (1.0 + gate * (1.0 - sig)), pack, slots)
        to_up = spread(grad * act, pack, slots)
        expert = lax.axis_index("exp")
        lane = lax.broadcasted_iota(jnp.int32, (rows, LANES), 1)
        by_expert = jnp.zeros((rows, LANES), F32)
        by_split = jnp.zeros((rows, LANES), F32)
        for h, value in enumerate(spread(jnp.broadcast_to(score, (rows, LANES)), pack, slots)):
            delta_ref[:, 2 * h * hidden_n : (2 * h + 1) * hidden_n] = to_gate[h].astype(BF16)
            delta_ref[:, (2 * h + 1) * hidden_n : (2 * h + 2) * hidden_n] = to_up[h].astype(BF16)
            for n, piece in enumerate(split3(value)):
                piece = piece.astype(F32)
                by_split = jnp.where(lane == 3 * h + n, piece, by_split)
                if n < 2:
                    by_expert = jnp.where(lane == (n * pack + h) * experts + expert, piece, by_expert)
        columns[...] = by_split.astype(BF16)
        delta_ref[:, 2 * pack * hidden_n :] = by_expert.astype(BF16)
        total_ref[...] = jnp.broadcast_to(-jnp.sum(score, axis=0, keepdims=True), total_ref.shape)
        for j, chunk in enumerate(chunks):
            now = slice(j * width, (j + 1) * width)
            for copy in chunk:
                copy.wait()
            send_blocks(mm(delta_ref[...], side[now, :], LAST).astype(BF16), out_refs, seq_n, now)
        for j in range(STEPS):
            now = slice(j * width, (j + 1) * width)
            told = mm(columns[...], x_ref[:, now], ROWS)
            for h in range(pack):
                router_out[h : h + 1, now] = jnp.sum(told[3 * h : 3 * h + 3], axis=0, keepdims=True)

    return pl.pallas_call(
        body,
        in_specs=[ANYWHERE] * n_blocks + [IN_HBM] * 4 + [IN_VMEM] * 3,
        out_specs=[IN_VMEM] * (4 + n_sends),
        out_shape=[
            shape((rows, part)),
            shape((rows, total)),
            shape((pack, part), F32),
            shape((1, LANES), F32),
        ]
        + [shape((block_rows, part))] * n_sends,
        scratch_shapes=[
            pltpu.VMEM((part, total), BF16),
            pltpu.VMEM((pack * hidden_n, part), BF16),
            pltpu.VMEM((rows, LANES), BF16),
            pltpu.SemaphoreType.DMA((seq_n,)),
            pltpu.SemaphoreType.DMA((STEPS, 2 * pack + 1)),
            pltpu.SemaphoreType.DMA((pack,)),
        ],
        compiler_params=limit(28),
        cost_estimate=cost(6 * rows * part * pack * hidden_n, 6 * part * pack * hidden_n),
    )(*arrivals.blocks, router_side, w_gate, w_up, w_down, hid_scale, x, pre)


def side_grads(x, delta, pack, hidden_n):
    rows, part = x.shape
    width = part // STEPS

    def body(x_ref, delta_ref, gate_out, up_out):
        both = mm(x_ref[...], delta_ref[...], ROWS)
        gate_out[...] = both[:, :hidden_n]
        up_out[...] = both[:, hidden_n:]

    tall = pl.BlockSpec((None, width, hidden_n), lambda h, i: (0, h * STEPS + i, 0))
    return pl.pallas_call(
        body,
        grid=(pack, STEPS),
        in_specs=[
            pl.BlockSpec((rows, width), lambda h, i: (0, i)),
            pl.BlockSpec((rows, 2 * hidden_n), lambda h, i: (0, h)),
        ],
        out_specs=[tall, tall],
        out_shape=[shape((1, part * pack, hidden_n), F32)] * 2,
        compiler_params=limit(16),
        cost_estimate=cost(4 * rows * part * pack * hidden_n, 8 * part * pack * hidden_n),
    )(x, delta)


def down_grads(c, hidden, pack, hidden_n):
    rows, part = c.shape
    width = part // 2

    def body(c_ref, hidden_ref, out):
        out[...] = mm(hidden_ref[...], c_ref[...], ROWS)

    return pl.pallas_call(
        body,
        grid=(pack, 2),
        in_specs=[
            pl.BlockSpec((rows, width), lambda h, i: (0, i)),
            pl.BlockSpec((rows, hidden_n), lambda h, i: (0, h)),
        ],
        out_specs=pl.BlockSpec((None, hidden_n, width), lambda h, i: (0, 0, h * 2 + i)),
        out_shape=shape((1, hidden_n, part * pack), F32),
        compiler_params=limit(16),
        cost_estimate=cost(2 * rows * part * pack * hidden_n, 4 * part * pack * hidden_n),
    )(c, hidden)


def up_line(block, n, first=0, last=None):
    last = n - 1 if last is None else last
    return lax.ppermute(block, "seq", [(s, s + 1) for s in range(first, last)])


def down_line(block, n, first=1, last=None):
    last = n if last is None else last
    return lax.ppermute(block, "seq", [(s, s - 1) for s in range(first, last)])


def line_gather(block, n):
    if n == 4:
        far = lax.ppermute(block, "seq", [(s, (s + 2) % 4) for s in range(4)])
        below = up_line(block, n)
        above = down_line(block, n)
        ends = lax.ppermute(far, "seq", [(2, 3), (1, 0)])
        return Arrivals([block, below, above, far, ends], [(0, 0, 0), (1, 4, 1), (3, 3, 0), (4, 2, 3)])
    ups, downs = [], []
    up = down = block
    for j in range(1, n):
        up = up_line(up, n, j - 1)
        down = down_line(down, n, 1, n - j + 1)
        ups.append(up)
        downs.append(down)
    plan = [(0, 0, 0)] + [(k, 2 * n - 1 - k, k) for k in range(1, n)]
    return Arrivals([block] + ups + downs, plan)


def add(*parts):
    return sum(part.astype(F32) for part in parts).astype(BF16)


def line_sum(parts, n):
    if n == 4:
        ends = lax.ppermute(parts[4], "seq", [(3, 2), (0, 1)])
        below = up_line(parts[3], n)
        above = down_line(parts[1], n)
        far = lax.ppermute(add(parts[2], ends), "seq", [(s, (s + 2) % 4) for s in range(4)])
        return add(parts[0], below, above, far), ends
    up, down = parts[1], parts[n - 1]
    first = None
    for j in range(1, n):
        if j > 1:
            up, down = add(parts[j], up), add(parts[n - j], down)
        up = up_line(up, n, 0, j)
        down = down_line(down, n, n - j)
        first = up if first is None else first
    return add(parts[0], up, down), first


def on_device(tokens, cotangent, router, threshold, w_gate, w_up, w_down, hid_scale, picks, counts):
    experts, slots = picks.shape[1:]
    features = tokens.shape[1]
    true_hidden = w_gate.shape[2]
    extra = -true_hidden % LANES
    if extra:
        w_gate, w_up = (jnp.pad(w, ((0, 0), (0, 0), (0, extra))) for w in (w_gate, w_up))
        w_down = jnp.pad(w_down, ((0, 0), (0, extra), (0, 0)))
        hid_scale = jnp.pad(hid_scale, ((0, 0), (0, extra)))
    hidden_n = true_hidden + extra
    seq_n = lax.axis_size("seq")
    everyone = seq_n * lax.axis_size("exp")
    pack = max(1, 8 // slots)
    chosen = picks[0].T

    def to_experts(block):
        block = block.reshape(experts, -1, block.shape[1])
        return lax.all_to_all(block, "exp", split_axis=0, concat_axis=0, tiled=True).reshape(-1, block.shape[2])

    x_rows, _ = choose_rows(tokens, chosen, counts, pack, False)
    c_rows, hot = choose_rows(cotangent, chosen, counts, pack, True)
    x_in = line_gather(to_experts(x_rows), seq_n)
    c_in = line_gather(to_experts(c_rows), seq_n)
    halves = list(router.reshape(pack, features // pack, experts))
    router_side = jnp.concatenate(halves + halves, axis=1)
    router_side = jnp.pad(router_side, ((0, 0), (0, LANES - router_side.shape[1])))

    x, pre, hidden, *out = expert_forward(
        x_in, seq_n, slots, experts, pack, router_side, threshold, w_gate, w_up, w_down, hid_scale
    )
    out, began = line_sum(out, seq_n)
    c_in.blocks[0], _ = lax.optimization_barrier((c_in.blocks[0], began))
    c, delta, router_part, total, *back = expert_backward(
        c_in, seq_n, slots, experts, pack, x, pre, router_side, w_gate, w_up, w_down, hid_scale
    )
    back, began = line_sum(back, seq_n)
    x, c, _ = lax.optimization_barrier((x, c, began))
    down_grad = down_grads(c, hidden, pack, hidden_n)
    gate_grad, up_grad = side_grads(x, delta, pack, hidden_n)
    if extra:
        gate_grad, up_grad = gate_grad[:, :, :true_hidden], up_grad[:, :, :true_hidden]
        down_grad = down_grad[:, :true_hidden]
    mixture = scatter_rows(to_experts(out), hot)
    token_grad = scatter_rows(to_experts(back), hot)

    message = jnp.concatenate(
        [router_part.reshape(everyone, -1), jnp.broadcast_to(total[:, :1], (everyone, 1))], axis=1
    )
    told = lax.all_to_all(message, BOTH, split_axis=0, concat_axis=0, tiled=True)
    told = jnp.sum(told.reshape(seq_n, experts, -1), axis=0)
    return mixture, token_grad, told[:, :-1].T, told[:, -1], gate_grad, up_grad, down_grad


def solution(mesh):
    by_owner = P(BOTH, None)
    columns = P("exp", None, "seq")
    down = P("exp", "seq", None)
    return jax.shard_map(
        on_device,
        mesh=mesh,
        in_specs=(
            by_owner,
            by_owner,
            P(),
            P(),
            columns,
            columns,
            down,
            P("exp", "seq"),
            P(BOTH, None, None),
            by_owner,
        ),
        out_specs=(by_owner, by_owner, by_owner, P(), columns, columns, down),
        check_vma=False,
    )
```

```python
import jax
import jax.numpy as jnp
from jax import lax
from jax.experimental import pallas as pl
from jax.experimental.pallas import tpu as pltpu
from jax.sharding import PartitionSpec as P

BOTH = ("seq", "exp")
F32 = jnp.float32
BF16 = jnp.bfloat16
ROWS = ((0,), (0,))
LAST = ((1,), (1,))
STEPS = 4
LANES = 128


def mm(a, b, dims=((1,), (0,))):
    return lax.dot_general(a, b, (dims, ((), ())), preferred_element_type=F32)


PARAMS = pltpu.CompilerParams(vmem_limit_bytes=56 * 2**20)


def cost(flops, moved):
    return pl.CostEstimate(flops=flops, bytes_accessed=moved, transcendentals=0)


def shape(dims, dtype=BF16):
    return jax.ShapeDtypeStruct(dims, dtype)


ANYWHERE = pl.BlockSpec(memory_space=pl.ANY)
IN_VMEM = pl.BlockSpec(memory_space=pltpu.VMEM)


def choose_rows(tokens, cotangent, picks, counts, pack):
    own, features = tokens.shape
    slots, experts = picks.shape
    count = experts * pack * slots
    part = features // pack
    width = part // STEPS

    def body(picks_ref, counts_ref, c_ref, x_ref, c_out, x_out, hot_ref, picks_s, counts_s, c_v, x_v, hot, sems):
        small = [
            pltpu.make_async_copy(picks_ref, picks_s, sems.at[2 * STEPS]),
            pltpu.make_async_copy(counts_ref, counts_s, sems.at[2 * STEPS + 1]),
        ]
        for copy in small:
            copy.start()
        large = []
        for n, (ref, held) in enumerate(((c_ref, c_v), (x_ref, x_v))):
            for j in range(STEPS):
                now = pl.ds(j * pack * width, pack * width)
                large.append(pltpu.make_async_copy(ref.at[:, now], held.at[:, now], sems.at[n * STEPS + j]))
                large[-1].start()
        for copy in small:
            copy.wait()
        dims = (count, own)
        row = lax.broadcasted_iota(jnp.int32, dims, 0)
        token = lax.broadcasted_iota(jnp.int32, dims, 1)
        place = row // (pack * slots) * slots + row % slots
        part_of = (row // slots) % pack
        want = jnp.full(dims, -1, jnp.int32)
        want_live = want
        for e in range(experts):
            for k in range(slots):
                here = place == e * slots + k
                want = jnp.where(here, picks_s[k, e], want)
                want_live = jnp.where(here, jnp.where(k < counts_s[0, e], picks_s[k, e], -1), want_live)
        for h in range(pack):
            hot[h] = jnp.where((want == token) & (part_of == h), 1.0, 0.0).astype(BF16)
            hot_ref[h] = jnp.where((want_live == token) & (part_of == h), 1.0, 0.0).astype(BF16)
        for n, (chooser, held, out_ref) in enumerate(((hot_ref, c_v, c_out), (hot, x_v, x_out))):
            for copy in large[n * STEPS : (n + 1) * STEPS]:
                copy.wait()
            for j in range(STEPS):
                out_ref[:, j * width : (j + 1) * width] = sum(
                    mm(chooser[h], held[:, h * part + j * width : h * part + (j + 1) * width]) for h in range(pack)
                ).astype(BF16)

    return pl.pallas_call(
        body,
        in_specs=[ANYWHERE] * 4,
        out_specs=[IN_VMEM] * 3,
        out_shape=[shape((count, part))] * 2 + [shape((pack, count, own))],
        scratch_shapes=[
            pltpu.SMEM(picks.shape, jnp.int32),
            pltpu.SMEM(counts.shape, jnp.int32),
            pltpu.VMEM(tokens.shape, BF16),
            pltpu.VMEM(tokens.shape, BF16),
            pltpu.VMEM((pack, count, own), BF16),
            pltpu.SemaphoreType.DMA((2 * STEPS + 2,)),
        ],
        compiler_params=PARAMS,
        cost_estimate=cost(4 * count * own * features, 4 * features * own),
    )(picks, counts, cotangent, tokens)


def by_place(arrivals, seq_n, groups):
    blocks = [block.reshape(groups, -1, block.shape[1]) for block in arrivals.blocks]
    _, rows, part = blocks[0].shape

    def body(*refs):
        out_ref, sems = refs[-2:]
        arrivals.start(refs[:-2], [out_ref.at[:, k] for k in range(seq_n)], sems)
        arrivals.wait(refs[:-2], [out_ref.at[:, k] for k in range(seq_n)], sems)

    return pl.pallas_call(
        body,
        in_specs=[ANYWHERE] * len(blocks),
        out_specs=ANYWHERE,
        out_shape=shape((groups, seq_n, rows, part)),
        scratch_shapes=[pltpu.SemaphoreType.DMA((seq_n,))],
        compiler_params=PARAMS,
        cost_estimate=cost(0, 4 * groups * seq_n * rows * part),
    )(*blocks)


def scatter_rows(back, hot, message=None):
    pack, count, own = hot.shape
    part = back.shape[1] if message is None else message[0]
    width = part // 2

    def body(hot_ref, back_ref, *refs):
        out_ref = refs[-1] if message is None else refs[-3]
        out_ref[...] = mm(hot_ref[...], back_ref[...], ROWS).astype(BF16)
        if message is not None:
            message_refs, router_ref, total_ref = refs[:-3], refs[-2], refs[-1]

            @pl.when((pl.program_id(0) == 0) & (pl.program_id(1) == 0))
            def _():
                experts = router_ref.shape[1]
                group = count // experts
                row = lax.broadcasted_iota(jnp.int32, (count, experts), 0)
                expert = lax.broadcasted_iota(jnp.int32, (count, experts), 1)
                mine = row // group == expert
                even = jnp.where(mine & (row % 2 == 0), 1.0, 0.0).astype(BF16)
                odd = jnp.where(mine & (row % 2 == 1), 1.0, 0.0).astype(BF16)
                router = sum(mm(ref[...], even, ROWS) for ref in message_refs)
                total = sum(mm(ref[...], odd, ROWS) for ref in message_refs)
                router_ref[...] = router[: router_ref.shape[0]]
                total_ref[...] = jnp.sum(total[:3], axis=0, keepdims=True)

    in_specs = [
        pl.BlockSpec((None, count, own), lambda h, i: (h, 0, 0)),
        pl.BlockSpec((count, width), lambda h, i: (0, i)),
    ]
    out_specs = [pl.BlockSpec((own, width), lambda h, i: (0, h * 2 + i))]
    out_shape = [shape((own, part * pack))]
    args = [hot, back]
    if message is not None:
        _, per, experts = message
        for t in range((back.shape[1] - part) // LANES):
            in_specs.append(pl.BlockSpec((count, LANES), lambda h, i, t=t: (0, part // LANES + t)))
            args.append(back)
        out_specs += [
            pl.BlockSpec((per, experts), lambda h, i: (0, 0)),
            pl.BlockSpec((1, experts), lambda h, i: (0, 0)),
        ]
        out_shape += [shape((per, experts), F32), shape((1, experts), F32)]
    return pl.pallas_call(
        body,
        grid=(pack, 2),
        in_specs=in_specs,
        out_specs=out_specs,
        out_shape=out_shape,
        compiler_params=PARAMS,
        cost_estimate=cost(2 * count * own * part * pack, 2 * part * pack * own),
    )(*args)


def regroup(value, group, outer, inner):
    return jnp.concatenate(
        [value[(o * inner + i) * group : (o * inner + i + 1) * group] for i in range(inner) for o in range(outer)]
    )


def first_part(rows, pack, slots):
    return (lax.broadcasted_iota(jnp.int32, (rows, 1), 0) // slots) % pack == 0


def fold(parts, slots):
    rows = parts[0].shape[0]
    total = parts[0]
    for h in range(1, len(parts)):
        total = total + pltpu.roll(parts[h], rows - h * slots, 0)
    return total


def spread(value, pack, slots):
    return [value if h == 0 else pltpu.roll(value, h * slots, 0) for h in range(pack)]


class Arrivals:
    def __init__(self, blocks, plan):
        self.blocks, self.plan = blocks, plan

    def start(self, refs, places, sems):
        here = lax.axis_index("seq")
        for k, (a, b, t) in enumerate(self.plan):
            if a == b:
                pltpu.make_async_copy(refs[a], places[k], sems.at[k]).start()
            else:

                @pl.when(here >= t)
                def _():
                    pltpu.make_async_copy(refs[a], places[k], sems.at[k]).start()

                @pl.when(here < t)
                def _():
                    pltpu.make_async_copy(refs[b], places[k], sems.at[k]).start()

    def wait(self, refs, places, sems):
        for k, (a, _, _) in enumerate(self.plan):
            pltpu.make_async_copy(refs[a], places[k], sems.at[k]).wait()


def side_copies(gate_ref, up_ref, router_ref, side, sems, pack, j, width):
    part = side.shape[0]
    hidden_n = gate_ref.shape[2]
    rows = pl.ds(j * width, width)
    copies = []
    for h in range(pack):
        for n, ref in enumerate((gate_ref, up_ref)):
            columns = pl.ds((2 * h + n) * hidden_n, hidden_n)
            copies.append((ref.at[0, pl.ds(h * part + j * width, width), :], side.at[rows, columns]))
    columns = pl.ds(2 * pack * hidden_n, LANES)
    copies.append((router_ref.at[rows, :], side.at[rows, columns]))
    return [pltpu.make_async_copy(a, b, sems.at[j, n]) for n, (a, b) in enumerate(copies)]


def down_copies(down_ref, stack, sems, pack):
    hidden_n = down_ref.shape[1]
    part = stack.shape[1]
    return [
        pltpu.make_async_copy(
            down_ref.at[0, :, pl.ds(h * part, part)], stack.at[pl.ds(h * hidden_n, hidden_n), :], sems.at[h]
        )
        for h in range(pack)
    ]


def send_blocks(out, out_refs, seq_n, columns):
    rows = out.shape[0] // seq_n
    for k in range(seq_n):
        out_refs[k][:, columns] = out[k * rows : (k + 1) * rows]
    if len(out_refs) > seq_n:
        here = lax.axis_index("seq")

        @pl.when(here == 0)
        def _():
            out_refs[seq_n][:, columns] = out[rows : 2 * rows]

        @pl.when(here > 0)
        def _():
            out_refs[seq_n][:, columns] = out[(seq_n - 1) * rows :]


def sends(seq_n):
    return seq_n + 1 if seq_n == 4 else seq_n


def expert_forward(arrivals, seq_n, slots, experts, pack, router_side, threshold, w_gate, w_up, w_down, hid_scale):
    block_rows, part = arrivals.blocks[0].shape
    rows = block_rows * seq_n
    hidden_n = w_gate.shape[2]
    width = part // STEPS
    total = 2 * pack * hidden_n + LANES
    group = pack * slots
    n_blocks = len(arrivals.blocks)
    n_sends = sends(seq_n)

    def body(*refs):
        blocks = refs[:n_blocks]
        router_ref, gate_ref, up_ref, down_ref, threshold_ref, scale_ref = refs[n_blocks : n_blocks + 6]
        x_ref, pre_ref, hidden_ref = refs[n_blocks + 6 : n_blocks + 9]
        out_refs = refs[n_blocks + 9 : n_blocks + 9 + n_sends]
        held, side, stack, x_sems, side_sems, stack_sems = refs[n_blocks + 9 + n_sends :]
        places = [x_ref.at[pl.ds(k * block_rows, block_rows), :] for k in range(seq_n)]
        arrivals.start(blocks, places, x_sems)
        chunks = [side_copies(gate_ref, up_ref, router_ref, side, side_sems, pack, j, width) for j in range(STEPS)]
        downs = down_copies(down_ref, stack, stack_sems, pack)
        for chunk in chunks:
            for copy in chunk:
                copy.start()
        for copy in downs:
            copy.start()
        arrivals.wait(blocks, places, x_sems)
        for j, chunk in enumerate(chunks):
            for copy in chunk:
                copy.wait()
            y = mm(x_ref[:, j * width : (j + 1) * width], side[j * width : (j + 1) * width, :])
            if j == 0:
                acc = y
            else:
                acc = acc + y
        columns = [acc[:, n * hidden_n : (n + 1) * hidden_n] for n in range(2 * pack)]
        gate = fold(columns[0::2], slots)
        up = fold(columns[1::2], slots)
        scores = acc[:, 2 * pack * hidden_n :]
        lane = lax.broadcasted_iota(jnp.int32, scores.shape, 1)
        expert = lax.axis_index("exp")
        score = fold([jnp.where(lane == h * experts + expert, scores, 0.0) for h in range(pack)], slots)
        lane = lax.broadcasted_iota(jnp.int32, threshold_ref.shape, 1)
        score = score - jnp.where(lane == expert, threshold_ref[...], 0.0)
        g = jax.nn.sigmoid(jnp.sum(score, axis=1, keepdims=True))
        pre_ref[:, :hidden_n] = gate
        pre_ref[:, hidden_n : 2 * hidden_n] = up
        pre_ref[:, 2 * hidden_n :] = jnp.broadcast_to(g, (rows, LANES))
        hidden = gate * jax.nn.sigmoid(gate) * up * scale_ref[...] * g
        hidden = jnp.where(first_part(rows, pack, slots), hidden, 0.0)
        for h, value in enumerate(spread(hidden, pack, slots)):
            now = slice(h * hidden_n, (h + 1) * hidden_n)
            held[:, now] = value.astype(BF16)
            hidden_ref[:, now] = regroup(value, group, seq_n, rows // seq_n // group).astype(BF16)
        for copy in downs:
            copy.wait()
        for j in range(STEPS):
            now = slice(j * width, (j + 1) * width)
            send_blocks(mm(held[...], stack[:, now]).astype(BF16), out_refs, seq_n, now)

    padded = jnp.zeros((1, LANES), F32).at[:, :experts].set(threshold[None, :])
    return pl.pallas_call(
        body,
        in_specs=[ANYWHERE] * n_blocks + [ANYWHERE] * 4 + [IN_VMEM] * 2,
        out_specs=[IN_VMEM] * (3 + n_sends),
        out_shape=[
            shape((rows, part)),
            shape((rows, 2 * hidden_n + LANES), F32),
            shape((rows, pack * hidden_n)),
        ]
        + [shape((block_rows, part))] * n_sends,
        scratch_shapes=[
            pltpu.VMEM((rows, pack * hidden_n), BF16),
            pltpu.VMEM((part, total), BF16),
            pltpu.VMEM((pack * hidden_n, part), BF16),
            pltpu.SemaphoreType.DMA((seq_n,)),
            pltpu.SemaphoreType.DMA((STEPS, 2 * pack + 1)),
            pltpu.SemaphoreType.DMA((pack,)),
        ],
        compiler_params=PARAMS,
        cost_estimate=cost(6 * rows * part * pack * hidden_n, 6 * part * pack * hidden_n),
    )(*arrivals.blocks, router_side, w_gate, w_up, w_down, padded, hid_scale)


def split3(v):
    hi = v.astype(BF16)
    rest = v - hi.astype(F32)
    mid = rest.astype(BF16)
    return hi, mid, (rest - mid.astype(F32)).astype(BF16)


def riding(seq_n, group):
    return LANES * -(-2 * seq_n // group)


def expert_backward(c, seq_n, exp_n, slots, pack, x, pre, router_side, w_gate, w_up, w_down, hid_scale):
    rows, part = x.shape
    block_rows = rows // seq_n
    hidden_n = w_gate.shape[2]
    width = part // STEPS
    total = 2 * pack * hidden_n + LANES
    group = pack * slots
    extra = riding(seq_n, group)
    per = part * pack // (seq_n * exp_n)
    n_sends = sends(seq_n)

    def body(*refs):
        c_ref, router_ref, gate_ref, up_ref, down_ref, x_ref, scale_ref, pre_ref, delta_ref = refs[:9]
        out_refs = refs[9 : 9 + n_sends]
        c_v, x_v, side, stack, columns, message, c_sem, x_sem, side_sems, stack_sems = refs[9 + n_sends :]
        c_copy = pltpu.make_async_copy(c_ref, c_v, c_sem)
        x_copy = pltpu.make_async_copy(x_ref, x_v, x_sem)
        chunks = [side_copies(gate_ref, up_ref, router_ref, side, side_sems, pack, j, width) for j in range(STEPS)]
        downs = down_copies(down_ref, stack, stack_sems, pack)
        c_copy.start()
        for copy in downs:
            copy.start()
        for chunk in chunks:
            for copy in chunk:
                copy.start()
        x_copy.start()
        c_copy.wait()
        parts = []
        for h, copy in enumerate(downs):
            copy.wait()
            parts.append(mm(c_v[...], stack[h * hidden_n : (h + 1) * hidden_n, :], LAST))
        raw = regroup(fold(parts, slots), group, block_rows // group, seq_n)
        raw = jnp.where(first_part(rows, pack, slots), raw * scale_ref[...], 0.0)
        gate = pre_ref[:, :hidden_n]
        up = pre_ref[:, hidden_n : 2 * hidden_n]
        g = pre_ref[:, 2 * hidden_n : 2 * hidden_n + 1]
        sig = jax.nn.sigmoid(gate)
        act = gate * sig
        score = jnp.sum(act * up * raw, axis=1, keepdims=True) * g * (1.0 - g)
        grad = raw * g
        to_gate = spread(grad * up * sig * (1.0 + gate * (1.0 - sig)), pack, slots)
        to_up = spread(grad * act, pack, slots)
        expert = lax.axis_index("exp")
        lane = lax.broadcasted_iota(jnp.int32, (rows, LANES), 1)
        by_expert = jnp.zeros((rows, LANES), F32)
        by_split = jnp.zeros((rows, LANES), F32)
        for h, value in enumerate(spread(jnp.broadcast_to(score, (rows, LANES)), pack, slots)):
            delta_ref[:, 2 * h * hidden_n : (2 * h + 1) * hidden_n] = to_gate[h].astype(BF16)
            delta_ref[:, (2 * h + 1) * hidden_n : (2 * h + 2) * hidden_n] = to_up[h].astype(BF16)
            for n, piece in enumerate(split3(value)):
                piece = piece.astype(F32)
                by_split = jnp.where(lane == 3 * h + n, piece, by_split)
                if n < 2:
                    by_expert = jnp.where(lane == (n * pack + h) * exp_n + expert, piece, by_expert)
        columns[...] = by_split.astype(BF16)
        delta_ref[:, 2 * pack * hidden_n :] = by_expert.astype(BF16)
        for j, chunk in enumerate(chunks):
            now = slice(j * width, (j + 1) * width)
            for copy in chunk:
                copy.wait()
            send_blocks(mm(delta_ref[...], side[now, :], LAST).astype(BF16), out_refs, seq_n, now)

        here = lax.axis_index("seq")
        x_copy.wait()
        told = mm(columns[...], x_v[...], ROWS)
        sub = lax.broadcasted_iota(jnp.int32, (group, LANES), 0)
        lane = lax.broadcasted_iota(jnp.int32, (group, LANES), 1)
        minus = jnp.broadcast_to(-jnp.sum(score, axis=0, keepdims=True), (group, LANES))
        pieces = [piece.astype(F32) for piece in split3(minus)]
        threshold_row = jnp.zeros((group, LANES), F32)
        for n, piece in enumerate(pieces):
            threshold_row = jnp.where(lane == n, piece, threshold_row)
        for owner in range(seq_n * exp_n):
            h, first = divmod(owner * per, part)
            shift = first % LANES
            value = jnp.sum(told[3 * h : 3 * h + 3, first - shift : first - shift + LANES], axis=0, keepdims=True)
            value = jnp.broadcast_to(value, (group, LANES))
            if shift:
                value = pltpu.roll(value, LANES - shift, 1)
            if per < LANES:
                value = jnp.where(lane < per, value, 0.0)
            d, place = divmod(owner, exp_n)
            for t in range(extra // LANES):
                row = sub + t * group
                message[d, place * group : (place + 1) * group, t * LANES : (t + 1) * LANES] = jnp.where(
                    row == 2 * here, value, jnp.where(row == 2 * here + 1, threshold_row, 0.0)
                )
        ride = [message[lax.rem(here - k + seq_n, seq_n)] for k in range(seq_n)]
        send_blocks(jnp.concatenate(ride).astype(BF16), out_refs, seq_n, slice(part, part + extra))

    return pl.pallas_call(
        body,
        in_specs=[ANYWHERE] * 6 + [IN_VMEM] * 2,
        out_specs=[IN_VMEM] * (1 + n_sends),
        out_shape=[shape((rows, total))] + [shape((block_rows, part + extra))] * n_sends,
        scratch_shapes=[
            pltpu.VMEM((rows, part), BF16),
            pltpu.VMEM((rows, part), BF16),
            pltpu.VMEM((part, total), BF16),
            pltpu.VMEM((pack * hidden_n, part), BF16),
            pltpu.VMEM((rows, LANES), BF16),
            pltpu.VMEM((seq_n, block_rows, extra), F32),
            pltpu.SemaphoreType.DMA,
            pltpu.SemaphoreType.DMA,
            pltpu.SemaphoreType.DMA((STEPS, 2 * pack + 1)),
            pltpu.SemaphoreType.DMA((pack,)),
        ],
        compiler_params=PARAMS,
        cost_estimate=cost(6 * rows * part * pack * hidden_n, 6 * part * pack * hidden_n),
    )(c, router_side, w_gate, w_up, w_down, x, hid_scale, pre)


def side_grads(x, delta, pack, hidden_n):
    rows, part = x.shape
    width = part // STEPS

    def body(x_ref, delta_ref, gate_out, up_out):
        both = mm(x_ref[...], delta_ref[...], ROWS)
        gate_out[...] = both[:, :hidden_n]
        up_out[...] = both[:, hidden_n:]

    tall = pl.BlockSpec((None, width, hidden_n), lambda h, i: (0, h * STEPS + i, 0))
    return pl.pallas_call(
        body,
        grid=(pack, STEPS),
        in_specs=[
            pl.BlockSpec((rows, width), lambda h, i: (0, i)),
            pl.BlockSpec((rows, 2 * hidden_n), lambda h, i: (0, h)),
        ],
        out_specs=[tall, tall],
        out_shape=[shape((1, part * pack, hidden_n), F32)] * 2,
        compiler_params=PARAMS,
        cost_estimate=cost(4 * rows * part * pack * hidden_n, 8 * part * pack * hidden_n),
    )(x, delta)


def down_grads(c, hidden, pack, hidden_n):
    rows, part = c.shape
    width = part // 2

    def body(c_ref, hidden_ref, out):
        out[...] = mm(hidden_ref[...], c_ref[...], ROWS)

    return pl.pallas_call(
        body,
        grid=(pack, 2),
        in_specs=[
            pl.BlockSpec((rows, width), lambda h, i: (0, i)),
            pl.BlockSpec((rows, hidden_n), lambda h, i: (0, h)),
        ],
        out_specs=pl.BlockSpec((None, hidden_n, width), lambda h, i: (0, 0, h * 2 + i)),
        out_shape=shape((1, hidden_n, part * pack), F32),
        compiler_params=PARAMS,
        cost_estimate=cost(2 * rows * part * pack * hidden_n, 4 * part * pack * hidden_n),
    )(c, hidden)


def up_line(block, n, first=0, last=None):
    last = n - 1 if last is None else last
    return lax.ppermute(block, "seq", [(s, s + 1) for s in range(first, last)])


def down_line(block, n, first=1, last=None):
    last = n if last is None else last
    return lax.ppermute(block, "seq", [(s, s - 1) for s in range(first, last)])


def line_gather(block, n):
    ups, downs = [], []
    up = down = block
    for j in range(1, n):
        up = up_line(up, n, j - 1)
        down = down_line(down, n, 1, n - j + 1)
        ups.append(up)
        downs.append(down)
    plan = [(0, 0, 0)] + [(k, 2 * n - 1 - k, k) for k in range(1, n)]
    return Arrivals([block] + ups + downs, plan)


def add(*parts):
    return sum(part.astype(F32) for part in parts).astype(BF16)


def after(value, *others):
    return lax.optimization_barrier((value, *others))[0]


def line_begin(parts, n):
    if n == 4:
        return lax.ppermute(parts[4], "seq", [(3, 2), (0, 1)])
    return up_line(parts[1], n, 0, 1)


def line_sum(parts, n, begun, wait_far, wait_sum):
    if n == 4:
        ends = begun
        below = up_line(parts[3], n)
        above = down_line(parts[1], n)
        middle = after(add(parts[2], ends), *wait_far)
        far = lax.ppermute(middle, "seq", [(s, (s + 2) % 4) for s in range(4)])
        return add(parts[0], below, above, after(far, *wait_sum))
    up, down = parts[1], parts[n - 1]
    for j in range(1, n):
        if j > 1:
            up, down = add(parts[j], up), add(parts[n - j], down)
        up = begun if j == 1 else up_line(up, n, 0, j)
        down = down_line(down, n, n - j)
    return add(parts[0], up, down)


def on_device(tokens, cotangent, router, threshold, w_gate, w_up, w_down, hid_scale, picks, counts):
    experts, slots = picks.shape[1:]
    features = tokens.shape[1]
    true_hidden = w_gate.shape[2]
    extra = -true_hidden % LANES
    if extra:
        w_gate, w_up = (jnp.pad(w, ((0, 0), (0, 0), (0, extra))) for w in (w_gate, w_up))
        w_down = jnp.pad(w_down, ((0, 0), (0, extra), (0, 0)))
        hid_scale = jnp.pad(hid_scale, ((0, 0), (0, extra)))
    hidden_n = true_hidden + extra
    seq_n = lax.axis_size("seq")
    exp_n = lax.axis_size("exp")
    everyone = seq_n * exp_n
    pack = max(1, 8 // slots)
    chosen = picks[0].T

    def to_experts(block):
        block = block.reshape(experts, -1, block.shape[1])
        return lax.all_to_all(block, "exp", split_axis=0, concat_axis=0, tiled=True).reshape(-1, block.shape[2])

    c_rows, x_rows, hot = choose_rows(tokens, cotangent, chosen, counts, pack)
    c_in = line_gather(c_rows, seq_n)
    x_in = line_gather(to_experts(x_rows), seq_n)
    c = lax.all_to_all(by_place(c_in, seq_n, experts), "exp", split_axis=0, concat_axis=0, tiled=True)
    c = c.reshape(-1, c.shape[-1])
    halves = list(router.reshape(pack, features // pack, experts))
    router_side = jnp.concatenate(halves + halves, axis=1)
    router_side = jnp.pad(router_side, ((0, 0), (0, LANES - router_side.shape[1])))

    x, pre, hidden, *out = expert_forward(
        x_in, seq_n, slots, experts, pack, router_side, threshold, w_gate, w_up, w_down, hid_scale
    )
    out_begun = line_begin(out, seq_n)
    delta, *back = expert_backward(
        after(c, out_begun), seq_n, exp_n, slots, pack, x, pre, router_side, w_gate, w_up, w_down, hid_scale
    )
    back_begun = line_begin(back, seq_n)
    out = line_sum(out, seq_n, out_begun, (), (delta,))
    back = line_sum(back, seq_n, back_begun, (out,), ())
    x, c, _ = lax.optimization_barrier((x, c, back_begun))
    down_grad = down_grads(c, hidden, pack, hidden_n)
    gate_grad, up_grad = side_grads(x, delta, pack, hidden_n)
    out = to_experts(out)
    back, gate_grad, up_grad, down_grad, out = lax.optimization_barrier((back, gate_grad, up_grad, down_grad, out))
    (mixture,) = scatter_rows(out, hot)
    message = (features // pack, features // everyone, experts)
    token_grad, router_grad, threshold_grad = scatter_rows(to_experts(back), hot, message)
    if extra:
        gate_grad, up_grad = gate_grad[:, :, :true_hidden], up_grad[:, :, :true_hidden]
        down_grad = down_grad[:, :true_hidden]
    return mixture, token_grad, router_grad, threshold_grad[0], gate_grad, up_grad, down_grad


def solution(mesh):
    by_owner = P(BOTH, None)
    columns = P("exp", None, "seq")
    down = P("exp", "seq", None)
    return jax.shard_map(
        on_device,
        mesh=mesh,
        in_specs=(
            by_owner,
            by_owner,
            P(),
            P(),
            columns,
            columns,
            down,
            P("exp", "seq"),
            P(BOTH, None, None),
            by_owner,
        ),
        out_specs=(by_owner, by_owner, by_owner, P(), columns, columns, down),
        check_vma=False,
    )
```

```python
import jax
import jax.numpy as jnp
from jax import lax
from jax.experimental import pallas as pl
from jax.experimental.pallas import tpu as pltpu
from jax.sharding import PartitionSpec as P

BOTH = ("seq", "exp")
F32 = jnp.float32
BF16 = jnp.bfloat16
ROWS = ((0,), (0,))
LAST = ((1,), (1,))
STEPS = 4
LANES = 128


def mm(a, b, dims=((1,), (0,))):
    return lax.dot_general(a, b, (dims, ((), ())), preferred_element_type=F32)


PARAMS = pltpu.CompilerParams(vmem_limit_bytes=20 * 2**20)


def to_vmem(x):
    return pltpu.with_memory_space_constraint(x, pltpu.VMEM)


def to_hbm(x):
    return pltpu.with_memory_space_constraint(x, pltpu.HBM)


def held(dims, dtype=BF16):
    return pltpu.VMEM(dims, dtype)


def sent(dims, dtype=BF16):
    return pltpu.HBM(dims, dtype)


def cost(flops, moved):
    return pl.CostEstimate(flops=flops, bytes_accessed=moved, transcendentals=0)


def shape(dims, dtype=BF16):
    return jax.ShapeDtypeStruct(dims, dtype)


ANYWHERE = pl.BlockSpec(memory_space=pl.ANY)
IN_VMEM = pl.BlockSpec(memory_space=pltpu.VMEM)


def choose_rows(tokens, cotangent, picks, counts, pack):
    own, features = tokens.shape
    slots, experts = picks.shape
    count = experts * pack * slots
    part = features // pack
    width = part // STEPS

    def body(picks_ref, counts_ref, c_ref, x_ref, c_out, x_out, hot_ref, picks_s, counts_s, c_v, x_v, hot, sems):
        small = [
            pltpu.make_async_copy(picks_ref, picks_s, sems.at[2 * STEPS]),
            pltpu.make_async_copy(counts_ref, counts_s, sems.at[2 * STEPS + 1]),
        ]
        for copy in small:
            copy.start()
        large = []
        for n, (ref, held) in enumerate(((c_ref, c_v), (x_ref, x_v))):
            for j in range(STEPS):
                now = pl.ds(j * pack * width, pack * width)
                large.append(pltpu.make_async_copy(ref.at[:, now], held.at[:, now], sems.at[n * STEPS + j]))
                large[-1].start()
        for copy in small:
            copy.wait()
        dims = (count, own)
        row = lax.broadcasted_iota(jnp.int32, dims, 0)
        token = lax.broadcasted_iota(jnp.int32, dims, 1)
        place = row // (pack * slots) * slots + row % slots
        part_of = (row // slots) % pack
        want = jnp.full(dims, -1, jnp.int32)
        want_live = want
        for e in range(experts):
            for k in range(slots):
                here = place == e * slots + k
                want = jnp.where(here, picks_s[k, e], want)
                want_live = jnp.where(here, jnp.where(k < counts_s[0, e], picks_s[k, e], -1), want_live)
        for h in range(pack):
            hot[h] = jnp.where((want == token) & (part_of == h), 1.0, 0.0).astype(BF16)
            hot_ref[h] = jnp.where((want_live == token) & (part_of == h), 1.0, 0.0).astype(BF16)
        for n, (chooser, held, out_ref) in enumerate(((hot_ref, c_v, c_out), (hot, x_v, x_out))):
            for copy in large[n * STEPS : (n + 1) * STEPS]:
                copy.wait()
            for j in range(STEPS):
                out_ref[:, j * width : (j + 1) * width] = sum(
                    mm(chooser[h], held[:, h * part + j * width : h * part + (j + 1) * width]) for h in range(pack)
                ).astype(BF16)

    return pl.pallas_call(
        body,
        in_specs=[ANYWHERE] * 4,
        out_specs=[IN_VMEM] * 3,
        out_shape=[sent((count, part))] * 2 + [held((pack, count, own))],
        scratch_shapes=[
            pltpu.SMEM(picks.shape, jnp.int32),
            pltpu.SMEM(counts.shape, jnp.int32),
            pltpu.VMEM(tokens.shape, BF16),
            pltpu.VMEM(tokens.shape, BF16),
            pltpu.VMEM((pack, count, own), BF16),
            pltpu.SemaphoreType.DMA((2 * STEPS + 2,)),
        ],
        compiler_params=PARAMS,
        cost_estimate=cost(4 * count * own * features, 4 * features * own),
    )(*(to_hbm(x) for x in (picks, counts, cotangent, tokens)))


def by_place(arrivals, seq_n, groups):
    blocks = [block.reshape(groups, -1, block.shape[1]) for block in arrivals.blocks]
    _, rows, part = blocks[0].shape

    def body(*refs):
        out_ref, sems = refs[-2:]
        arrivals.start(refs[:-2], [out_ref.at[:, k] for k in range(seq_n)], sems)
        arrivals.wait(refs[:-2], [out_ref.at[:, k] for k in range(seq_n)], sems)

    return pl.pallas_call(
        body,
        in_specs=[ANYWHERE] * len(blocks),
        out_specs=IN_VMEM,
        out_shape=sent((groups, seq_n, rows, part)),
        scratch_shapes=[pltpu.SemaphoreType.DMA((seq_n,))],
        compiler_params=PARAMS,
        cost_estimate=cost(0, 4 * groups * seq_n * rows * part),
    )(*blocks)


def scatter_rows(back, hot, message=None):
    pack, count, own = hot.shape
    part = back.shape[1] if message is None else message[0]
    width = part // 2

    def body(hot_ref, back_ref, *refs):
        out_ref = refs[-1] if message is None else refs[-3]
        out_ref[...] = mm(hot_ref[...], back_ref[...], ROWS).astype(BF16)
        if message is not None:
            message_refs, router_ref, total_ref = refs[:-3], refs[-2], refs[-1]

            @pl.when((pl.program_id(0) == 0) & (pl.program_id(1) == 0))
            def _():
                experts = router_ref.shape[0]
                group = count // experts
                row = lax.broadcasted_iota(jnp.int32, (count, experts), 0)
                expert = lax.broadcasted_iota(jnp.int32, (count, experts), 1)
                mine = row // group == expert
                even = jnp.where(mine & (row % 2 == 0), 1.0, 0.0).astype(BF16)
                odd = jnp.where(mine & (row % 2 == 1), 1.0, 0.0).astype(BF16)
                router = sum(mm(even, ref[...], ROWS) for ref in message_refs)
                total = sum(mm(ref[...], odd, ROWS) for ref in message_refs)
                router_ref[...] = router[:, : router_ref.shape[1]]
                total_ref[...] = jnp.sum(total[:3], axis=0, keepdims=True)

    in_specs = [
        pl.BlockSpec((None, count, own), lambda h, i: (h, 0, 0)),
        pl.BlockSpec((count, width), lambda h, i: (0, i)),
    ]
    out_specs = [pl.BlockSpec((own, width), lambda h, i: (0, h * 2 + i))]
    out_shape = [shape((own, part * pack))]
    args = [to_vmem(hot), back]
    if message is not None:
        _, per, experts = message
        for t in range((back.shape[1] - part) // LANES):
            in_specs.append(pl.BlockSpec((count, LANES), lambda h, i, t=t: (0, part // LANES + t)))
            args.append(back)
        out_specs += [
            pl.BlockSpec((experts, per), lambda h, i: (0, 0)),
            pl.BlockSpec((1, experts), lambda h, i: (0, 0)),
        ]
        out_shape += [shape((experts, per), F32), shape((1, experts), F32)]
    return pl.pallas_call(
        body,
        grid=(pack, 2),
        in_specs=in_specs,
        out_specs=out_specs,
        out_shape=out_shape,
        compiler_params=PARAMS,
        cost_estimate=cost(2 * count * own * part * pack, 2 * part * pack * own),
    )(*args)


def regroup(value, group, outer, inner):
    return jnp.concatenate(
        [value[(o * inner + i) * group : (o * inner + i + 1) * group] for i in range(inner) for o in range(outer)]
    )


def first_part(rows, pack, slots):
    return (lax.broadcasted_iota(jnp.int32, (rows, 1), 0) // slots) % pack == 0


def fold(parts, slots):
    rows = parts[0].shape[0]
    total = parts[0]
    for h in range(1, len(parts)):
        total = total + pltpu.roll(parts[h], rows - h * slots, 0)
    return total


def spread(value, pack, slots):
    return [value if h == 0 else pltpu.roll(value, h * slots, 0) for h in range(pack)]


class Arrivals:
    def __init__(self, blocks, plan):
        self.blocks, self.plan = blocks, plan

    def start(self, refs, places, sems):
        here = lax.axis_index("seq")
        for k, (a, b, t) in enumerate(self.plan):
            if a == b:
                pltpu.make_async_copy(refs[a], places[k], sems.at[k]).start()
            else:

                @pl.when(here >= t)
                def _():
                    pltpu.make_async_copy(refs[a], places[k], sems.at[k]).start()

                @pl.when(here < t)
                def _():
                    pltpu.make_async_copy(refs[b], places[k], sems.at[k]).start()

    def wait(self, refs, places, sems):
        for k, (a, _, _) in enumerate(self.plan):
            pltpu.make_async_copy(refs[a], places[k], sems.at[k]).wait()


def hold_weights(router, w_gate, w_up, w_down, pack):
    features, experts = router.shape
    part = features // pack
    hidden_n = w_gate.shape[2]
    total = 2 * pack * hidden_n + LANES

    def body(router_ref, gate_ref, up_ref, down_ref, side, stack, router_v, sems):
        copies = [pltpu.make_async_copy(router_ref, router_v, sems.at[0])]
        for h in range(pack):
            now = pl.ds(h * part, part)
            for n, ref in enumerate((gate_ref, up_ref)):
                columns = pl.ds((2 * h + n) * hidden_n, hidden_n)
                copies.append(pltpu.make_async_copy(ref.at[0, now, :], side.at[:, columns], sems.at[len(copies)]))
            rows = pl.ds(h * hidden_n, hidden_n)
            copies.append(pltpu.make_async_copy(down_ref.at[0, :, now], stack.at[rows, :], sems.at[len(copies)]))
        for copy in copies:
            copy.start()
        copies[0].wait()
        row = lax.broadcasted_iota(jnp.int32, (experts, LANES), 0)
        lane = lax.broadcasted_iota(jnp.int32, (experts, LANES), 1)
        columns = jnp.zeros((part, LANES), F32)
        for h in range(pack):
            place = (lane == h * experts + row) | (lane == (pack + h) * experts + row)
            columns = columns + mm(router_v[h * part : (h + 1) * part, :], jnp.where(place, 1.0, 0.0).astype(BF16))
        side[:, 2 * pack * hidden_n :] = columns.astype(BF16)
        for copy in copies[1:]:
            copy.wait()

    return pl.pallas_call(
        body,
        in_specs=[ANYWHERE] * 4,
        out_specs=[IN_VMEM] * 2,
        out_shape=[held((part, total)), held((pack * hidden_n, part))],
        scratch_shapes=[pltpu.VMEM(router.shape, BF16), pltpu.SemaphoreType.DMA((3 * pack + 1,))],
        compiler_params=PARAMS,
        cost_estimate=cost(0, 12 * features * hidden_n),
    )(*(to_hbm(x) for x in (router, w_gate, w_up, w_down)))


def send_blocks(out, out_refs, seq_n, columns):
    rows = out.shape[0] // seq_n
    for k in range(seq_n):
        out_refs[k][:, columns] = out[k * rows : (k + 1) * rows]
    if len(out_refs) > seq_n:
        here = lax.axis_index("seq")

        @pl.when(here == 0)
        def _():
            out_refs[seq_n][:, columns] = out[rows : 2 * rows]

        @pl.when(here > 0)
        def _():
            out_refs[seq_n][:, columns] = out[(seq_n - 1) * rows :]


def sends(seq_n):
    return seq_n + 1 if seq_n == 4 else seq_n


def expert_forward(arrivals, seq_n, slots, experts, pack, side, stack, threshold, hid_scale):
    block_rows, part = arrivals.blocks[0].shape
    rows = block_rows * seq_n
    hidden_n = hid_scale.shape[1]
    width = part // STEPS
    group = pack * slots
    n_blocks = len(arrivals.blocks)
    n_sends = sends(seq_n)

    def body(*refs):
        blocks = refs[:n_blocks]
        side_ref, stack_ref, threshold_ref, scale_ref, x_ref, pre_ref, hidden_ref = refs[n_blocks : n_blocks + 7]
        out_refs = refs[n_blocks + 7 : n_blocks + 7 + n_sends]
        here, sems = refs[n_blocks + 7 + n_sends :]
        places = [x_ref.at[pl.ds(k * block_rows, block_rows), :] for k in range(seq_n)]
        arrivals.start(blocks, places, sems)
        arrivals.wait(blocks, places, sems)
        both = 2 * hidden_n
        columns = []
        for h in range(pack):
            y = mm(x_ref[...], side_ref[:, h * both : (h + 1) * both])
            columns += [y[:, :hidden_n], y[:, hidden_n:]]
        scores = mm(x_ref[...], side_ref[:, pack * both :])
        gate = fold(columns[0::2], slots)
        up = fold(columns[1::2], slots)
        lane = lax.broadcasted_iota(jnp.int32, scores.shape, 1)
        expert = lax.axis_index("exp")
        score = fold([jnp.where(lane == h * experts + expert, scores, 0.0) for h in range(pack)], slots)
        lane = lax.broadcasted_iota(jnp.int32, threshold_ref.shape, 1)
        cut = jnp.sum(jnp.where(lane == expert, threshold_ref[...], 0.0), axis=1, keepdims=True)
        g = jax.nn.sigmoid(jnp.sum(score, axis=1, keepdims=True) - cut)
        pre_ref[:, :hidden_n] = gate
        pre_ref[:, hidden_n:both] = up
        pre_ref[:, both:] = jnp.broadcast_to(g, (rows, LANES))
        hidden = gate * jax.nn.sigmoid(gate) * up * scale_ref[...] * g
        hidden = jnp.where(first_part(rows, pack, slots), hidden, 0.0)
        for h, value in enumerate(spread(hidden, pack, slots)):
            now = slice(h * hidden_n, (h + 1) * hidden_n)
            here[:, now] = value.astype(BF16)
            hidden_ref[:, now] = regroup(value, group, seq_n, block_rows // group).astype(BF16)
        for j in range(STEPS):
            now = slice(j * width, (j + 1) * width)
            send_blocks(mm(here[...], stack_ref[:, now]).astype(BF16), out_refs, seq_n, now)

    return pl.pallas_call(
        body,
        in_specs=[ANYWHERE] * n_blocks + [IN_VMEM] * 4,
        out_specs=[IN_VMEM] * (3 + n_sends),
        out_shape=[
            held((rows, part)),
            held((rows, 2 * hidden_n + LANES), F32),
            held((rows, pack * hidden_n)),
        ]
        + [sent((block_rows, part))] * n_sends,
        scratch_shapes=[
            pltpu.VMEM((rows, pack * hidden_n), BF16),
            pltpu.SemaphoreType.DMA((seq_n,)),
        ],
        compiler_params=PARAMS,
        cost_estimate=cost(6 * rows * part * pack * hidden_n, 6 * part * pack * hidden_n),
    )(*arrivals.blocks, to_vmem(side), to_vmem(stack), threshold.reshape(1, -1), hid_scale)


def split3(v):
    hi = v.astype(BF16)
    rest = v - hi.astype(F32)
    mid = rest.astype(BF16)
    return hi, mid, (rest - mid.astype(F32)).astype(BF16)


def riding(seq_n, group):
    return LANES * -(-2 * seq_n // group)


def expert_backward(c, seq_n, exp_n, slots, pack, x, pre, side, stack, hid_scale):
    rows, part = x.shape
    block_rows = rows // seq_n
    hidden_n = hid_scale.shape[1]
    width = part // STEPS
    total = 2 * pack * hidden_n + LANES
    group = pack * slots
    extra = riding(seq_n, group)
    per = part * pack // (seq_n * exp_n)
    n_sends = sends(seq_n)

    def body(*refs):
        c_ref, side_ref, stack_ref, x_ref, scale_ref, pre_ref, delta_ref = refs[:7]
        out_refs = refs[7 : 7 + n_sends]
        c_v, columns, message, c_sem = refs[7 + n_sends :]
        c_copy = pltpu.make_async_copy(c_ref, c_v, c_sem)
        c_copy.start()
        c_copy.wait()
        both = mm(c_v[...], stack_ref[...], LAST)
        parts = [both[:, h * hidden_n : (h + 1) * hidden_n] for h in range(pack)]
        raw = regroup(fold(parts, slots), group, block_rows // group, seq_n)
        raw = jnp.where(first_part(rows, pack, slots), raw * scale_ref[...], 0.0)
        gate = pre_ref[:, :hidden_n]
        up = pre_ref[:, hidden_n : 2 * hidden_n]
        g = pre_ref[:, 2 * hidden_n : 2 * hidden_n + 1]
        sig = jax.nn.sigmoid(gate)
        act = gate * sig
        score = jnp.sum(act * up * raw, axis=1, keepdims=True) * g * (1.0 - g)
        grad = raw * g
        to_gate = spread(grad * up * sig * (1.0 + gate * (1.0 - sig)), pack, slots)
        to_up = spread(grad * act, pack, slots)
        expert = lax.axis_index("exp")
        lane = lax.broadcasted_iota(jnp.int32, (rows, LANES), 1)
        by_expert = jnp.zeros((rows, LANES), F32)
        by_split = jnp.zeros((rows, LANES), F32)
        for h, value in enumerate(spread(jnp.broadcast_to(score, (rows, LANES)), pack, slots)):
            delta_ref[:, 2 * h * hidden_n : (2 * h + 1) * hidden_n] = to_gate[h].astype(BF16)
            delta_ref[:, (2 * h + 1) * hidden_n : (2 * h + 2) * hidden_n] = to_up[h].astype(BF16)
            for n, piece in enumerate(split3(value)):
                piece = piece.astype(F32)
                by_split = jnp.where(lane == 3 * h + n, piece, by_split)
                if n < 2:
                    by_expert = jnp.where(lane == (n * pack + h) * exp_n + expert, piece, by_expert)
        columns[...] = by_split.astype(BF16)
        delta_ref[:, 2 * pack * hidden_n :] = by_expert.astype(BF16)
        for j in range(STEPS):
            now = slice(j * width, (j + 1) * width)
            send_blocks(mm(delta_ref[...], side_ref[now, :], LAST).astype(BF16), out_refs, seq_n, now)

        here = lax.axis_index("seq")
        told = mm(columns[...], x_ref[...], ROWS)
        sub = lax.broadcasted_iota(jnp.int32, (group, LANES), 0)
        lane = lax.broadcasted_iota(jnp.int32, (group, LANES), 1)
        minus = jnp.broadcast_to(-jnp.sum(score, axis=0, keepdims=True), (group, LANES))
        pieces = [piece.astype(F32) for piece in split3(minus)]
        threshold_row = jnp.zeros((group, LANES), F32)
        for n, piece in enumerate(pieces):
            threshold_row = jnp.where(lane == n, piece, threshold_row)
        for owner in range(seq_n * exp_n):
            h, first = divmod(owner * per, part)
            shift = first % LANES
            value = jnp.sum(told[3 * h : 3 * h + 3, first - shift : first - shift + LANES], axis=0, keepdims=True)
            value = jnp.broadcast_to(value, (group, LANES))
            if shift:
                value = pltpu.roll(value, LANES - shift, 1)
            if per < LANES:
                value = jnp.where(lane < per, value, 0.0)
            d, place = divmod(owner, exp_n)
            for t in range(extra // LANES):
                row = sub + t * group
                message[d, place * group : (place + 1) * group, t * LANES : (t + 1) * LANES] = jnp.where(
                    row == 2 * here, value, jnp.where(row == 2 * here + 1, threshold_row, 0.0)
                )
        ride = [message[lax.rem(here - k + seq_n, seq_n)] for k in range(seq_n)]
        send_blocks(jnp.concatenate(ride).astype(BF16), out_refs, seq_n, slice(part, part + extra))

    return pl.pallas_call(
        body,
        in_specs=[ANYWHERE] + [IN_VMEM] * 5,
        out_specs=[IN_VMEM] * (1 + n_sends),
        out_shape=[held((rows, total))] + [sent((block_rows, part + extra))] * n_sends,
        scratch_shapes=[
            pltpu.VMEM((rows, part), BF16),
            pltpu.VMEM((rows, LANES), BF16),
            pltpu.VMEM((seq_n, block_rows, extra), F32),
            pltpu.SemaphoreType.DMA,
        ],
        compiler_params=PARAMS,
        cost_estimate=cost(6 * rows * part * pack * hidden_n, 6 * part * pack * hidden_n),
    )(c, to_vmem(side), to_vmem(stack), to_vmem(x), hid_scale, to_vmem(pre))


def side_grads(x, delta, pack, hidden_n):
    rows, part = x.shape
    width = part // STEPS

    def body(x_ref, delta_ref, gate_out, up_out):
        for h in range(pack):
            both = mm(x_ref[...], delta_ref[:, 2 * h * hidden_n : 2 * (h + 1) * hidden_n], ROWS)
            gate_out[h] = both[:, :hidden_n]
            up_out[h] = both[:, hidden_n:]

    tall = pl.BlockSpec((pack, width, hidden_n), lambda i: (0, i, 0))
    gate, up = pl.pallas_call(
        body,
        grid=(STEPS,),
        in_specs=[
            pl.BlockSpec((rows, width), lambda i: (0, i)),
            pl.BlockSpec(delta.shape, lambda i: (0, 0)),
        ],
        out_specs=[tall, tall],
        out_shape=[shape((pack, part, hidden_n), F32)] * 2,
        compiler_params=PARAMS,
        cost_estimate=cost(4 * rows * part * pack * hidden_n, 8 * part * pack * hidden_n),
    )(to_vmem(x), to_vmem(delta))
    return gate.reshape(1, part * pack, hidden_n), up.reshape(1, part * pack, hidden_n)


def down_grads(c, hidden, pack, hidden_n):
    rows, part = c.shape
    width = part // 2

    def body(c_ref, hidden_ref, out):
        out[...] = mm(hidden_ref[...], c_ref[...], ROWS)

    return pl.pallas_call(
        body,
        grid=(pack, 2),
        in_specs=[
            pl.BlockSpec((rows, width), lambda h, i: (0, i)),
            pl.BlockSpec((rows, hidden_n), lambda h, i: (0, h)),
        ],
        out_specs=pl.BlockSpec((None, hidden_n, width), lambda h, i: (0, 0, h * 2 + i)),
        out_shape=shape((1, hidden_n, part * pack), F32),
        compiler_params=PARAMS,
        cost_estimate=cost(2 * rows * part * pack * hidden_n, 4 * part * pack * hidden_n),
    )(c, to_vmem(hidden))


def up_line(block, n, first=0, last=None):
    last = n - 1 if last is None else last
    return lax.ppermute(block, "seq", [(s, s + 1) for s in range(first, last)])


def down_line(block, n, first=1, last=None):
    last = n if last is None else last
    return lax.ppermute(block, "seq", [(s, s - 1) for s in range(first, last)])


def line_gather(block, n):
    ups, downs = [], []
    up = down = block
    for j in range(1, n):
        up = up_line(up, n, j - 1)
        down = down_line(down, n, 1, n - j + 1)
        ups.append(up)
        downs.append(down)
    plan = [(0, 0, 0)] + [(k, 2 * n - 1 - k, k) for k in range(1, n)]
    return Arrivals([block] + ups + downs, plan)


def add(*parts):
    return sum(part.astype(F32) for part in parts).astype(BF16)


def after(value, *others):
    return lax.optimization_barrier((value, *others))[0]


def line_begin(parts, n):
    if n == 4:
        return lax.ppermute(parts[4], "seq", [(3, 2), (0, 1)])
    return up_line(parts[1], n, 0, 1)


def line_sum(parts, n, begun, wait_far, wait_sum):
    if n == 4:
        ends = begun
        below = up_line(parts[3], n)
        above = down_line(parts[1], n)
        middle = after(add(parts[2], ends), *wait_far)
        far = lax.ppermute(middle, "seq", [(s, (s + 2) % 4) for s in range(4)])
        return add(parts[0], below, above, after(far, *wait_sum))
    up, down = parts[1], parts[n - 1]
    for j in range(1, n):
        if j > 1:
            up, down = add(parts[j], up), add(parts[n - j], down)
        up = begun if j == 1 else up_line(up, n, 0, j)
        down = down_line(down, n, n - j)
    return add(parts[0], up, down)


def on_device(tokens, cotangent, router, threshold, w_gate, w_up, w_down, hid_scale, picks, counts):
    experts, slots = picks.shape[1:]
    features = tokens.shape[1]
    true_hidden = w_gate.shape[2]
    extra = -true_hidden % LANES
    if extra:
        w_gate, w_up = (jnp.pad(w, ((0, 0), (0, 0), (0, extra))) for w in (w_gate, w_up))
        w_down = jnp.pad(w_down, ((0, 0), (0, extra), (0, 0)))
        hid_scale = jnp.pad(hid_scale, ((0, 0), (0, extra)))
    hidden_n = true_hidden + extra
    seq_n = lax.axis_size("seq")
    exp_n = lax.axis_size("exp")
    everyone = seq_n * exp_n
    pack = max(1, 8 // slots)
    chosen = picks[0].T

    def to_experts(block):
        block = block.reshape(experts, -1, block.shape[1])
        return lax.all_to_all(block, "exp", split_axis=0, concat_axis=0, tiled=True).reshape(-1, block.shape[2])

    c_rows, x_rows, hot = choose_rows(tokens, cotangent, chosen, counts, pack)
    c_in = line_gather(c_rows, seq_n)
    x_in = line_gather(to_experts(x_rows), seq_n)
    c = lax.all_to_all(by_place(c_in, seq_n, experts), "exp", split_axis=0, concat_axis=0, tiled=True)
    c = c.reshape(-1, c.shape[-1])
    w_down, w_gate, w_up, _ = lax.optimization_barrier((w_down, w_gate, w_up, c_in.blocks[1]))
    side, stack = hold_weights(router, w_gate, w_up, w_down, pack)

    x, pre, hidden, *out = expert_forward(x_in, seq_n, slots, experts, pack, side, stack, threshold, hid_scale)
    out_begun = line_begin(out, seq_n)
    delta, *back = expert_backward(
        after(c, out_begun), seq_n, exp_n, slots, pack, x, pre, side, stack, hid_scale
    )
    back_begun = line_begin(back, seq_n)
    out = line_sum(out, seq_n, out_begun, (), (delta,))
    back = line_sum(back, seq_n, back_begun, (out,), ())
    x, c, _ = lax.optimization_barrier((x, c, back_begun))
    down_grad = down_grads(c, hidden, pack, hidden_n)
    gate_grad, up_grad = side_grads(x, delta, pack, hidden_n)
    out = to_experts(out)
    back, gate_grad, up_grad, down_grad, out = lax.optimization_barrier((back, gate_grad, up_grad, down_grad, out))
    (mixture,) = scatter_rows(out, hot)
    message = (features // pack, features // everyone, experts)
    token_grad, router_grad, threshold_grad = scatter_rows(to_experts(back), hot, message)
    if extra:
        gate_grad, up_grad = gate_grad[:, :, :true_hidden], up_grad[:, :, :true_hidden]
        down_grad = down_grad[:, :true_hidden]
    return mixture, token_grad, router_grad.T, threshold_grad[0], gate_grad, up_grad, down_grad


def solution(mesh):
    by_owner = P(BOTH, None)
    columns = P("exp", None, "seq")
    down = P("exp", "seq", None)
    return jax.shard_map(
        on_device,
        mesh=mesh,
        in_specs=(
            by_owner,
            by_owner,
            P(),
            P(),
            columns,
            columns,
            down,
            P("exp", "seq"),
            P(BOTH, None, None),
            by_owner,
        ),
        out_specs=(by_owner, by_owner, by_owner, P(), columns, columns, down),
        check_vma=False,
    )
```

```python
import jax
import jax.numpy as jnp
from jax import lax
from jax.experimental import pallas as pl
from jax.experimental.pallas import tpu as pltpu
from jax.sharding import PartitionSpec as P

BOTH = ("seq", "exp")
F32 = jnp.float32
BF16 = jnp.bfloat16
ROWS = ((0,), (0,))
LAST = ((1,), (1,))
STEPS = 4
LANES = 128


def mm(a, b, dims=((1,), (0,))):
    return lax.dot_general(a, b, (dims, ((), ())), preferred_element_type=F32)


PARAMS = pltpu.CompilerParams(vmem_limit_bytes=56 * 2**20)


def cost(flops, moved):
    return pl.CostEstimate(flops=flops, bytes_accessed=moved, transcendentals=0)


def shape(dims, dtype=BF16):
    return jax.ShapeDtypeStruct(dims, dtype)


ANYWHERE = pl.BlockSpec(memory_space=pl.ANY)
IN_VMEM = pl.BlockSpec(memory_space=pltpu.VMEM)


def choose_rows(tokens, cotangent, picks, counts, pack):
    own, features = tokens.shape
    slots, experts = picks.shape
    count = experts * pack * slots
    part = features // pack
    width = part // STEPS

    def body(picks_ref, counts_ref, c_ref, x_ref, c_out, x_out, hot_ref, picks_s, counts_s, c_v, x_v, hot, sems):
        small = [
            pltpu.make_async_copy(picks_ref, picks_s, sems.at[2 * STEPS]),
            pltpu.make_async_copy(counts_ref, counts_s, sems.at[2 * STEPS + 1]),
        ]
        for copy in small:
            copy.start()
        large = []
        for n, (ref, held) in enumerate(((c_ref, c_v), (x_ref, x_v))):
            for j in range(STEPS):
                now = pl.ds(j * pack * width, pack * width)
                large.append(pltpu.make_async_copy(ref.at[:, now], held.at[:, now], sems.at[n * STEPS + j]))
                large[-1].start()
        for copy in small:
            copy.wait()
        dims = (count, own)
        row = lax.broadcasted_iota(jnp.int32, dims, 0)
        token = lax.broadcasted_iota(jnp.int32, dims, 1)
        place = row // (pack * slots) * slots + row % slots
        part_of = (row // slots) % pack
        want = jnp.full(dims, -1, jnp.int32)
        want_live = want
        for e in range(experts):
            for k in range(slots):
                here = place == e * slots + k
                want = jnp.where(here, picks_s[k, e], want)
                want_live = jnp.where(here, jnp.where(k < counts_s[0, e], picks_s[k, e], -1), want_live)
        for h in range(pack):
            hot[h] = jnp.where((want == token) & (part_of == h), 1.0, 0.0).astype(BF16)
            hot_ref[h] = jnp.where((want_live == token) & (part_of == h), 1.0, 0.0).astype(BF16)
        for n, (chooser, held, out_ref) in enumerate(((hot_ref, c_v, c_out), (hot, x_v, x_out))):
            for copy in large[n * STEPS : (n + 1) * STEPS]:
                copy.wait()
            for j in range(STEPS):
                out_ref[:, j * width : (j + 1) * width] = sum(
                    mm(chooser[h], held[:, h * part + j * width : h * part + (j + 1) * width]) for h in range(pack)
                ).astype(BF16)

    return pl.pallas_call(
        body,
        in_specs=[ANYWHERE] * 4,
        out_specs=[IN_VMEM] * 3,
        out_shape=[shape((count, part))] * 2 + [shape((pack, count, own))],
        scratch_shapes=[
            pltpu.SMEM(picks.shape, jnp.int32),
            pltpu.SMEM(counts.shape, jnp.int32),
            pltpu.VMEM(tokens.shape, BF16),
            pltpu.VMEM(tokens.shape, BF16),
            pltpu.VMEM((pack, count, own), BF16),
            pltpu.SemaphoreType.DMA((2 * STEPS + 2,)),
        ],
        compiler_params=PARAMS,
        cost_estimate=cost(4 * count * own * features, 4 * features * own),
    )(picks, counts, cotangent, tokens)


def scatter_rows(back, hot, seq_n, message=None):
    pack, count, own = hot.shape
    rows = back.shape[0]
    extra = 0 if message is None else riding(seq_n, count // message[1])
    part = back.shape[1] - extra
    width = part // 2

    def body(hot_ref, back_ref, *refs):
        out_ref = refs[-1] if message is None else refs[-3]
        chooser = jnp.concatenate([hot_ref[...]] * seq_n, axis=0)
        out_ref[...] = mm(chooser, back_ref[...], ROWS).astype(BF16)
        if message is not None:
            message_refs, router_ref, total_ref = refs[:-3], refs[-2], refs[-1]

            @pl.when((pl.program_id(0) == 0) & (pl.program_id(1) == 0))
            def _():
                experts, per = router_ref.shape
                group = count // experts
                row = lax.broadcasted_iota(jnp.int32, (rows, experts), 0)
                expert = lax.broadcasted_iota(jnp.int32, (rows, experts), 1)
                mine = row % count // group == expert
                even = jnp.where(mine & (row % 2 == 0), 1.0, 0.0).astype(BF16)
                odd = jnp.where(mine & (row % 2 == 1), 1.0, 0.0).astype(BF16)
                router = sum(mm(even, ref[...], ROWS) for ref in message_refs)
                total = sum(mm(ref[...], odd, ROWS) for ref in message_refs)
                router_ref[...] = router[:, :per]
                total_ref[...] = jnp.sum(total[:3], axis=0, keepdims=True)

    in_specs = [
        pl.BlockSpec((None, count, own), lambda h, i: (h, 0, 0)),
        pl.BlockSpec((rows, width), lambda h, i: (0, i)),
    ]
    out_specs = [pl.BlockSpec((own, width), lambda h, i: (0, h * 2 + i))]
    out_shape = [shape((own, part * pack))]
    args = [hot, back]
    if message is not None:
        per, experts = message
        for t in range(extra // LANES):
            in_specs.append(pl.BlockSpec((rows, LANES), lambda h, i, t=t: (0, part // LANES + t)))
            args.append(back)
        out_specs += [
            pl.BlockSpec((experts, per), lambda h, i: (0, 0)),
            pl.BlockSpec((1, experts), lambda h, i: (0, 0)),
        ]
        out_shape += [shape((experts, per), F32), shape((1, experts), F32)]
    return pl.pallas_call(
        body,
        grid=(pack, 2),
        in_specs=in_specs,
        out_specs=out_specs,
        out_shape=out_shape,
        compiler_params=PARAMS,
        cost_estimate=cost(2 * rows * own * part * pack, 2 * part * pack * own),
    )(*args)


def first_part(rows, pack, slots):
    return (lax.broadcasted_iota(jnp.int32, (rows, 1), 0) // slots) % pack == 0


def fold(parts, slots):
    rows = parts[0].shape[0]
    total = parts[0]
    for h in range(1, len(parts)):
        total = total + pltpu.roll(parts[h], rows - h * slots, 0)
    return total


def spread(value, pack, slots):
    return [value if h == 0 else pltpu.roll(value, h * slots, 0) for h in range(pack)]


class Arrivals:
    def __init__(self, blocks, plan):
        self.blocks, self.plan = blocks, plan

    def start(self, refs, places, sems):
        here = lax.axis_index("seq")
        for k, (a, b, t) in enumerate(self.plan):
            if a == b:
                pltpu.make_async_copy(refs[a], places[k], sems.at[k]).start()
            else:

                @pl.when(here >= t)
                def _():
                    pltpu.make_async_copy(refs[a], places[k], sems.at[k]).start()

                @pl.when(here < t)
                def _():
                    pltpu.make_async_copy(refs[b], places[k], sems.at[k]).start()

    def wait(self, refs, places, sems):
        for k, (a, _, _) in enumerate(self.plan):
            pltpu.make_async_copy(refs[a], places[k], sems.at[k]).wait()


def side_copies(gate_ref, up_ref, router_ref, side, sems, pack, j, width):
    part = side.shape[0]
    hidden_n = gate_ref.shape[2]
    rows = pl.ds(j * width, width)
    copies = []
    for h in range(pack):
        for n, ref in enumerate((gate_ref, up_ref)):
            columns = pl.ds((2 * h + n) * hidden_n, hidden_n)
            copies.append((ref.at[0, pl.ds(h * part + j * width, width), :], side.at[rows, columns]))
    copies.append((router_ref.at[rows, :], side.at[rows, pl.ds(2 * pack * hidden_n, LANES)]))
    return [pltpu.make_async_copy(a, b, sems.at[j, n]) for n, (a, b) in enumerate(copies)]


def down_copies(down_ref, stack, sems, pack):
    hidden_n = down_ref.shape[1]
    part = stack.shape[1]
    return [
        pltpu.make_async_copy(
            down_ref.at[0, :, pl.ds(h * part, part)], stack.at[pl.ds(h * hidden_n, hidden_n), :], sems.at[h]
        )
        for h in range(pack)
    ]


def put_blocks(out, target, columns):
    seq_n, rows, _ = target.shape
    here = lax.axis_index("seq")
    for k in range(seq_n):
        target[lax.rem(here - k + seq_n, seq_n), :, columns] = out[k * rows : (k + 1) * rows]


def expert_forward(arrivals, seq_n, slots, experts, pack, router_side, threshold, w_gate, w_up, w_down, hid_scale):
    block_rows, part = arrivals.blocks[0].shape
    rows = block_rows * seq_n
    hidden_n = w_gate.shape[2]
    both = 2 * hidden_n
    width = part // STEPS
    total = pack * both + LANES
    n_blocks = len(arrivals.blocks)

    def body(*refs):
        blocks = refs[:n_blocks]
        router_ref, gate_ref, up_ref, down_ref, threshold_ref, scale_ref = refs[n_blocks : n_blocks + 6]
        x_ref, out_ref, pre_ref, hidden_ref = refs[n_blocks + 6 : n_blocks + 10]
        x_v, out_v, side, stack, x_sems, side_sems, stack_sems, out_sems = refs[n_blocks + 10 :]
        places = [x_v.at[pl.ds(k * block_rows, block_rows), :] for k in range(seq_n)]
        arrivals.start(blocks, places, x_sems)
        chunks = [side_copies(gate_ref, up_ref, router_ref, side, side_sems, pack, j, width) for j in range(STEPS)]
        downs = down_copies(down_ref, stack, stack_sems, pack)
        for copy in sum(chunks, []) + downs:
            copy.start()
        arrivals.wait(blocks, places, x_sems)
        leaving = [pltpu.make_async_copy(x_v, x_ref, out_sems.at[STEPS])]
        leaving[0].start()
        sums = [0.0] * (pack + 1)
        for j, chunk in enumerate(chunks):
            for copy in chunk:
                copy.wait()
            now = slice(j * width, (j + 1) * width)
            for n in range(pack + 1):
                sums[n] = sums[n] + mm(x_v[:, now], side[now, n * both : min((n + 1) * both, total)])
        gate = fold([y[:, :hidden_n] for y in sums[:pack]], slots)
        up = fold([y[:, hidden_n:] for y in sums[:pack]], slots)
        scores = sums[pack]
        lane = lax.broadcasted_iota(jnp.int32, scores.shape, 1)
        expert = lax.axis_index("exp")
        score = fold([jnp.where(lane == h * experts + expert, scores, 0.0) for h in range(pack)], slots)
        lane = lax.broadcasted_iota(jnp.int32, threshold_ref.shape, 1)
        cut = jnp.sum(jnp.where(lane == expert, threshold_ref[...], 0.0), axis=1, keepdims=True)
        g = jax.nn.sigmoid(jnp.sum(score, axis=1, keepdims=True) - cut)
        hidden = gate * jax.nn.sigmoid(gate) * up * scale_ref[...] * g
        hidden = jnp.where(first_part(rows, pack, slots), hidden, 0.0)
        for h, value in enumerate(spread(hidden, pack, slots)):
            hidden_ref[:, h * hidden_n : (h + 1) * hidden_n] = value.astype(BF16)
        for copy in downs:
            copy.wait()
        for j in range(STEPS):
            now = slice(j * width, (j + 1) * width)
            put_blocks(mm(hidden_ref[...], stack[:, now]).astype(BF16), out_v, now)
            columns = pl.ds(j * width, width)
            leaving.append(pltpu.make_async_copy(out_v.at[:, :, columns], out_ref.at[:, :, columns], out_sems.at[j]))
            leaving[-1].start()
        pre_ref[:, :hidden_n] = gate
        pre_ref[:, hidden_n:both] = up
        pre_ref[:, both:] = jnp.broadcast_to(g, (rows, LANES))
        for copy in leaving:
            copy.wait()

    return pl.pallas_call(
        body,
        in_specs=[ANYWHERE] * (n_blocks + 4) + [IN_VMEM] * 2,
        out_specs=[ANYWHERE] * 2 + [IN_VMEM] * 2,
        out_shape=[
            shape((rows, part)),
            shape((seq_n, block_rows, part)),
            shape((rows, both + LANES), F32),
            shape((rows, pack * hidden_n)),
        ],
        scratch_shapes=[
            pltpu.VMEM((rows, part), BF16),
            pltpu.VMEM((seq_n, block_rows, part), BF16),
            pltpu.VMEM((part, total), BF16),
            pltpu.VMEM((pack * hidden_n, part), BF16),
            pltpu.SemaphoreType.DMA((seq_n,)),
            pltpu.SemaphoreType.DMA((STEPS, 2 * pack + 1)),
            pltpu.SemaphoreType.DMA((pack,)),
            pltpu.SemaphoreType.DMA((STEPS + 1,)),
        ],
        compiler_params=PARAMS,
        cost_estimate=cost(6 * rows * part * pack * hidden_n, 6 * part * pack * hidden_n),
    )(*arrivals.blocks, router_side, w_gate, w_up, w_down, threshold.reshape(1, -1), hid_scale)


def split3(v):
    hi = v.astype(BF16)
    rest = v - hi.astype(F32)
    mid = rest.astype(BF16)
    return hi, mid, (rest - mid.astype(F32)).astype(BF16)


def riding(seq_n, group):
    return LANES * -(-2 * seq_n // group)


def expert_backward(arrivals, seq_n, exp_n, slots, pack, x, pre, router_side, w_gate, w_up, w_down, hid_scale):
    block_rows, part = arrivals.blocks[0].shape
    rows = block_rows * seq_n
    hidden_n = w_gate.shape[2]
    width = part // STEPS
    total = 2 * pack * hidden_n + LANES
    group = pack * slots
    extra = riding(seq_n, group)
    per = part * pack // (seq_n * exp_n)
    n_blocks = len(arrivals.blocks)

    def body(*refs):
        blocks = refs[:n_blocks]
        router_ref, gate_ref, up_ref, down_ref, x_ref, pre_ref, scale_ref = refs[n_blocks : n_blocks + 7]
        c_ref, out_ref, delta_ref = refs[n_blocks + 7 : n_blocks + 10]
        c_v, x_v, pre_v, out_v, side, stack, columns, c_sems, x_sems, side_sems, stack_sems, out_sems = refs[
            n_blocks + 10 :
        ]
        places = [c_v.at[pl.ds(k * block_rows, block_rows), :] for k in range(seq_n)]
        arrivals.start(blocks, places, c_sems)
        chunks = [side_copies(gate_ref, up_ref, router_ref, side, side_sems, pack, j, width) for j in range(STEPS)]
        downs = down_copies(down_ref, stack, stack_sems, pack)
        x_copy = pltpu.make_async_copy(x_ref, x_v, x_sems.at[0])
        pre_copy = pltpu.make_async_copy(pre_ref, pre_v, x_sems.at[1])
        for copy in downs + [pre_copy] + sum(chunks, []) + [x_copy]:
            copy.start()
        arrivals.wait(blocks, places, c_sems)
        leaving = [pltpu.make_async_copy(c_v, c_ref, out_sems.at[STEPS])]
        leaving[0].start()
        for copy in downs:
            copy.wait()
        both = mm(c_v[...], stack[...], LAST)
        parts = [both[:, h * hidden_n : (h + 1) * hidden_n] for h in range(pack)]
        pre_copy.wait()
        raw = jnp.where(first_part(rows, pack, slots), fold(parts, slots) * scale_ref[...], 0.0)
        gate = pre_v[:, :hidden_n]
        up = pre_v[:, hidden_n : 2 * hidden_n]
        g = pre_v[:, 2 * hidden_n : 2 * hidden_n + 1]
        sig = jax.nn.sigmoid(gate)
        act = gate * sig
        score = jnp.sum(act * up * raw, axis=1, keepdims=True) * g * (1.0 - g)
        grad = raw * g
        to_gate = spread(grad * up * sig * (1.0 + gate * (1.0 - sig)), pack, slots)
        to_up = spread(grad * act, pack, slots)
        expert = lax.axis_index("exp")
        lane = lax.broadcasted_iota(jnp.int32, (rows, LANES), 1)
        by_expert = jnp.zeros((rows, LANES), F32)
        by_split = jnp.zeros((rows, LANES), F32)
        for h, value in enumerate(spread(jnp.broadcast_to(score, (rows, LANES)), pack, slots)):
            delta_ref[:, 2 * h * hidden_n : (2 * h + 1) * hidden_n] = to_gate[h].astype(BF16)
            delta_ref[:, (2 * h + 1) * hidden_n : (2 * h + 2) * hidden_n] = to_up[h].astype(BF16)
            for n, piece in enumerate(split3(value)):
                piece = piece.astype(F32)
                by_split = jnp.where(lane == 3 * h + n, piece, by_split)
                if n < 2:
                    by_expert = jnp.where(lane == (n * pack + h) * exp_n + expert, piece, by_expert)
        columns[...] = by_split.astype(BF16)
        delta_ref[:, 2 * pack * hidden_n :] = by_expert.astype(BF16)
        for j, chunk in enumerate(chunks):
            for copy in chunk:
                copy.wait()
            now = slice(j * width, (j + 1) * width)
            put_blocks(mm(delta_ref[...], side[now, :], LAST).astype(BF16), out_v, now)
            if j + 1 < STEPS:
                now = pl.ds(j * width, width)
                leaving.append(pltpu.make_async_copy(out_v.at[:, :, now], out_ref.at[:, :, now], out_sems.at[j]))
                leaving[-1].start()

        here = lax.axis_index("seq")
        x_copy.wait()
        told = mm(columns[...], x_v[...], ROWS)
        sub = lax.broadcasted_iota(jnp.int32, (group, LANES), 0)
        lane = lax.broadcasted_iota(jnp.int32, (group, LANES), 1)
        minus = jnp.broadcast_to(-jnp.sum(score, axis=0, keepdims=True), (group, LANES))
        pieces = [piece.astype(F32) for piece in split3(minus)]
        threshold_row = jnp.zeros((group, LANES), F32)
        for n, piece in enumerate(pieces):
            threshold_row = jnp.where(lane == n, piece, threshold_row)
        for owner in range(seq_n * exp_n):
            h, first = divmod(owner * per, part)
            shift = first % LANES
            value = jnp.sum(told[3 * h : 3 * h + 3, first - shift : first - shift + LANES], axis=0, keepdims=True)
            value = jnp.broadcast_to(value, (group, LANES))
            if shift:
                value = pltpu.roll(value, LANES - shift, 1)
            if per < LANES:
                value = jnp.where(lane < per, value, 0.0)
            d, place = divmod(owner, exp_n)
            for t in range(extra // LANES):
                row = sub + t * group
                now = slice(part + t * LANES, part + (t + 1) * LANES)
                out_v[d, place * group : (place + 1) * group, now] = jnp.where(
                    row == 2 * here, value, jnp.where(row == 2 * here + 1, threshold_row, 0.0)
                ).astype(BF16)
        now = pl.ds((STEPS - 1) * width, width + extra)
        leaving.append(pltpu.make_async_copy(out_v.at[:, :, now], out_ref.at[:, :, now], out_sems.at[STEPS - 1]))
        leaving[-1].start()
        for copy in leaving:
            copy.wait()

    return pl.pallas_call(
        body,
        in_specs=[ANYWHERE] * (n_blocks + 6) + [IN_VMEM],
        out_specs=[ANYWHERE] * 2 + [IN_VMEM],
        out_shape=[
            shape((rows, part)),
            shape((seq_n, block_rows, part + extra)),
            shape((rows, total)),
        ],
        scratch_shapes=[
            pltpu.VMEM((rows, part), BF16),
            pltpu.VMEM((rows, part), BF16),
            pltpu.VMEM(pre.shape, F32),
            pltpu.VMEM((seq_n, block_rows, part + extra), BF16),
            pltpu.VMEM((part, total), BF16),
            pltpu.VMEM((pack * hidden_n, part), BF16),
            pltpu.VMEM((rows, LANES), BF16),
            pltpu.SemaphoreType.DMA((seq_n,)),
            pltpu.SemaphoreType.DMA((2,)),
            pltpu.SemaphoreType.DMA((STEPS, 2 * pack + 1)),
            pltpu.SemaphoreType.DMA((pack,)),
            pltpu.SemaphoreType.DMA((STEPS + 1,)),
        ],
        compiler_params=PARAMS,
        cost_estimate=cost(6 * rows * part * pack * hidden_n, 6 * part * pack * hidden_n),
    )(*arrivals.blocks, router_side, w_gate, w_up, w_down, x, pre, hid_scale)


def side_grads(x, delta, pack, hidden_n):
    rows, part = x.shape
    width = part // STEPS

    def body(x_ref, delta_ref, gate_out, up_out):
        for h in range(pack):
            both = mm(x_ref[...], delta_ref[:, 2 * h * hidden_n : 2 * (h + 1) * hidden_n], ROWS)
            gate_out[h] = both[:, :hidden_n]
            up_out[h] = both[:, hidden_n:]

    tall = pl.BlockSpec((pack, width, hidden_n), lambda i: (0, i, 0))
    gate, up = pl.pallas_call(
        body,
        grid=(STEPS,),
        in_specs=[
            pl.BlockSpec((rows, width), lambda i: (0, i)),
            pl.BlockSpec(delta.shape, lambda i: (0, 0)),
        ],
        out_specs=[tall, tall],
        out_shape=[shape((pack, part, hidden_n), F32)] * 2,
        compiler_params=PARAMS,
        cost_estimate=cost(4 * rows * part * pack * hidden_n, 8 * part * pack * hidden_n),
    )(x, delta)
    return gate.reshape(1, part * pack, hidden_n), up.reshape(1, part * pack, hidden_n)


def down_grads(c, hidden, pack, hidden_n):
    rows, part = c.shape
    width = part // 2

    def body(c_ref, hidden_ref, out):
        out[...] = mm(hidden_ref[...], c_ref[...], ROWS)

    return pl.pallas_call(
        body,
        grid=(pack, 2),
        in_specs=[
            pl.BlockSpec((rows, width), lambda h, i: (0, i)),
            pl.BlockSpec((rows, hidden_n), lambda h, i: (0, h)),
        ],
        out_specs=pl.BlockSpec((None, hidden_n, width), lambda h, i: (0, 0, h * 2 + i)),
        out_shape=shape((1, hidden_n, part * pack), F32),
        compiler_params=PARAMS,
        cost_estimate=cost(2 * rows * part * pack * hidden_n, 4 * part * pack * hidden_n),
    )(c, hidden)


def up_line(block, n, first=0, last=None):
    last = n - 1 if last is None else last
    return lax.ppermute(block, "seq", [(s, s + 1) for s in range(first, last)])


def down_line(block, n, first=1, last=None):
    last = n if last is None else last
    return lax.ppermute(block, "seq", [(s, s - 1) for s in range(first, last)])


def line_gather(block, n):
    ups, downs = [], []
    up = down = block
    for j in range(1, n):
        up = up_line(up, n, j - 1)
        down = down_line(down, n, 1, n - j + 1)
        ups.append(up)
        downs.append(down)
    plan = [(0, 0, 0)] + [(k, 2 * n - 1 - k, k) for k in range(1, n)]
    return Arrivals([block] + ups + downs, plan)


def after(value, *others):
    return lax.optimization_barrier((value, *others))[0]


def on_device(tokens, cotangent, router, threshold, w_gate, w_up, w_down, hid_scale, picks, counts):
    experts, slots = picks.shape[1:]
    features = tokens.shape[1]
    true_hidden = w_gate.shape[2]
    extra = -true_hidden % LANES
    if extra:
        w_gate, w_up = (jnp.pad(w, ((0, 0), (0, 0), (0, extra))) for w in (w_gate, w_up))
        w_down = jnp.pad(w_down, ((0, 0), (0, extra), (0, 0)))
        hid_scale = jnp.pad(hid_scale, ((0, 0), (0, extra)))
    hidden_n = true_hidden + extra
    seq_n = lax.axis_size("seq")
    exp_n = lax.axis_size("exp")
    everyone = seq_n * exp_n
    pack = max(1, 8 // slots)
    chosen = picks[0].T

    def to_experts(block):
        block = block.reshape(experts, -1, block.shape[1])
        return lax.all_to_all(block, "exp", split_axis=0, concat_axis=0, tiled=True).reshape(-1, block.shape[2])

    def to_owners(parts):
        parts = parts.reshape(everyone, -1, parts.shape[2])
        return lax.all_to_all(parts, BOTH, split_axis=0, concat_axis=0, tiled=True).reshape(-1, parts.shape[2])

    c_rows, x_rows, hot = choose_rows(tokens, cotangent, chosen, counts, pack)
    x_in = line_gather(to_experts(x_rows), seq_n)
    c_in = line_gather(to_experts(after(c_rows, x_in.blocks[1])), seq_n)
    halves = list(router.reshape(pack, features // pack, experts))
    router_side = jnp.concatenate(halves + halves, axis=1)
    router_side = jnp.pad(router_side, ((0, 0), (0, LANES - router_side.shape[1])))

    x_in.blocks[0] = after(x_in.blocks[0], c_in.blocks[1])
    x, out, pre, hidden = expert_forward(
        x_in, seq_n, slots, experts, pack, router_side, threshold, w_gate, w_up, w_down, hid_scale
    )
    out = to_owners(out)
    c, back, delta = expert_backward(
        c_in, seq_n, exp_n, slots, pack, x, pre, router_side, w_gate, w_up, w_down, hid_scale
    )
    back = to_owners(back)
    down_grad = down_grads(c, hidden, pack, hidden_n)
    gate_grad, up_grad = side_grads(x, delta, pack, hidden_n)
    (mixture,) = scatter_rows(out, hot, seq_n)
    token_grad, router_grad, threshold_grad = scatter_rows(back, hot, seq_n, (features // everyone, experts))
    if extra:
        gate_grad, up_grad = gate_grad[:, :, :true_hidden], up_grad[:, :, :true_hidden]
        down_grad = down_grad[:, :true_hidden]
    return mixture, token_grad, router_grad.T, threshold_grad[0], gate_grad, up_grad, down_grad


def solution(mesh):
    by_owner = P(BOTH, None)
    columns = P("exp", None, "seq")
    down = P("exp", "seq", None)
    return jax.shard_map(
        on_device,
        mesh=mesh,
        in_specs=(
            by_owner,
            by_owner,
            P(),
            P(),
            columns,
            columns,
            down,
            P("exp", "seq"),
            P(BOTH, None, None),
            by_owner,
        ),
        out_specs=(by_owner, by_owner, by_owner, P(), columns, columns, down),
        check_vma=False,
    )
```

```python
import jax
import jax.numpy as jnp
from jax import lax
from jax.experimental import pallas as pl
from jax.experimental.pallas import tpu as pltpu
from jax.sharding import PartitionSpec as P

BOTH = ("seq", "exp")
F32 = jnp.float32
BF16 = jnp.bfloat16
ROWS = ((0,), (0,))
LAST = ((1,), (1,))
STEPS = 4
LANES = 128


def mm(a, b, dims=((1,), (0,))):
    return lax.dot_general(a, b, (dims, ((), ())), preferred_element_type=F32)


PARAMS = pltpu.CompilerParams(vmem_limit_bytes=56 * 2**20)


def to_hbm(*arrays):
    return [pltpu.with_memory_space_constraint(x, pltpu.HBM) for x in arrays]


def cost(flops, moved):
    return pl.CostEstimate(flops=flops, bytes_accessed=moved, transcendentals=0)


def shape(dims, dtype=BF16):
    return jax.ShapeDtypeStruct(dims, dtype)


ANYWHERE = pl.BlockSpec(memory_space=pl.ANY)
IN_VMEM = pl.BlockSpec(memory_space=pltpu.VMEM)


def choose_rows(tokens, cotangent, picks, counts, pack):
    own, features = tokens.shape
    slots, experts = picks.shape
    count = experts * pack * slots
    part = features // pack
    width = part // STEPS

    def body(picks_ref, counts_ref, c_ref, x_ref, c_out, x_out, hot_ref, picks_s, counts_s, c_v, x_v, hot, sems):
        small = [
            pltpu.make_async_copy(picks_ref, picks_s, sems.at[2 * STEPS]),
            pltpu.make_async_copy(counts_ref, counts_s, sems.at[2 * STEPS + 1]),
        ]
        for copy in small:
            copy.start()
        large = []
        for n, (ref, held) in enumerate(((c_ref, c_v), (x_ref, x_v))):
            for j in range(STEPS):
                now = pl.ds(j * pack * width, pack * width)
                large.append(pltpu.make_async_copy(ref.at[:, now], held.at[:, now], sems.at[n * STEPS + j]))
                large[-1].start()
        for copy in small:
            copy.wait()
        dims = (count, own)
        row = lax.broadcasted_iota(jnp.int32, dims, 0)
        token = lax.broadcasted_iota(jnp.int32, dims, 1)
        place = row // (pack * slots) * slots + row % slots
        part_of = (row // slots) % pack
        want = jnp.full(dims, -1, jnp.int32)
        want_live = want
        for e in range(experts):
            for k in range(slots):
                here = place == e * slots + k
                want = jnp.where(here, picks_s[k, e], want)
                want_live = jnp.where(here, jnp.where(k < counts_s[0, e], picks_s[k, e], -1), want_live)
        for h in range(pack):
            hot[h] = jnp.where((want == token) & (part_of == h), 1.0, 0.0).astype(BF16)
            hot_ref[h] = jnp.where((want_live == token) & (part_of == h), 1.0, 0.0).astype(BF16)
        for n, (chooser, held, out_ref) in enumerate(((hot_ref, c_v, c_out), (hot, x_v, x_out))):
            for copy in large[n * STEPS : (n + 1) * STEPS]:
                copy.wait()
            for j in range(STEPS):
                out_ref[:, j * width : (j + 1) * width] = sum(
                    mm(chooser[h], held[:, h * part + j * width : h * part + (j + 1) * width]) for h in range(pack)
                ).astype(BF16)

    return pl.pallas_call(
        body,
        in_specs=[ANYWHERE] * 4,
        out_specs=[IN_VMEM] * 3,
        out_shape=[shape((count, part))] * 2 + [shape((pack, count, own))],
        scratch_shapes=[
            pltpu.SMEM(picks.shape, jnp.int32),
            pltpu.SMEM(counts.shape, jnp.int32),
            pltpu.VMEM(tokens.shape, BF16),
            pltpu.VMEM(tokens.shape, BF16),
            pltpu.VMEM((pack, count, own), BF16),
            pltpu.SemaphoreType.DMA((2 * STEPS + 2,)),
        ],
        compiler_params=PARAMS,
        cost_estimate=cost(4 * count * own * features, 4 * features * own),
    )(*to_hbm(picks, counts, cotangent, tokens))


def by_place(arrivals, seq_n, groups):
    blocks = [block.reshape(groups, -1, block.shape[1]) for block in arrivals.blocks]
    _, rows, part = blocks[0].shape

    def body(*refs):
        out_ref, sems = refs[-2:]
        arrivals.start(refs[:-2], [out_ref.at[:, k] for k in range(seq_n)], sems)
        arrivals.wait(refs[:-2], [out_ref.at[:, k] for k in range(seq_n)], sems)

    return pl.pallas_call(
        body,
        in_specs=[ANYWHERE] * len(blocks),
        out_specs=IN_VMEM,
        out_shape=shape((groups, seq_n, rows, part)),
        scratch_shapes=[pltpu.SemaphoreType.DMA((seq_n,))],
        compiler_params=PARAMS,
        cost_estimate=cost(0, 4 * groups * seq_n * rows * part),
    )(*to_hbm(*blocks))


def scatter_rows(back, hot, seq_n, message=None):
    pack, count, own = hot.shape
    rows = back.shape[0]
    extra = 0 if message is None else riding(seq_n, count // message[1])
    part = back.shape[1] - extra
    width = part // STEPS

    def body(hot_ref, back_ref, *refs):
        hot_v, back_v, out_v, hot_sem, in_sems, out_sems = refs[-6:]
        out_ref = refs[0]
        hot_copy = pltpu.make_async_copy(hot_ref, hot_v, hot_sem)
        hot_copy.start()
        arriving = []
        for i in range(STEPS):
            now = pl.ds(i * width, width + (extra if i + 1 == STEPS else 0))
            arriving.append(pltpu.make_async_copy(back_ref.at[:, now], back_v.at[:, now], in_sems.at[i]))
            arriving[-1].start()
        hot_copy.wait()
        choosers = [jnp.concatenate([hot_v[h]] * seq_n, axis=0) for h in range(pack)]
        leaving = []
        for i in range(STEPS):
            arriving[i].wait()
            for h in range(pack):
                first = h * part + i * width
                rows_now = back_v[:, i * width : (i + 1) * width]
                out_v[:, first : first + width] = mm(choosers[h], rows_now, ROWS).astype(BF16)
                now = pl.ds(first, width)
                leaving.append(pltpu.make_async_copy(out_v.at[:, now], out_ref.at[:, now], out_sems.at[h, i]))
                leaving[-1].start()
        if message is not None:
            router_ref, total_ref = refs[1], refs[2]
            experts, per = router_ref.shape
            group = count // experts
            row = lax.broadcasted_iota(jnp.int32, (rows, experts), 0)
            expert = lax.broadcasted_iota(jnp.int32, (rows, experts), 1)
            mine = row % count // group == expert
            even = jnp.where(mine & (row % 2 == 0), 1.0, 0.0).astype(BF16)
            odd = jnp.where(mine & (row % 2 == 1), 1.0, 0.0).astype(BF16)
            rides = [back_v[:, part + t * LANES : part + (t + 1) * LANES] for t in range(extra // LANES)]
            router = sum(mm(even, ride, ROWS) for ride in rides)
            total = sum(mm(ride, odd, ROWS) for ride in rides)
            router_ref[...] = router[:, :per]
            total_ref[...] = jnp.sum(total[:3], axis=0, keepdims=True)
        for copy in leaving:
            copy.wait()

    out_specs = [ANYWHERE]
    out_shape = [shape((own, part * pack))]
    if message is not None:
        per, experts = message
        out_specs += [IN_VMEM] * 2
        out_shape += [shape((experts, per), F32), shape((1, experts), F32)]
    return pl.pallas_call(
        body,
        in_specs=[ANYWHERE] * 2,
        out_specs=out_specs,
        out_shape=out_shape,
        scratch_shapes=[
            pltpu.VMEM(hot.shape, BF16),
            pltpu.VMEM(back.shape, BF16),
            pltpu.VMEM((own, part * pack), BF16),
            pltpu.SemaphoreType.DMA,
            pltpu.SemaphoreType.DMA((STEPS,)),
            pltpu.SemaphoreType.DMA((pack, STEPS)),
        ],
        compiler_params=PARAMS,
        cost_estimate=cost(2 * rows * own * part * pack, 2 * part * pack * own),
    )(*to_hbm(hot, back))


def regroup(value, group, outer, inner):
    return jnp.concatenate(
        [value[(o * inner + i) * group : (o * inner + i + 1) * group] for i in range(inner) for o in range(outer)]
    )


def first_part(rows, pack, slots):
    return (lax.broadcasted_iota(jnp.int32, (rows, 1), 0) // slots) % pack == 0


def fold(parts, slots):
    rows = parts[0].shape[0]
    total = parts[0]
    for h in range(1, len(parts)):
        total = total + pltpu.roll(parts[h], rows - h * slots, 0)
    return total


def spread(value, pack, slots):
    return [value if h == 0 else pltpu.roll(value, h * slots, 0) for h in range(pack)]


class Arrivals:
    def __init__(self, blocks, plan):
        self.blocks, self.plan = blocks, plan

    def start(self, refs, places, sems):
        here = lax.axis_index("seq")
        for k, (a, b, t) in enumerate(self.plan):
            if a == b:
                pltpu.make_async_copy(refs[a], places[k], sems.at[k]).start()
            else:

                @pl.when(here >= t)
                def _():
                    pltpu.make_async_copy(refs[a], places[k], sems.at[k]).start()

                @pl.when(here < t)
                def _():
                    pltpu.make_async_copy(refs[b], places[k], sems.at[k]).start()

    def wait(self, refs, places, sems):
        for k, (a, _, _) in enumerate(self.plan):
            pltpu.make_async_copy(refs[a], places[k], sems.at[k]).wait()


def side_copies(gate_ref, up_ref, router_ref, side, sems, pack, j, width):
    part = side.shape[0]
    hidden_n = gate_ref.shape[2]
    rows = pl.ds(j * width, width)
    copies = []
    for h in range(pack):
        for n, ref in enumerate((gate_ref, up_ref)):
            columns = pl.ds((2 * h + n) * hidden_n, hidden_n)
            copies.append((ref.at[0, pl.ds(h * part + j * width, width), :], side.at[rows, columns]))
    copies.append((router_ref.at[rows, :], side.at[rows, pl.ds(2 * pack * hidden_n, LANES)]))
    return [pltpu.make_async_copy(a, b, sems.at[j, n]) for n, (a, b) in enumerate(copies)]


def down_copies(down_ref, stack, sems, pack):
    hidden_n = down_ref.shape[1]
    part = stack.shape[1]
    return [
        pltpu.make_async_copy(
            down_ref.at[0, :, pl.ds(h * part, part)], stack.at[pl.ds(h * hidden_n, hidden_n), :], sems.at[h]
        )
        for h in range(pack)
    ]


def put_blocks(out, target, columns):
    seq_n, rows, _ = target.shape
    here = lax.axis_index("seq")
    for k in range(seq_n):
        target[lax.rem(here - k + seq_n, seq_n), :, columns] = out[k * rows : (k + 1) * rows]


def expert_forward(arrivals, seq_n, slots, experts, pack, router_side, threshold, w_gate, w_up, w_down, hid_scale):
    block_rows, part = arrivals.blocks[0].shape
    rows = block_rows * seq_n
    hidden_n = w_gate.shape[2]
    both = 2 * hidden_n
    group = pack * slots
    width = part // STEPS
    total = pack * both + LANES
    n_blocks = len(arrivals.blocks)

    def body(*refs):
        blocks = refs[:n_blocks]
        router_ref, gate_ref, up_ref, down_ref, threshold_ref, scale_ref = refs[n_blocks : n_blocks + 6]
        x_ref, out_ref, pre_ref, hidden_ref = refs[n_blocks + 6 : n_blocks + 10]
        pre_v, hidden_v, other_v, x_v, out_v, side, stack, x_sems, side_sems, stack_sems, out_sems = refs[n_blocks + 10 :]
        places = [x_v.at[pl.ds(k * block_rows, block_rows), :] for k in range(seq_n)]
        arrivals.start(blocks, places, x_sems)
        chunks = [side_copies(gate_ref, up_ref, router_ref, side, side_sems, pack, j, width) for j in range(STEPS)]
        downs = down_copies(down_ref, stack, stack_sems, pack)
        for copy in sum(chunks, []) + downs:
            copy.start()
        arrivals.wait(blocks, places, x_sems)
        leaving = [pltpu.make_async_copy(x_v, x_ref, out_sems.at[STEPS])]
        leaving[0].start()
        sums = [0.0] * (pack + 1)
        for j, chunk in enumerate(chunks):
            for copy in chunk:
                copy.wait()
            now = slice(j * width, (j + 1) * width)
            for n in range(pack + 1):
                sums[n] = sums[n] + mm(x_v[:, now], side[now, n * both : min((n + 1) * both, total)])
        gate = fold([y[:, :hidden_n] for y in sums[:pack]], slots)
        up = fold([y[:, hidden_n:] for y in sums[:pack]], slots)
        scores = sums[pack]
        lane = lax.broadcasted_iota(jnp.int32, scores.shape, 1)
        expert = lax.axis_index("exp")
        score = fold([jnp.where(lane == h * experts + expert, scores, 0.0) for h in range(pack)], slots)
        lane = lax.broadcasted_iota(jnp.int32, threshold_ref.shape, 1)
        cut = jnp.sum(jnp.where(lane == expert, threshold_ref[...], 0.0), axis=1, keepdims=True)
        g = jax.nn.sigmoid(jnp.sum(score, axis=1, keepdims=True) - cut)
        hidden = gate * jax.nn.sigmoid(gate) * up * scale_ref[...] * g
        hidden = jnp.where(first_part(rows, pack, slots), hidden, 0.0)
        for h, value in enumerate(spread(hidden, pack, slots)):
            now = slice(h * hidden_n, (h + 1) * hidden_n)
            hidden_v[:, now] = value.astype(BF16)
            other_v[:, now] = regroup(value, group, seq_n, block_rows // group).astype(BF16)
        pre_v[:, :hidden_n] = gate
        pre_v[:, hidden_n:both] = up
        pre_v[:, both:] = jnp.broadcast_to(g, (rows, LANES))
        leaving.append(pltpu.make_async_copy(pre_v, pre_ref, out_sems.at[STEPS + 1]))
        leaving.append(pltpu.make_async_copy(other_v, hidden_ref, out_sems.at[STEPS + 2]))
        for copy in leaving[1:]:
            copy.start()
        for copy in downs:
            copy.wait()
        for j in range(STEPS):
            now = slice(j * width, (j + 1) * width)
            put_blocks(mm(hidden_v[...], stack[:, now]).astype(BF16), out_v, now)
            columns = pl.ds(j * width, width)
            leaving.append(pltpu.make_async_copy(out_v.at[:, :, columns], out_ref.at[:, :, columns], out_sems.at[j]))
            leaving[-1].start()
        for copy in leaving:
            copy.wait()

    return pl.pallas_call(
        body,
        in_specs=[ANYWHERE] * (n_blocks + 4) + [IN_VMEM] * 2,
        out_specs=[ANYWHERE] * 4,
        out_shape=[
            shape((rows, part)),
            shape((seq_n, block_rows, part)),
            shape((rows, both + LANES), F32),
            shape((rows, pack * hidden_n)),
        ],
        scratch_shapes=[
            pltpu.VMEM((rows, both + LANES), F32),
            pltpu.VMEM((rows, pack * hidden_n), BF16),
            pltpu.VMEM((rows, pack * hidden_n), BF16),
            pltpu.VMEM((rows, part), BF16),
            pltpu.VMEM((seq_n, block_rows, part), BF16),
            pltpu.VMEM((part, total), BF16),
            pltpu.VMEM((pack * hidden_n, part), BF16),
            pltpu.SemaphoreType.DMA((seq_n,)),
            pltpu.SemaphoreType.DMA((STEPS, 2 * pack + 1)),
            pltpu.SemaphoreType.DMA((pack,)),
            pltpu.SemaphoreType.DMA((STEPS + 3,)),
        ],
        compiler_params=PARAMS,
        cost_estimate=cost(rows * part, rows * part),
    )(*to_hbm(*arrivals.blocks, router_side, w_gate, w_up, w_down), threshold.reshape(1, -1), hid_scale)


def split3(v):
    hi = v.astype(BF16)
    rest = v - hi.astype(F32)
    mid = rest.astype(BF16)
    return hi, mid, (rest - mid.astype(F32)).astype(BF16)


def riding(seq_n, group):
    return LANES * -(-2 * seq_n // group)


def expert_backward(c, seq_n, exp_n, slots, pack, x, pre, router_side, w_gate, w_up, w_down, hid_scale):
    rows, part = c.shape
    block_rows = rows // seq_n
    hidden_n = w_gate.shape[2]
    width = part // STEPS
    total = 2 * pack * hidden_n + LANES
    group = pack * slots
    extra = riding(seq_n, group)
    per = part * pack // (seq_n * exp_n)

    def body(*refs):
        c_ref, router_ref, gate_ref, up_ref, down_ref, x_ref, pre_ref, scale_ref, out_ref, delta_ref = refs[:10]
        c_v, x_v, pre_v, out_v, side, stack, columns, x_sems, side_sems, stack_sems, out_sems = refs[10:]
        c_copy = pltpu.make_async_copy(c_ref, c_v, x_sems.at[2])
        c_copy.start()
        chunks = [side_copies(gate_ref, up_ref, router_ref, side, side_sems, pack, j, width) for j in range(STEPS)]
        downs = down_copies(down_ref, stack, stack_sems, pack)
        x_copy = pltpu.make_async_copy(x_ref, x_v, x_sems.at[0])
        pre_copy = pltpu.make_async_copy(pre_ref, pre_v, x_sems.at[1])
        for copy in downs + [pre_copy] + sum(chunks, []) + [x_copy]:
            copy.start()
        c_copy.wait()
        leaving = []
        for copy in downs:
            copy.wait()
        both = mm(c_v[...], stack[...], LAST)
        parts = [both[:, h * hidden_n : (h + 1) * hidden_n] for h in range(pack)]
        pre_copy.wait()
        raw = regroup(fold(parts, slots), group, block_rows // group, seq_n)
        raw = jnp.where(first_part(rows, pack, slots), raw * scale_ref[...], 0.0)
        gate = pre_v[:, :hidden_n]
        up = pre_v[:, hidden_n : 2 * hidden_n]
        g = pre_v[:, 2 * hidden_n : 2 * hidden_n + 1]
        sig = jax.nn.sigmoid(gate)
        act = gate * sig
        score = jnp.sum(act * up * raw, axis=1, keepdims=True) * g * (1.0 - g)
        grad = raw * g
        to_gate = spread(grad * up * sig * (1.0 + gate * (1.0 - sig)), pack, slots)
        to_up = spread(grad * act, pack, slots)
        expert = lax.axis_index("exp")
        lane = lax.broadcasted_iota(jnp.int32, (rows, LANES), 1)
        by_expert = jnp.zeros((rows, LANES), F32)
        by_split = jnp.zeros((rows, LANES), F32)
        for h, value in enumerate(spread(jnp.broadcast_to(score, (rows, LANES)), pack, slots)):
            delta_ref[:, 2 * h * hidden_n : (2 * h + 1) * hidden_n] = to_gate[h].astype(BF16)
            delta_ref[:, (2 * h + 1) * hidden_n : (2 * h + 2) * hidden_n] = to_up[h].astype(BF16)
            for n, piece in enumerate(split3(value)):
                piece = piece.astype(F32)
                by_split = jnp.where(lane == 3 * h + n, piece, by_split)
                if n < 2:
                    by_expert = jnp.where(lane == (n * pack + h) * exp_n + expert, piece, by_expert)
        columns[...] = by_split.astype(BF16)
        delta_ref[:, 2 * pack * hidden_n :] = by_expert.astype(BF16)
        for j, chunk in enumerate(chunks):
            for copy in chunk:
                copy.wait()
            now = slice(j * width, (j + 1) * width)
            put_blocks(mm(delta_ref[...], side[now, :], LAST).astype(BF16), out_v, now)
            if j + 1 < STEPS:
                now = pl.ds(j * width, width)
                leaving.append(pltpu.make_async_copy(out_v.at[:, :, now], out_ref.at[:, :, now], out_sems.at[j]))
                leaving[-1].start()

        here = lax.axis_index("seq")
        x_copy.wait()
        told = mm(columns[...], x_v[...], ROWS)
        sub = lax.broadcasted_iota(jnp.int32, (group, LANES), 0)
        lane = lax.broadcasted_iota(jnp.int32, (group, LANES), 1)
        minus = jnp.broadcast_to(-jnp.sum(score, axis=0, keepdims=True), (group, LANES))
        pieces = [piece.astype(F32) for piece in split3(minus)]
        threshold_row = jnp.zeros((group, LANES), F32)
        for n, piece in enumerate(pieces):
            threshold_row = jnp.where(lane == n, piece, threshold_row)
        for owner in range(seq_n * exp_n):
            h, first = divmod(owner * per, part)
            shift = first % LANES
            value = jnp.sum(told[3 * h : 3 * h + 3, first - shift : first - shift + LANES], axis=0, keepdims=True)
            value = jnp.broadcast_to(value, (group, LANES))
            if shift:
                value = pltpu.roll(value, LANES - shift, 1)
            if per < LANES:
                value = jnp.where(lane < per, value, 0.0)
            d, place = divmod(owner, exp_n)
            for t in range(extra // LANES):
                row = sub + t * group
                now = slice(part + t * LANES, part + (t + 1) * LANES)
                out_v[d, place * group : (place + 1) * group, now] = jnp.where(
                    row == 2 * here, value, jnp.where(row == 2 * here + 1, threshold_row, 0.0)
                ).astype(BF16)
        now = pl.ds((STEPS - 1) * width, width + extra)
        leaving.append(pltpu.make_async_copy(out_v.at[:, :, now], out_ref.at[:, :, now], out_sems.at[STEPS - 1]))
        leaving[-1].start()
        for copy in leaving:
            copy.wait()

    return pl.pallas_call(
        body,
        in_specs=[ANYWHERE] * 7 + [IN_VMEM],
        out_specs=[ANYWHERE, IN_VMEM],
        out_shape=[
            shape((seq_n, block_rows, part + extra)),
            shape((rows, total)),
        ],
        scratch_shapes=[
            pltpu.VMEM((rows, part), BF16),
            pltpu.VMEM((rows, part), BF16),
            pltpu.VMEM(pre.shape, F32),
            pltpu.VMEM((seq_n, block_rows, part + extra), BF16),
            pltpu.VMEM((part, total), BF16),
            pltpu.VMEM((pack * hidden_n, part), BF16),
            pltpu.VMEM((rows, LANES), BF16),
            pltpu.SemaphoreType.DMA((3,)),
            pltpu.SemaphoreType.DMA((STEPS, 2 * pack + 1)),
            pltpu.SemaphoreType.DMA((pack,)),
            pltpu.SemaphoreType.DMA((STEPS,)),
        ],
        compiler_params=PARAMS,
        cost_estimate=cost(6 * rows * part * pack * hidden_n, 6 * part * pack * hidden_n),
    )(*to_hbm(c, router_side, w_gate, w_up, w_down, x, pre), hid_scale)


def side_grads(x, delta, pack, hidden_n):
    rows, part = x.shape
    width = part // STEPS

    def body(x_ref, delta_ref, gate_out, up_out):
        for h in range(pack):
            both = mm(x_ref[...], delta_ref[:, 2 * h * hidden_n : 2 * (h + 1) * hidden_n], ROWS)
            gate_out[h] = both[:, :hidden_n]
            up_out[h] = both[:, hidden_n:]

    tall = pl.BlockSpec((pack, width, hidden_n), lambda i: (0, i, 0))
    gate, up = pl.pallas_call(
        body,
        grid=(STEPS,),
        in_specs=[
            pl.BlockSpec((rows, width), lambda i: (0, i)),
            pl.BlockSpec(delta.shape, lambda i: (0, 0)),
        ],
        out_specs=[tall, tall],
        out_shape=[shape((pack, part, hidden_n), F32)] * 2,
        compiler_params=PARAMS,
        cost_estimate=cost(4 * rows * part * pack * hidden_n, 8 * part * pack * hidden_n),
    )(*to_hbm(x, delta))
    return gate.reshape(1, part * pack, hidden_n), up.reshape(1, part * pack, hidden_n)


def down_grads(c, hidden, pack, hidden_n):
    rows, part = c.shape
    width = part // 2

    def body(c_ref, hidden_ref, out):
        out[...] = mm(hidden_ref[...], c_ref[...], ROWS)

    return pl.pallas_call(
        body,
        grid=(pack, 2),
        in_specs=[
            pl.BlockSpec((rows, width), lambda h, i: (0, i)),
            pl.BlockSpec((rows, hidden_n), lambda h, i: (0, h)),
        ],
        out_specs=pl.BlockSpec((None, hidden_n, width), lambda h, i: (0, 0, h * 2 + i)),
        out_shape=shape((1, hidden_n, part * pack), F32),
        compiler_params=PARAMS,
        cost_estimate=cost(2 * rows * part * pack * hidden_n, 4 * part * pack * hidden_n),
    )(*to_hbm(c, hidden))


def up_line(block, n, first=0, last=None):
    last = n - 1 if last is None else last
    return lax.ppermute(block, "seq", [(s, s + 1) for s in range(first, last)])


def down_line(block, n, first=1, last=None):
    last = n if last is None else last
    return lax.ppermute(block, "seq", [(s, s - 1) for s in range(first, last)])


def line_gather(block, n, hold=()):
    ups, downs = [], []
    up = down = block
    for j in range(1, n):
        up = up_line(up, n, j - 1)
        down = down_line(down, n, 1, n - j + 1)
        if j == 1 and hold:
            up, down, *_ = lax.optimization_barrier((up, down, *hold))
        ups.append(up)
        downs.append(down)
    plan = [(0, 0, 0)] + [(k, 2 * n - 1 - k, k) for k in range(1, n)]
    return Arrivals([block] + ups + downs, plan)


def on_device(tokens, cotangent, router, threshold, w_gate, w_up, w_down, hid_scale, picks, counts):
    experts, slots = picks.shape[1:]
    features = tokens.shape[1]
    true_hidden = w_gate.shape[2]
    extra = -true_hidden % LANES
    if extra:
        w_gate, w_up = (jnp.pad(w, ((0, 0), (0, 0), (0, extra))) for w in (w_gate, w_up))
        w_down = jnp.pad(w_down, ((0, 0), (0, extra), (0, 0)))
        hid_scale = jnp.pad(hid_scale, ((0, 0), (0, extra)))
    hidden_n = true_hidden + extra
    seq_n = lax.axis_size("seq")
    exp_n = lax.axis_size("exp")
    everyone = seq_n * exp_n
    pack = max(1, 8 // slots)
    chosen = picks[0].T

    def to_experts(block):
        block = block.reshape(experts, -1, block.shape[1])
        return lax.all_to_all(block, "exp", split_axis=0, concat_axis=0, tiled=True).reshape(-1, block.shape[2])

    def to_owners(parts):
        parts = parts.reshape(everyone, -1, parts.shape[2])
        return lax.all_to_all(parts, BOTH, split_axis=0, concat_axis=0, tiled=True).reshape(-1, parts.shape[2])

    c_rows, x_rows, hot = choose_rows(tokens, cotangent, chosen, counts, pack)
    c_in = line_gather(c_rows, seq_n)
    c_sent = by_place(c_in, seq_n, experts)
    x_in = line_gather(to_experts(x_rows), seq_n, (c_sent,))
    c = lax.all_to_all(c_sent, "exp", split_axis=0, concat_axis=0, tiled=True)
    c = c.reshape(-1, c.shape[-1])
    halves = list(router.reshape(pack, features // pack, experts))
    router_side = jnp.concatenate(halves + halves, axis=1)
    router_side = jnp.pad(router_side, ((0, 0), (0, LANES - router_side.shape[1])))

    x, out, pre, hidden = expert_forward(
        x_in, seq_n, slots, experts, pack, router_side, threshold, w_gate, w_up, w_down, hid_scale
    )
    out = to_owners(out)
    back, delta = expert_backward(
        c, seq_n, exp_n, slots, pack, x, pre, router_side, w_gate, w_up, w_down, hid_scale
    )
    back, out = lax.optimization_barrier((back, out))
    back = to_owners(back)
    down_grad = down_grads(c, hidden, pack, hidden_n)
    gate_grad, up_grad = side_grads(x, delta, pack, hidden_n)
    (mixture,) = scatter_rows(out, hot, seq_n)
    token_grad, router_grad, threshold_grad = scatter_rows(back, hot, seq_n, (features // everyone, experts))
    if extra:
        gate_grad, up_grad = gate_grad[:, :, :true_hidden], up_grad[:, :, :true_hidden]
        down_grad = down_grad[:, :true_hidden]
    return mixture, token_grad, router_grad.T, threshold_grad[0], gate_grad, up_grad, down_grad


def solution(mesh):
    by_owner = P(BOTH, None)
    columns = P("exp", None, "seq")
    down = P("exp", "seq", None)
    return jax.shard_map(
        on_device,
        mesh=mesh,
        in_specs=(
            by_owner,
            by_owner,
            P(),
            P(),
            columns,
            columns,
            down,
            P("exp", "seq"),
            P(BOTH, None, None),
            by_owner,
        ),
        out_specs=(by_owner, by_owner, by_owner, P(), columns, columns, down),
        check_vma=False,
    )
```

```python
import jax
import jax.numpy as jnp
from jax import lax
from jax.experimental import pallas as pl
from jax.experimental.pallas import tpu as pltpu
from jax.sharding import PartitionSpec as P

BOTH = ("seq", "exp")
F32 = jnp.float32
BF16 = jnp.bfloat16
ROWS = ((0,), (0,))
LAST = ((1,), (1,))
STEPS = 4
LANES = 128


def mm(a, b, dims=((1,), (0,))):
    return lax.dot_general(a, b, (dims, ((), ())), preferred_element_type=F32)


PARAMS = pltpu.CompilerParams(vmem_limit_bytes=56 * 2**20)
SMALL = pltpu.CompilerParams(vmem_limit_bytes=12 * 2**20)


def to_hbm(*arrays):
    return [pltpu.with_memory_space_constraint(x, pltpu.HBM) for x in arrays]


def cost(flops, moved):
    return pl.CostEstimate(flops=flops, bytes_accessed=moved, transcendentals=0)


def shape(dims, dtype=BF16):
    return jax.ShapeDtypeStruct(dims, dtype)


ANYWHERE = pl.BlockSpec(memory_space=pl.ANY)
IN_VMEM = pl.BlockSpec(memory_space=pltpu.VMEM)


def choose_rows(tokens, cotangent, picks, counts, pack):
    own, features = tokens.shape
    slots, experts = picks.shape
    count = experts * pack * slots
    part = features // pack
    width = part // STEPS

    def body(picks_ref, counts_ref, c_ref, x_ref, c_out, x_out, hot_ref, picks_s, counts_s, c_v, x_v, hot, sems):
        small = [
            pltpu.make_async_copy(picks_ref, picks_s, sems.at[2 * STEPS]),
            pltpu.make_async_copy(counts_ref, counts_s, sems.at[2 * STEPS + 1]),
        ]
        for copy in small:
            copy.start()
        large = []
        for n, (ref, held) in enumerate(((c_ref, c_v), (x_ref, x_v))):
            for j in range(STEPS):
                now = pl.ds(j * pack * width, pack * width)
                large.append(pltpu.make_async_copy(ref.at[:, now], held.at[:, now], sems.at[n * STEPS + j]))
                large[-1].start()
        for copy in small:
            copy.wait()
        dims = (count, own)
        row = lax.broadcasted_iota(jnp.int32, dims, 0)
        token = lax.broadcasted_iota(jnp.int32, dims, 1)
        place = row // (pack * slots) * slots + row % slots
        part_of = (row // slots) % pack
        want = jnp.full(dims, -1, jnp.int32)
        want_live = want
        for e in range(experts):
            for k in range(slots):
                here = place == e * slots + k
                want = jnp.where(here, picks_s[k, e], want)
                want_live = jnp.where(here, jnp.where(k < counts_s[0, e], picks_s[k, e], -1), want_live)
        for h in range(pack):
            hot[h] = jnp.where((want == token) & (part_of == h), 1.0, 0.0).astype(BF16)
            hot_ref[h] = jnp.where((want_live == token) & (part_of == h), 1.0, 0.0).astype(BF16)
        for n, (chooser, held, out_ref) in enumerate(((hot_ref, c_v, c_out), (hot, x_v, x_out))):
            for copy in large[n * STEPS : (n + 1) * STEPS]:
                copy.wait()
            for j in range(STEPS):
                out_ref[:, j * width : (j + 1) * width] = sum(
                    mm(chooser[h], held[:, h * part + j * width : h * part + (j + 1) * width]) for h in range(pack)
                ).astype(BF16)

    return pl.pallas_call(
        body,
        in_specs=[ANYWHERE] * 4,
        out_specs=[IN_VMEM] * 3,
        out_shape=[shape((count, part))] * 2 + [shape((pack, count, own))],
        scratch_shapes=[
            pltpu.SMEM(picks.shape, jnp.int32),
            pltpu.SMEM(counts.shape, jnp.int32),
            pltpu.VMEM(tokens.shape, BF16),
            pltpu.VMEM(tokens.shape, BF16),
            pltpu.VMEM((pack, count, own), BF16),
            pltpu.SemaphoreType.DMA((2 * STEPS + 2,)),
        ],
        compiler_params=PARAMS,
        cost_estimate=cost(4 * count * own * features, 4 * features * own),
    )(*to_hbm(picks, counts, cotangent, tokens))


def by_place(arrivals, seq_n, groups):
    blocks = [block.reshape(groups, -1, block.shape[1]) for block in arrivals.blocks]
    _, rows, part = blocks[0].shape

    def body(*refs):
        out_ref, sems = refs[-2:]
        arrivals.start(refs[:-2], [out_ref.at[:, k] for k in range(seq_n)], sems)
        arrivals.wait(refs[:-2], [out_ref.at[:, k] for k in range(seq_n)], sems)

    return pl.pallas_call(
        body,
        in_specs=[ANYWHERE] * len(blocks),
        out_specs=IN_VMEM,
        out_shape=shape((groups, seq_n, rows, part)),
        scratch_shapes=[pltpu.SemaphoreType.DMA((seq_n,))],
        compiler_params=PARAMS,
        cost_estimate=cost(0, 4 * groups * seq_n * rows * part),
    )(*to_hbm(*blocks))


def scatter_rows(back, hot, seq_n, message=None):
    pack, count, own = hot.shape
    rows = back.shape[0]
    extra = 0 if message is None else riding(seq_n, count // message[1])
    part = back.shape[1] - extra
    width = part // STEPS

    def body(hot_ref, back_ref, *refs):
        hot_v, back_v, out_v, hot_sem, in_sems, out_sems = refs[-6:]
        out_ref = refs[0]
        hot_copy = pltpu.make_async_copy(hot_ref, hot_v, hot_sem)
        hot_copy.start()
        arriving = []
        for i in range(STEPS):
            now = pl.ds(i * width, width + (extra if i + 1 == STEPS else 0))
            arriving.append(pltpu.make_async_copy(back_ref.at[:, now], back_v.at[:, now], in_sems.at[i]))
            arriving[-1].start()
        hot_copy.wait()
        choosers = [jnp.concatenate([hot_v[h]] * seq_n, axis=0) for h in range(pack)]
        leaving = []
        for i in range(STEPS):
            arriving[i].wait()
            for h in range(pack):
                first = h * part + i * width
                rows_now = back_v[:, i * width : (i + 1) * width]
                out_v[:, first : first + width] = mm(choosers[h], rows_now, ROWS).astype(BF16)
                now = pl.ds(first, width)
                leaving.append(pltpu.make_async_copy(out_v.at[:, now], out_ref.at[:, now], out_sems.at[h, i]))
                leaving[-1].start()
        if message is not None:
            router_ref, total_ref = refs[1], refs[2]
            experts, per = router_ref.shape
            group = count // experts
            row = lax.broadcasted_iota(jnp.int32, (rows, experts), 0)
            expert = lax.broadcasted_iota(jnp.int32, (rows, experts), 1)
            mine = row % count // group == expert
            even = jnp.where(mine & (row % 2 == 0), 1.0, 0.0).astype(BF16)
            odd = jnp.where(mine & (row % 2 == 1), 1.0, 0.0).astype(BF16)
            rides = [back_v[:, part + t * LANES : part + (t + 1) * LANES] for t in range(extra // LANES)]
            router = sum(mm(even, ride, ROWS) for ride in rides)
            total = sum(mm(ride, odd, ROWS) for ride in rides)
            router_ref[...] = router[:, :per]
            total_ref[...] = jnp.sum(total[:3], axis=0, keepdims=True)
        for copy in leaving:
            copy.wait()

    out_specs = [ANYWHERE]
    out_shape = [shape((own, part * pack))]
    if message is not None:
        per, experts = message
        out_specs += [IN_VMEM] * 2
        out_shape += [shape((experts, per), F32), shape((1, experts), F32)]
    return pl.pallas_call(
        body,
        in_specs=[ANYWHERE] * 2,
        out_specs=out_specs,
        out_shape=out_shape,
        scratch_shapes=[
            pltpu.VMEM(hot.shape, BF16),
            pltpu.VMEM(back.shape, BF16),
            pltpu.VMEM((own, part * pack), BF16),
            pltpu.SemaphoreType.DMA,
            pltpu.SemaphoreType.DMA((STEPS,)),
            pltpu.SemaphoreType.DMA((pack, STEPS)),
        ],
        compiler_params=SMALL,
        cost_estimate=cost(2 * rows * own * part * pack, 2 * part * pack * own),
    )(*to_hbm(hot), back)


def regroup(value, group, outer, inner):
    return jnp.concatenate(
        [value[(o * inner + i) * group : (o * inner + i + 1) * group] for i in range(inner) for o in range(outer)]
    )


def first_part(rows, pack, slots):
    return (lax.broadcasted_iota(jnp.int32, (rows, 1), 0) // slots) % pack == 0


def fold(parts, slots):
    rows = parts[0].shape[0]
    total = parts[0]
    for h in range(1, len(parts)):
        total = total + pltpu.roll(parts[h], rows - h * slots, 0)
    return total


def spread(value, pack, slots):
    return [value if h == 0 else pltpu.roll(value, h * slots, 0) for h in range(pack)]


class Arrivals:
    def __init__(self, blocks, plan):
        self.blocks, self.plan = blocks, plan

    def start(self, refs, places, sems):
        here = lax.axis_index("seq")
        for k, (a, b, t) in enumerate(self.plan):
            if a == b:
                pltpu.make_async_copy(refs[a], places[k], sems.at[k]).start()
            else:

                @pl.when(here >= t)
                def _():
                    pltpu.make_async_copy(refs[a], places[k], sems.at[k]).start()

                @pl.when(here < t)
                def _():
                    pltpu.make_async_copy(refs[b], places[k], sems.at[k]).start()

    def wait(self, refs, places, sems):
        for k, (a, _, _) in enumerate(self.plan):
            pltpu.make_async_copy(refs[a], places[k], sems.at[k]).wait()


def side_copies(gate_ref, up_ref, router_ref, side, sems, pack, j, width):
    part = side.shape[0]
    hidden_n = gate_ref.shape[2]
    rows = pl.ds(j * width, width)
    copies = []
    for h in range(pack):
        for n, ref in enumerate((gate_ref, up_ref)):
            columns = pl.ds((2 * h + n) * hidden_n, hidden_n)
            copies.append((ref.at[0, pl.ds(h * part + j * width, width), :], side.at[rows, columns]))
    copies.append((router_ref.at[rows, :], side.at[rows, pl.ds(2 * pack * hidden_n, LANES)]))
    return [pltpu.make_async_copy(a, b, sems.at[j, n]) for n, (a, b) in enumerate(copies)]


def down_copies(down_ref, stack, sems, pack):
    hidden_n = down_ref.shape[1]
    part = stack.shape[1]
    return [
        pltpu.make_async_copy(
            down_ref.at[0, :, pl.ds(h * part, part)], stack.at[pl.ds(h * hidden_n, hidden_n), :], sems.at[h]
        )
        for h in range(pack)
    ]


def put_blocks(out, target, columns):
    seq_n, rows, _ = target.shape
    here = lax.axis_index("seq")
    for k in range(seq_n):
        target[lax.rem(here - k + seq_n, seq_n), :, columns] = out[k * rows : (k + 1) * rows]


def expert_forward(arrivals, seq_n, slots, experts, pack, router_side, threshold, w_gate, w_up, w_down, hid_scale):
    block_rows, part = arrivals.blocks[0].shape
    rows = block_rows * seq_n
    hidden_n = w_gate.shape[2]
    both = 2 * hidden_n
    group = pack * slots
    width = part // STEPS
    total = pack * both + LANES
    n_blocks = len(arrivals.blocks)

    def body(*refs):
        blocks = refs[:n_blocks]
        router_ref, gate_ref, up_ref, down_ref, threshold_ref, scale_ref = refs[n_blocks : n_blocks + 6]
        x_ref, out_ref, pre_ref, hidden_ref = refs[n_blocks + 6 : n_blocks + 10]
        pre_v, hidden_v, other_v, x_v, out_v, side, stack, x_sems, side_sems, stack_sems, out_sems = refs[n_blocks + 10 :]
        places = [x_v.at[pl.ds(k * block_rows, block_rows), :] for k in range(seq_n)]
        arrivals.start(blocks, places, x_sems)
        chunks = [side_copies(gate_ref, up_ref, router_ref, side, side_sems, pack, j, width) for j in range(STEPS)]
        downs = down_copies(down_ref, stack, stack_sems, pack)
        for copy in sum(chunks, []) + downs:
            copy.start()
        arrivals.wait(blocks, places, x_sems)
        leaving = [pltpu.make_async_copy(x_v, x_ref, out_sems.at[STEPS])]
        leaving[0].start()
        sums = [0.0] * (pack + 1)
        for j, chunk in enumerate(chunks):
            for copy in chunk:
                copy.wait()
            now = slice(j * width, (j + 1) * width)
            for n in range(pack + 1):
                sums[n] = sums[n] + mm(x_v[:, now], side[now, n * both : min((n + 1) * both, total)])
        gate = fold([y[:, :hidden_n] for y in sums[:pack]], slots)
        up = fold([y[:, hidden_n:] for y in sums[:pack]], slots)
        scores = sums[pack]
        lane = lax.broadcasted_iota(jnp.int32, scores.shape, 1)
        expert = lax.axis_index("exp")
        score = fold([jnp.where(lane == h * experts + expert, scores, 0.0) for h in range(pack)], slots)
        lane = lax.broadcasted_iota(jnp.int32, threshold_ref.shape, 1)
        cut = jnp.sum(jnp.where(lane == expert, threshold_ref[...], 0.0), axis=1, keepdims=True)
        g = jax.nn.sigmoid(jnp.sum(score, axis=1, keepdims=True) - cut)
        hidden = gate * jax.nn.sigmoid(gate) * up * scale_ref[...] * g
        hidden = jnp.where(first_part(rows, pack, slots), hidden, 0.0)
        for h, value in enumerate(spread(hidden, pack, slots)):
            now = slice(h * hidden_n, (h + 1) * hidden_n)
            hidden_v[:, now] = value.astype(BF16)
            other_v[:, now] = regroup(value, group, seq_n, block_rows // group).astype(BF16)
        pre_v[:, :hidden_n] = gate
        pre_v[:, hidden_n:both] = up
        pre_v[:, both:] = jnp.broadcast_to(g, (rows, LANES))
        leaving.append(pltpu.make_async_copy(pre_v, pre_ref, out_sems.at[STEPS + 1]))
        leaving.append(pltpu.make_async_copy(other_v, hidden_ref, out_sems.at[STEPS + 2]))
        for copy in leaving[1:]:
            copy.start()
        for copy in downs:
            copy.wait()
        for j in range(STEPS):
            now = slice(j * width, (j + 1) * width)
            put_blocks(mm(hidden_v[...], stack[:, now]).astype(BF16), out_v, now)
            columns = pl.ds(j * width, width)
            leaving.append(pltpu.make_async_copy(out_v.at[:, :, columns], out_ref.at[:, :, columns], out_sems.at[j]))
            leaving[-1].start()
        for copy in leaving:
            copy.wait()

    return pl.pallas_call(
        body,
        in_specs=[ANYWHERE] * (n_blocks + 4) + [IN_VMEM] * 2,
        out_specs=[ANYWHERE] * 4,
        out_shape=[
            shape((rows, part)),
            shape((seq_n, block_rows, part)),
            shape((rows, both + LANES), F32),
            shape((rows, pack * hidden_n)),
        ],
        scratch_shapes=[
            pltpu.VMEM((rows, both + LANES), F32),
            pltpu.VMEM((rows, pack * hidden_n), BF16),
            pltpu.VMEM((rows, pack * hidden_n), BF16),
            pltpu.VMEM((rows, part), BF16),
            pltpu.VMEM((seq_n, block_rows, part), BF16),
            pltpu.VMEM((part, total), BF16),
            pltpu.VMEM((pack * hidden_n, part), BF16),
            pltpu.SemaphoreType.DMA((seq_n,)),
            pltpu.SemaphoreType.DMA((STEPS, 2 * pack + 1)),
            pltpu.SemaphoreType.DMA((pack,)),
            pltpu.SemaphoreType.DMA((STEPS + 3,)),
        ],
        compiler_params=PARAMS,
        cost_estimate=cost(rows * part, rows * part),
    )(*to_hbm(*arrivals.blocks, router_side, w_gate, w_up, w_down), threshold.reshape(1, -1), hid_scale)


def split3(v):
    hi = v.astype(BF16)
    rest = v - hi.astype(F32)
    mid = rest.astype(BF16)
    return hi, mid, (rest - mid.astype(F32)).astype(BF16)


def riding(seq_n, group):
    return LANES * -(-2 * seq_n // group)


def expert_backward(c, seq_n, exp_n, slots, pack, x, pre, router_side, w_gate, w_up, w_down, hid_scale):
    rows, part = c.shape
    block_rows = rows // seq_n
    hidden_n = w_gate.shape[2]
    width = part // STEPS
    total = 2 * pack * hidden_n + LANES
    group = pack * slots
    extra = riding(seq_n, group)
    per = part * pack // (seq_n * exp_n)

    def body(*refs):
        c_ref, router_ref, gate_ref, up_ref, down_ref, x_ref, pre_ref, scale_ref, out_ref, delta_ref = refs[:10]
        c_v, x_v, pre_v, out_v, side, stack, columns, x_sems, side_sems, stack_sems, out_sems = refs[10:]
        c_copy = pltpu.make_async_copy(c_ref, c_v, x_sems.at[2])
        c_copy.start()
        chunks = [side_copies(gate_ref, up_ref, router_ref, side, side_sems, pack, j, width) for j in range(STEPS)]
        downs = down_copies(down_ref, stack, stack_sems, pack)
        x_copy = pltpu.make_async_copy(x_ref, x_v, x_sems.at[0])
        pre_copy = pltpu.make_async_copy(pre_ref, pre_v, x_sems.at[1])
        for copy in downs + [pre_copy] + sum(chunks, []) + [x_copy]:
            copy.start()
        c_copy.wait()
        leaving = []
        for copy in downs:
            copy.wait()
        both = mm(c_v[...], stack[...], LAST)
        parts = [both[:, h * hidden_n : (h + 1) * hidden_n] for h in range(pack)]
        pre_copy.wait()
        raw = regroup(fold(parts, slots), group, block_rows // group, seq_n)
        raw = jnp.where(first_part(rows, pack, slots), raw * scale_ref[...], 0.0)
        gate = pre_v[:, :hidden_n]
        up = pre_v[:, hidden_n : 2 * hidden_n]
        g = pre_v[:, 2 * hidden_n : 2 * hidden_n + 1]
        sig = jax.nn.sigmoid(gate)
        act = gate * sig
        score = jnp.sum(act * up * raw, axis=1, keepdims=True) * g * (1.0 - g)
        grad = raw * g
        to_gate = spread(grad * up * sig * (1.0 + gate * (1.0 - sig)), pack, slots)
        to_up = spread(grad * act, pack, slots)
        expert = lax.axis_index("exp")
        lane = lax.broadcasted_iota(jnp.int32, (rows, LANES), 1)
        by_expert = jnp.zeros((rows, LANES), F32)
        by_split = jnp.zeros((rows, LANES), F32)
        for h, value in enumerate(spread(jnp.broadcast_to(score, (rows, LANES)), pack, slots)):
            delta_ref[:, 2 * h * hidden_n : (2 * h + 1) * hidden_n] = to_gate[h].astype(BF16)
            delta_ref[:, (2 * h + 1) * hidden_n : (2 * h + 2) * hidden_n] = to_up[h].astype(BF16)
            for n, piece in enumerate(split3(value)):
                piece = piece.astype(F32)
                by_split = jnp.where(lane == 3 * h + n, piece, by_split)
                if n < 2:
                    by_expert = jnp.where(lane == (n * pack + h) * exp_n + expert, piece, by_expert)
        columns[...] = by_split.astype(BF16)
        delta_ref[:, 2 * pack * hidden_n :] = by_expert.astype(BF16)
        for j, chunk in enumerate(chunks):
            for copy in chunk:
                copy.wait()
            now = slice(j * width, (j + 1) * width)
            put_blocks(mm(delta_ref[...], side[now, :], LAST).astype(BF16), out_v, now)
            if j + 1 < STEPS:
                now = pl.ds(j * width, width)
                leaving.append(pltpu.make_async_copy(out_v.at[:, :, now], out_ref.at[:, :, now], out_sems.at[j]))
                leaving[-1].start()

        here = lax.axis_index("seq")
        x_copy.wait()
        told = mm(columns[...], x_v[...], ROWS)
        sub = lax.broadcasted_iota(jnp.int32, (group, LANES), 0)
        lane = lax.broadcasted_iota(jnp.int32, (group, LANES), 1)
        minus = jnp.broadcast_to(-jnp.sum(score, axis=0, keepdims=True), (group, LANES))
        pieces = [piece.astype(F32) for piece in split3(minus)]
        threshold_row = jnp.zeros((group, LANES), F32)
        for n, piece in enumerate(pieces):
            threshold_row = jnp.where(lane == n, piece, threshold_row)
        for owner in range(seq_n * exp_n):
            h, first = divmod(owner * per, part)
            shift = first % LANES
            value = jnp.sum(told[3 * h : 3 * h + 3, first - shift : first - shift + LANES], axis=0, keepdims=True)
            value = jnp.broadcast_to(value, (group, LANES))
            if shift:
                value = pltpu.roll(value, LANES - shift, 1)
            if per < LANES:
                value = jnp.where(lane < per, value, 0.0)
            d, place = divmod(owner, exp_n)
            for t in range(extra // LANES):
                row = sub + t * group
                now = slice(part + t * LANES, part + (t + 1) * LANES)
                out_v[d, place * group : (place + 1) * group, now] = jnp.where(
                    row == 2 * here, value, jnp.where(row == 2 * here + 1, threshold_row, 0.0)
                ).astype(BF16)
        now = pl.ds((STEPS - 1) * width, width + extra)
        leaving.append(pltpu.make_async_copy(out_v.at[:, :, now], out_ref.at[:, :, now], out_sems.at[STEPS - 1]))
        leaving[-1].start()
        for copy in leaving:
            copy.wait()

    return pl.pallas_call(
        body,
        in_specs=[ANYWHERE] * 7 + [IN_VMEM],
        out_specs=[ANYWHERE, IN_VMEM],
        out_shape=[
            shape((seq_n, block_rows, part + extra)),
            shape((rows, total)),
        ],
        scratch_shapes=[
            pltpu.VMEM((rows, part), BF16),
            pltpu.VMEM((rows, part), BF16),
            pltpu.VMEM(pre.shape, F32),
            pltpu.VMEM((seq_n, block_rows, part + extra), BF16),
            pltpu.VMEM((part, total), BF16),
            pltpu.VMEM((pack * hidden_n, part), BF16),
            pltpu.VMEM((rows, LANES), BF16),
            pltpu.SemaphoreType.DMA((3,)),
            pltpu.SemaphoreType.DMA((STEPS, 2 * pack + 1)),
            pltpu.SemaphoreType.DMA((pack,)),
            pltpu.SemaphoreType.DMA((STEPS,)),
        ],
        compiler_params=PARAMS,
        cost_estimate=cost(6 * rows * part * pack * hidden_n, 6 * part * pack * hidden_n),
    )(*to_hbm(c, router_side, w_gate, w_up, w_down, x, pre), hid_scale)


def side_grads(x, delta, pack, hidden_n):
    rows, part = x.shape
    width = part // STEPS

    def body(x_ref, delta_ref, gate_out, up_out):
        for h in range(pack):
            both = mm(x_ref[...], delta_ref[:, 2 * h * hidden_n : 2 * (h + 1) * hidden_n], ROWS)
            gate_out[h] = both[:, :hidden_n]
            up_out[h] = both[:, hidden_n:]

    tall = pl.BlockSpec((pack, width, hidden_n), lambda i: (0, i, 0))
    gate, up = pl.pallas_call(
        body,
        grid=(STEPS,),
        in_specs=[
            pl.BlockSpec((rows, width), lambda i: (0, i)),
            pl.BlockSpec(delta.shape, lambda i: (0, 0)),
        ],
        out_specs=[tall, tall],
        out_shape=[shape((pack, part, hidden_n), F32)] * 2,
        compiler_params=PARAMS,
        cost_estimate=cost(4 * rows * part * pack * hidden_n, 8 * part * pack * hidden_n),
    )(*to_hbm(x, delta))
    return gate.reshape(1, part * pack, hidden_n), up.reshape(1, part * pack, hidden_n)


def down_grads(c, hidden, pack, hidden_n):
    rows, part = c.shape
    width = part // 2

    def body(c_ref, hidden_ref, out):
        out[...] = mm(hidden_ref[...], c_ref[...], ROWS)

    return pl.pallas_call(
        body,
        grid=(pack, 2),
        in_specs=[
            pl.BlockSpec((rows, width), lambda h, i: (0, i)),
            pl.BlockSpec((rows, hidden_n), lambda h, i: (0, h)),
        ],
        out_specs=pl.BlockSpec((None, hidden_n, width), lambda h, i: (0, 0, h * 2 + i)),
        out_shape=shape((1, hidden_n, part * pack), F32),
        compiler_params=PARAMS,
        cost_estimate=cost(2 * rows * part * pack * hidden_n, 4 * part * pack * hidden_n),
    )(*to_hbm(c, hidden))


def up_line(block, n, first=0, last=None):
    last = n - 1 if last is None else last
    return lax.ppermute(block, "seq", [(s, s + 1) for s in range(first, last)])


def down_line(block, n, first=1, last=None):
    last = n if last is None else last
    return lax.ppermute(block, "seq", [(s, s - 1) for s in range(first, last)])


def line_gather(block, n, hold, step):
    ups, downs = [], []
    up = down = block
    for j in range(1, n):
        if j == step:
            up, down, _ = lax.optimization_barrier((up, down, hold))
        up = up_line(up, n, j - 1)
        down = down_line(down, n, 1, n - j + 1)
        ups.append(up)
        downs.append(down)
    plan = [(0, 0, 0)] + [(k, 2 * n - 1 - k, k) for k in range(1, n)]
    return Arrivals([block] + ups + downs, plan)


def on_device(tokens, cotangent, router, threshold, w_gate, w_up, w_down, hid_scale, picks, counts):
    experts, slots = picks.shape[1:]
    features = tokens.shape[1]
    true_hidden = w_gate.shape[2]
    extra = -true_hidden % LANES
    if extra:
        w_gate, w_up = (jnp.pad(w, ((0, 0), (0, 0), (0, extra))) for w in (w_gate, w_up))
        w_down = jnp.pad(w_down, ((0, 0), (0, extra), (0, 0)))
        hid_scale = jnp.pad(hid_scale, ((0, 0), (0, extra)))
    hidden_n = true_hidden + extra
    seq_n = lax.axis_size("seq")
    exp_n = lax.axis_size("exp")
    everyone = seq_n * exp_n
    pack = max(1, 8 // slots)
    chosen = picks[0].T

    def to_experts(block):
        block = block.reshape(experts, -1, block.shape[1])
        return lax.all_to_all(block, "exp", split_axis=0, concat_axis=0, tiled=True).reshape(-1, block.shape[2])

    def to_owners(parts):
        parts = parts.reshape(everyone, -1, parts.shape[2])
        return lax.all_to_all(parts, BOTH, split_axis=0, concat_axis=0, tiled=True).reshape(-1, parts.shape[2])

    c_rows, x_rows, hot = choose_rows(tokens, cotangent, chosen, counts, pack)
    x_rows = to_experts(x_rows)
    c_in = line_gather(c_rows, seq_n, x_rows, 2)
    c_sent = by_place(c_in, seq_n, experts)
    x_in = line_gather(x_rows, seq_n, c_sent, 3)
    c = lax.all_to_all(c_sent, "exp", split_axis=0, concat_axis=0, tiled=True)
    c = c.reshape(-1, c.shape[-1])
    halves = list(router.reshape(pack, features // pack, experts))
    router_side = jnp.concatenate(halves + halves, axis=1)
    router_side = jnp.pad(router_side, ((0, 0), (0, LANES - router_side.shape[1])))

    x, out, pre, hidden = expert_forward(
        x_in, seq_n, slots, experts, pack, router_side, threshold, w_gate, w_up, w_down, hid_scale
    )
    out = to_owners(out)
    back, delta = expert_backward(
        c, seq_n, exp_n, slots, pack, x, pre, router_side, w_gate, w_up, w_down, hid_scale
    )
    back, out = lax.optimization_barrier((back, out))
    back = to_owners(back)
    down_grad = down_grads(c, hidden, pack, hidden_n)
    gate_grad, up_grad = side_grads(x, delta, pack, hidden_n)
    (mixture,) = scatter_rows(out, hot, seq_n)
    token_grad, router_grad, threshold_grad = scatter_rows(back, hot, seq_n, (features // everyone, experts))
    if extra:
        gate_grad, up_grad = gate_grad[:, :, :true_hidden], up_grad[:, :, :true_hidden]
        down_grad = down_grad[:, :true_hidden]
    return mixture, token_grad, router_grad.T, threshold_grad[0], gate_grad, up_grad, down_grad


def solution(mesh):
    by_owner = P(BOTH, None)
    columns = P("exp", None, "seq")
    down = P("exp", "seq", None)
    return jax.shard_map(
        on_device,
        mesh=mesh,
        in_specs=(
            by_owner,
            by_owner,
            P(),
            P(),
            columns,
            columns,
            down,
            P("exp", "seq"),
            P(BOTH, None, None),
            by_owner,
        ),
        out_specs=(by_owner, by_owner, by_owner, P(), columns, columns, down),
        check_vma=False,
    )
```

```python
import jax
import jax.numpy as jnp
from jax import lax
from jax.experimental import pallas as pl
from jax.experimental.pallas import tpu as pltpu
from jax.sharding import PartitionSpec as P

BOTH = ("seq", "exp")
F32 = jnp.float32
BF16 = jnp.bfloat16
ROWS = ((0,), (0,))
LAST = ((1,), (1,))
STEPS = 4
LANES = 128


def mm(a, b, dims=((1,), (0,))):
    return lax.dot_general(a, b, (dims, ((), ())), preferred_element_type=F32)


PARAMS = pltpu.CompilerParams(vmem_limit_bytes=56 * 2**20)
SMALL = pltpu.CompilerParams(vmem_limit_bytes=12 * 2**20)


def to_hbm(*arrays):
    return [pltpu.with_memory_space_constraint(x, pltpu.HBM) for x in arrays]


def cost(flops, moved):
    return pl.CostEstimate(flops=flops, bytes_accessed=moved, transcendentals=0)


def shape(dims, dtype=BF16):
    return jax.ShapeDtypeStruct(dims, dtype)


ANYWHERE = pl.BlockSpec(memory_space=pl.ANY)
IN_VMEM = pl.BlockSpec(memory_space=pltpu.VMEM)


def choose_rows(tokens, cotangent, picks, counts, pack):
    own, features = tokens.shape
    slots, experts = picks.shape
    group = pack * slots
    count = 2 * experts * group
    part = features // pack
    width = part // STEPS

    def body(picks_ref, counts_ref, c_ref, x_ref, out_ref, hot_ref, picks_s, counts_s, c_v, x_v, out_v, sems, out_sems):
        small = [
            pltpu.make_async_copy(picks_ref, picks_s, sems.at[2 * STEPS]),
            pltpu.make_async_copy(counts_ref, counts_s, sems.at[2 * STEPS + 1]),
        ]
        for copy in small:
            copy.start()
        large = []
        for j in range(STEPS):
            now = pl.ds(j * pack * width, pack * width)
            large.append(pltpu.make_async_copy(x_ref.at[:, now], x_v.at[:, now], sems.at[2 * j]))
            large.append(pltpu.make_async_copy(c_ref.at[:, now], c_v.at[:, now], sems.at[2 * j + 1]))
        for copy in large:
            copy.start()
        for copy in small:
            copy.wait()
        dims = (count, own)
        row = lax.broadcasted_iota(jnp.int32, dims, 0)
        token = lax.broadcasted_iota(jnp.int32, dims, 1)
        second = (row // group) % 2
        place = (row // (2 * group) * slots + row % slots) * 2 + second
        want = jnp.full(dims, -1, jnp.int32)
        for e in range(experts):
            for k in range(slots):
                index = (e * slots + k) * 2
                want = jnp.where(place == index, picks_s[k, e], want)
                live = jnp.where(k < counts_s[0, e], picks_s[k, e], -1)
                want = jnp.where(place == index + 1, live, want)
        found = (want == token) & (second == 0)
        found_live = (want == token) & (second == 1)
        part_of = (row // slots) % pack
        chosen = [jnp.where(found & (part_of == h), 1.0, 0.0).astype(BF16) for h in range(pack)]
        live = [jnp.where(found_live & (part_of == h), 1.0, 0.0) for h in range(pack)]
        for h in range(pack):
            hot_ref[h] = jnp.concatenate(
                [live[h][(2 * e + 1) * group : (2 * e + 2) * group] for e in range(experts)]
            ).astype(BF16)
        live = [value.astype(BF16) for value in live]
        for copy in large:
            copy.wait()
        leaving = []
        for j in range(STEPS):
            total = 0.0
            for h in range(pack):
                now = slice(h * part + j * width, h * part + (j + 1) * width)
                total = total + mm(chosen[h], x_v[:, now]) + mm(live[h], c_v[:, now])
            out_v[:, j * width : (j + 1) * width] = total.astype(BF16)
            now = pl.ds(j * width, width)
            leaving.append(pltpu.make_async_copy(out_v.at[:, now], out_ref.at[:, now], out_sems.at[j]))
            leaving[-1].start()
        for copy in leaving:
            copy.wait()

    return pl.pallas_call(
        body,
        in_specs=[ANYWHERE] * 4,
        out_specs=[ANYWHERE, IN_VMEM],
        out_shape=[shape((count, part)), shape((pack, count // 2, own))],
        scratch_shapes=[
            pltpu.SMEM(picks.shape, jnp.int32),
            pltpu.SMEM(counts.shape, jnp.int32),
            pltpu.VMEM(tokens.shape, BF16),
            pltpu.VMEM(tokens.shape, BF16),
            pltpu.VMEM((count, part), BF16),
            pltpu.SemaphoreType.DMA((2 * STEPS + 2,)),
            pltpu.SemaphoreType.DMA((STEPS,)),
        ],
        compiler_params=PARAMS,
        cost_estimate=cost(4 * count * own * features, 4 * features * own),
    )(*to_hbm(picks, counts, cotangent, tokens))


def scatter_rows(back, hot, seq_n, message=None):
    pack, count, own = hot.shape
    rows = back.shape[0]
    extra = 0 if message is None else riding(seq_n, count // message[1])
    part = back.shape[1] - extra
    width = part // STEPS

    def body(hot_ref, back_ref, *refs):
        hot_v, back_v, out_v, hot_sem, in_sems, out_sems = refs[-6:]
        out_ref = refs[0]
        hot_copy = pltpu.make_async_copy(hot_ref, hot_v, hot_sem)
        hot_copy.start()
        arriving = []
        for i in range(STEPS):
            now = pl.ds(i * width, width + (extra if i + 1 == STEPS else 0))
            arriving.append(pltpu.make_async_copy(back_ref.at[:, now], back_v.at[:, now], in_sems.at[i]))
            arriving[-1].start()
        hot_copy.wait()
        choosers = [jnp.concatenate([hot_v[h]] * seq_n, axis=0) for h in range(pack)]
        leaving = []
        for i in range(STEPS):
            arriving[i].wait()
            for h in range(pack):
                first = h * part + i * width
                rows_now = back_v[:, i * width : (i + 1) * width]
                out_v[:, first : first + width] = mm(choosers[h], rows_now, ROWS).astype(BF16)
                now = pl.ds(first, width)
                leaving.append(pltpu.make_async_copy(out_v.at[:, now], out_ref.at[:, now], out_sems.at[h, i]))
                leaving[-1].start()
        if message is not None:
            router_ref, total_ref = refs[1], refs[2]
            experts, per = router_ref.shape
            group = count // experts
            row = lax.broadcasted_iota(jnp.int32, (rows, experts), 0)
            expert = lax.broadcasted_iota(jnp.int32, (rows, experts), 1)
            mine = row % count // group == expert
            even = jnp.where(mine & (row % 2 == 0), 1.0, 0.0).astype(BF16)
            odd = jnp.where(mine & (row % 2 == 1), 1.0, 0.0).astype(BF16)
            rides = [back_v[:, part + t * LANES : part + (t + 1) * LANES] for t in range(extra // LANES)]
            router = sum(mm(even, ride, ROWS) for ride in rides)
            total = sum(mm(ride, odd, ROWS) for ride in rides)
            router_ref[...] = router[:, :per]
            total_ref[...] = jnp.sum(total[:3], axis=0, keepdims=True)
        for copy in leaving:
            copy.wait()

    out_specs = [ANYWHERE]
    out_shape = [shape((own, part * pack))]
    if message is not None:
        per, experts = message
        out_specs += [IN_VMEM] * 2
        out_shape += [shape((experts, per), F32), shape((1, experts), F32)]
    return pl.pallas_call(
        body,
        in_specs=[ANYWHERE] * 2,
        out_specs=out_specs,
        out_shape=out_shape,
        scratch_shapes=[
            pltpu.VMEM(hot.shape, BF16),
            pltpu.VMEM(back.shape, BF16),
            pltpu.VMEM((own, part * pack), BF16),
            pltpu.SemaphoreType.DMA,
            pltpu.SemaphoreType.DMA((STEPS,)),
            pltpu.SemaphoreType.DMA((pack, STEPS)),
        ],
        compiler_params=SMALL,
        cost_estimate=cost(2 * rows * own * part * pack, 2 * part * pack * own),
    )(*to_hbm(hot), back)


def first_part(rows, pack, slots):
    return (lax.broadcasted_iota(jnp.int32, (rows, 1), 0) // slots) % pack == 0


def fold(parts, slots):
    rows = parts[0].shape[0]
    total = parts[0]
    for h in range(1, len(parts)):
        total = total + pltpu.roll(parts[h], rows - h * slots, 0)
    return total


def spread(value, pack, slots):
    return [value if h == 0 else pltpu.roll(value, h * slots, 0) for h in range(pack)]


class Arrivals:
    def __init__(self, blocks, plan):
        self.blocks, self.plan = blocks, plan

    def start(self, refs, places, sems):
        here = lax.axis_index("seq")
        for k, (a, b, t) in enumerate(self.plan):
            if a == b:
                pltpu.make_async_copy(refs[a], places[k], sems.at[k]).start()
            else:

                @pl.when(here >= t)
                def _():
                    pltpu.make_async_copy(refs[a], places[k], sems.at[k]).start()

                @pl.when(here < t)
                def _():
                    pltpu.make_async_copy(refs[b], places[k], sems.at[k]).start()

    def wait(self, refs, places, sems):
        for k, (a, _, _) in enumerate(self.plan):
            pltpu.make_async_copy(refs[a], places[k], sems.at[k]).wait()


def side_copies(gate_ref, up_ref, router_ref, side, sems, pack, j, width):
    part = side.shape[0]
    hidden_n = gate_ref.shape[2]
    rows = pl.ds(j * width, width)
    copies = []
    for h in range(pack):
        for n, ref in enumerate((gate_ref, up_ref)):
            columns = pl.ds((2 * h + n) * hidden_n, hidden_n)
            copies.append((ref.at[0, pl.ds(h * part + j * width, width), :], side.at[rows, columns]))
    copies.append((router_ref.at[rows, :], side.at[rows, pl.ds(2 * pack * hidden_n, LANES)]))
    return [pltpu.make_async_copy(a, b, sems.at[j, n]) for n, (a, b) in enumerate(copies)]


def down_copies(down_ref, stack, sems, pack):
    hidden_n = down_ref.shape[1]
    part = stack.shape[1]
    return [
        pltpu.make_async_copy(
            down_ref.at[0, :, pl.ds(h * part, part)], stack.at[pl.ds(h * hidden_n, hidden_n), :], sems.at[h]
        )
        for h in range(pack)
    ]


def put_blocks(out, target, columns):
    seq_n, rows, _ = target.shape
    here = lax.axis_index("seq")
    for k in range(seq_n):
        target[lax.rem(here - k + seq_n, seq_n), :, columns] = out[k * rows : (k + 1) * rows]


def expert_forward(arrivals, seq_n, slots, experts, pack, router_side, threshold, w_gate, w_up, w_down, hid_scale):
    block_rows, part = arrivals.blocks[0].shape
    rows = block_rows * seq_n
    hidden_n = w_gate.shape[2]
    both = 2 * hidden_n
    width = part // STEPS
    total = pack * both + LANES
    n_blocks = len(arrivals.blocks)

    def body(*refs):
        blocks = refs[:n_blocks]
        router_ref, gate_ref, up_ref, down_ref, threshold_ref, scale_ref = refs[n_blocks : n_blocks + 6]
        x_ref, out_ref, pre_ref, hidden_ref = refs[n_blocks + 6 : n_blocks + 10]
        pre_v, hidden_v, x_v, out_v, side, stack, x_sems, side_sems, stack_sems, out_sems = refs[n_blocks + 10 :]
        places = [x_v.at[pl.ds(k * block_rows, block_rows), :] for k in range(seq_n)]
        arrivals.start(blocks, places, x_sems)
        chunks = [side_copies(gate_ref, up_ref, router_ref, side, side_sems, pack, j, width) for j in range(STEPS)]
        downs = down_copies(down_ref, stack, stack_sems, pack)
        for copy in sum(chunks, []) + downs:
            copy.start()
        arrivals.wait(blocks, places, x_sems)
        leaving = [pltpu.make_async_copy(x_v, x_ref, out_sems.at[STEPS])]
        leaving[0].start()
        sums = [0.0] * (pack + 1)
        for j, chunk in enumerate(chunks):
            for copy in chunk:
                copy.wait()
            now = slice(j * width, (j + 1) * width)
            for n in range(pack + 1):
                sums[n] = sums[n] + mm(x_v[:, now], side[now, n * both : min((n + 1) * both, total)])
        gate = fold([y[:, :hidden_n] for y in sums[:pack]], slots)
        up = fold([y[:, hidden_n:] for y in sums[:pack]], slots)
        scores = sums[pack]
        lane = lax.broadcasted_iota(jnp.int32, scores.shape, 1)
        expert = lax.axis_index("exp")
        score = fold([jnp.where(lane == h * experts + expert, scores, 0.0) for h in range(pack)], slots)
        lane = lax.broadcasted_iota(jnp.int32, threshold_ref.shape, 1)
        cut = jnp.sum(jnp.where(lane == expert, threshold_ref[...], 0.0), axis=1, keepdims=True)
        g = jax.nn.sigmoid(jnp.sum(score, axis=1, keepdims=True) - cut)
        hidden = gate * jax.nn.sigmoid(gate) * up * scale_ref[...] * g
        hidden = jnp.where(first_part(rows, pack, slots), hidden, 0.0)
        for h, value in enumerate(spread(hidden, pack, slots)):
            now = slice(h * hidden_n, (h + 1) * hidden_n)
            hidden_v[:, now] = value.astype(BF16)
        pre_v[:, :hidden_n] = gate
        pre_v[:, hidden_n:both] = up
        pre_v[:, both:] = jnp.broadcast_to(g, (rows, LANES))
        leaving.append(pltpu.make_async_copy(pre_v, pre_ref, out_sems.at[STEPS + 1]))
        leaving.append(pltpu.make_async_copy(hidden_v, hidden_ref, out_sems.at[STEPS + 2]))
        for copy in leaving[1:]:
            copy.start()
        for copy in downs:
            copy.wait()
        for j in range(STEPS):
            now = slice(j * width, (j + 1) * width)
            put_blocks(mm(hidden_v[...], stack[:, now]).astype(BF16), out_v, now)
            columns = pl.ds(j * width, width)
            leaving.append(pltpu.make_async_copy(out_v.at[:, :, columns], out_ref.at[:, :, columns], out_sems.at[j]))
            leaving[-1].start()
        for copy in leaving:
            copy.wait()

    return pl.pallas_call(
        body,
        in_specs=[ANYWHERE] * (n_blocks + 4) + [IN_VMEM] * 2,
        out_specs=[ANYWHERE] * 4,
        out_shape=[
            shape((rows, part)),
            shape((seq_n, block_rows, part)),
            shape((rows, both + LANES), F32),
            shape((rows, pack * hidden_n)),
        ],
        scratch_shapes=[
            pltpu.VMEM((rows, both + LANES), F32),
            pltpu.VMEM((rows, pack * hidden_n), BF16),
            pltpu.VMEM((rows, part), BF16),
            pltpu.VMEM((seq_n, block_rows, part), BF16),
            pltpu.VMEM((part, total), BF16),
            pltpu.VMEM((pack * hidden_n, part), BF16),
            pltpu.SemaphoreType.DMA((seq_n,)),
            pltpu.SemaphoreType.DMA((STEPS, 2 * pack + 1)),
            pltpu.SemaphoreType.DMA((pack,)),
            pltpu.SemaphoreType.DMA((STEPS + 3,)),
        ],
        compiler_params=PARAMS,
        cost_estimate=cost(6 * rows * part * pack * hidden_n, 12 * part * pack * hidden_n),
    )(*to_hbm(*arrivals.blocks, router_side, w_gate, w_up, w_down), threshold.reshape(1, -1), hid_scale)


def split3(v):
    hi = v.astype(BF16)
    rest = v - hi.astype(F32)
    mid = rest.astype(BF16)
    return hi, mid, (rest - mid.astype(F32)).astype(BF16)


def riding(seq_n, group):
    return LANES * -(-2 * seq_n // group)


def expert_backward(arrivals, seq_n, exp_n, slots, pack, x, pre, router_side, w_gate, w_up, w_down, hid_scale):
    block_rows, part = arrivals.blocks[0].shape
    rows = block_rows * seq_n
    hidden_n = w_gate.shape[2]
    width = part // STEPS
    total = 2 * pack * hidden_n + LANES
    group = pack * slots
    extra = riding(seq_n, group)
    per = part * pack // (seq_n * exp_n)
    n_blocks = len(arrivals.blocks)

    def body(*refs):
        blocks = refs[:n_blocks]
        router_ref, gate_ref, up_ref, down_ref, x_ref, pre_ref, scale_ref = refs[n_blocks : n_blocks + 7]
        c_ref, out_ref, delta_ref = refs[n_blocks + 7 : n_blocks + 10]
        c_v, x_v, pre_v, out_v, side, stack, columns, c_sems, x_sems, side_sems, stack_sems, out_sems = refs[
            n_blocks + 10 :
        ]
        places = [c_v.at[pl.ds(k * block_rows, block_rows), :] for k in range(seq_n)]
        arrivals.start(blocks, places, c_sems)
        chunks = [side_copies(gate_ref, up_ref, router_ref, side, side_sems, pack, j, width) for j in range(STEPS)]
        downs = down_copies(down_ref, stack, stack_sems, pack)
        x_copy = pltpu.make_async_copy(x_ref, x_v, x_sems.at[0])
        pre_copy = pltpu.make_async_copy(pre_ref, pre_v, x_sems.at[1])
        for copy in downs + [pre_copy] + sum(chunks, []) + [x_copy]:
            copy.start()
        arrivals.wait(blocks, places, c_sems)
        leaving = [pltpu.make_async_copy(c_v, c_ref, out_sems.at[STEPS])]
        leaving[0].start()
        for copy in downs:
            copy.wait()
        both = mm(c_v[...], stack[...], LAST)
        parts = [both[:, h * hidden_n : (h + 1) * hidden_n] for h in range(pack)]
        pre_copy.wait()
        raw = jnp.where(first_part(rows, pack, slots), fold(parts, slots) * scale_ref[...], 0.0)
        gate = pre_v[:, :hidden_n]
        up = pre_v[:, hidden_n : 2 * hidden_n]
        g = pre_v[:, 2 * hidden_n : 2 * hidden_n + 1]
        sig = jax.nn.sigmoid(gate)
        act = gate * sig
        score = jnp.sum(act * up * raw, axis=1, keepdims=True) * g * (1.0 - g)
        grad = raw * g
        to_gate = spread(grad * up * sig * (1.0 + gate * (1.0 - sig)), pack, slots)
        to_up = spread(grad * act, pack, slots)
        expert = lax.axis_index("exp")
        lane = lax.broadcasted_iota(jnp.int32, (rows, LANES), 1)
        by_expert = jnp.zeros((rows, LANES), F32)
        by_split = jnp.zeros((rows, LANES), F32)
        for h, value in enumerate(spread(jnp.broadcast_to(score, (rows, LANES)), pack, slots)):
            delta_ref[:, 2 * h * hidden_n : (2 * h + 1) * hidden_n] = to_gate[h].astype(BF16)
            delta_ref[:, (2 * h + 1) * hidden_n : (2 * h + 2) * hidden_n] = to_up[h].astype(BF16)
            for n, piece in enumerate(split3(value)):
                piece = piece.astype(F32)
                by_split = jnp.where(lane == 3 * h + n, piece, by_split)
                if n < 2:
                    by_expert = jnp.where(lane == (n * pack + h) * exp_n + expert, piece, by_expert)
        columns[...] = by_split.astype(BF16)
        delta_ref[:, 2 * pack * hidden_n :] = by_expert.astype(BF16)
        for j, chunk in enumerate(chunks):
            for copy in chunk:
                copy.wait()
            now = slice(j * width, (j + 1) * width)
            put_blocks(mm(delta_ref[...], side[now, :], LAST).astype(BF16), out_v, now)
            if j + 1 < STEPS:
                now = pl.ds(j * width, width)
                leaving.append(pltpu.make_async_copy(out_v.at[:, :, now], out_ref.at[:, :, now], out_sems.at[j]))
                leaving[-1].start()

        here = lax.axis_index("seq")
        x_copy.wait()
        told = mm(columns[...], x_v[...], ROWS)
        sub = lax.broadcasted_iota(jnp.int32, (group, LANES), 0)
        lane = lax.broadcasted_iota(jnp.int32, (group, LANES), 1)
        minus = jnp.broadcast_to(-jnp.sum(score, axis=0, keepdims=True), (group, LANES))
        pieces = [piece.astype(F32) for piece in split3(minus)]
        threshold_row = jnp.zeros((group, LANES), F32)
        for n, piece in enumerate(pieces):
            threshold_row = jnp.where(lane == n, piece, threshold_row)
        for owner in range(seq_n * exp_n):
            h, first = divmod(owner * per, part)
            shift = first % LANES
            value = jnp.sum(told[3 * h : 3 * h + 3, first - shift : first - shift + LANES], axis=0, keepdims=True)
            value = jnp.broadcast_to(value, (group, LANES))
            if shift:
                value = pltpu.roll(value, LANES - shift, 1)
            if per < LANES:
                value = jnp.where(lane < per, value, 0.0)
            d, place = divmod(owner, exp_n)
            for t in range(extra // LANES):
                row = sub + t * group
                now = slice(part + t * LANES, part + (t + 1) * LANES)
                out_v[d, place * group : (place + 1) * group, now] = jnp.where(
                    row == 2 * here, value, jnp.where(row == 2 * here + 1, threshold_row, 0.0)
                ).astype(BF16)
        now = pl.ds((STEPS - 1) * width, width + extra)
        leaving.append(pltpu.make_async_copy(out_v.at[:, :, now], out_ref.at[:, :, now], out_sems.at[STEPS - 1]))
        leaving[-1].start()
        for copy in leaving:
            copy.wait()

    return pl.pallas_call(
        body,
        in_specs=[ANYWHERE] * (n_blocks + 6) + [IN_VMEM],
        out_specs=[ANYWHERE] * 2 + [IN_VMEM],
        out_shape=[
            shape((rows, part)),
            shape((seq_n, block_rows, part + extra)),
            shape((rows, total)),
        ],
        scratch_shapes=[
            pltpu.VMEM((rows, part), BF16),
            pltpu.VMEM((rows, part), BF16),
            pltpu.VMEM(pre.shape, F32),
            pltpu.VMEM((seq_n, block_rows, part + extra), BF16),
            pltpu.VMEM((part, total), BF16),
            pltpu.VMEM((pack * hidden_n, part), BF16),
            pltpu.VMEM((rows, LANES), BF16),
            pltpu.SemaphoreType.DMA((seq_n,)),
            pltpu.SemaphoreType.DMA((2,)),
            pltpu.SemaphoreType.DMA((STEPS, 2 * pack + 1)),
            pltpu.SemaphoreType.DMA((pack,)),
            pltpu.SemaphoreType.DMA((STEPS + 1,)),
        ],
        compiler_params=PARAMS,
        cost_estimate=cost(100 * rows * part * pack * hidden_n, 100 * part * pack * hidden_n),
    )(*to_hbm(*arrivals.blocks, router_side, w_gate, w_up, w_down, x, pre), hid_scale)


def side_grads(x, delta, pack, hidden_n):
    rows, part = x.shape
    width = part // STEPS

    def body(x_ref, delta_ref, gate_out, up_out):
        for h in range(pack):
            both = mm(x_ref[...], delta_ref[:, 2 * h * hidden_n : 2 * (h + 1) * hidden_n], ROWS)
            gate_out[h] = both[:, :hidden_n]
            up_out[h] = both[:, hidden_n:]

    tall = pl.BlockSpec((pack, width, hidden_n), lambda i: (0, i, 0))
    gate, up = pl.pallas_call(
        body,
        grid=(STEPS,),
        in_specs=[
            pl.BlockSpec((rows, width), lambda i: (0, i)),
            pl.BlockSpec(delta.shape, lambda i: (0, 0)),
        ],
        out_specs=[tall, tall],
        out_shape=[shape((pack, part, hidden_n), F32)] * 2,
        compiler_params=PARAMS,
        cost_estimate=cost(4 * rows * part * pack * hidden_n, 8 * part * pack * hidden_n),
    )(*to_hbm(x, delta))
    return gate.reshape(1, part * pack, hidden_n), up.reshape(1, part * pack, hidden_n)


def down_grads(c, hidden, pack, hidden_n):
    rows, part = c.shape
    width = part // 2

    def body(c_ref, hidden_ref, out):
        out[...] = mm(hidden_ref[...], c_ref[...], ROWS)

    return pl.pallas_call(
        body,
        grid=(pack, 2),
        in_specs=[
            pl.BlockSpec((rows, width), lambda h, i: (0, i)),
            pl.BlockSpec((rows, hidden_n), lambda h, i: (0, h)),
        ],
        out_specs=pl.BlockSpec((None, hidden_n, width), lambda h, i: (0, 0, h * 2 + i)),
        out_shape=shape((1, hidden_n, part * pack), F32),
        compiler_params=PARAMS,
        cost_estimate=cost(2 * rows * part * pack * hidden_n, 4 * part * pack * hidden_n),
    )(*to_hbm(c, hidden))


def up_line(block, n, first=0, last=None):
    last = n - 1 if last is None else last
    return lax.ppermute(block, "seq", [(s, s + 1) for s in range(first, last)])


def down_line(block, n, first=1, last=None):
    last = n if last is None else last
    return lax.ppermute(block, "seq", [(s, s - 1) for s in range(first, last)])


def line_gather(block, n):
    ups, downs = [], []
    up = down = block
    for j in range(1, n):
        up = up_line(up, n, j - 1)
        down = down_line(down, n, 1, n - j + 1)
        ups.append(up)
        downs.append(down)
    plan = [(0, 0, 0)] + [(k, 2 * n - 1 - k, k) for k in range(1, n)]
    return Arrivals([block] + ups + downs, plan)


def on_device(tokens, cotangent, router, threshold, w_gate, w_up, w_down, hid_scale, picks, counts):
    experts, slots = picks.shape[1:]
    features = tokens.shape[1]
    true_hidden = w_gate.shape[2]
    extra = -true_hidden % LANES
    if extra:
        w_gate, w_up = (jnp.pad(w, ((0, 0), (0, 0), (0, extra))) for w in (w_gate, w_up))
        w_down = jnp.pad(w_down, ((0, 0), (0, extra), (0, 0)))
        hid_scale = jnp.pad(hid_scale, ((0, 0), (0, extra)))
    hidden_n = true_hidden + extra
    seq_n = lax.axis_size("seq")
    exp_n = lax.axis_size("exp")
    everyone = seq_n * exp_n
    pack = max(1, 8 // slots)
    chosen = picks[0].T

    def to_owners(parts):
        parts = parts.reshape(everyone, -1, parts.shape[2])
        return lax.all_to_all(parts, BOTH, split_axis=0, concat_axis=0, tiled=True).reshape(-1, parts.shape[2])

    sent, hot = choose_rows(tokens, cotangent, chosen, counts, pack)
    sent = sent.reshape(experts, 2, -1, sent.shape[1])
    here = lax.all_to_all(sent, "exp", split_axis=0, concat_axis=0, tiled=True)
    x_in, c_in = (line_gather(here[:, n].reshape(-1, here.shape[3]), seq_n) for n in range(2))
    halves = list(router.reshape(pack, features // pack, experts))
    router_side = jnp.concatenate(halves + halves, axis=1)
    router_side = jnp.pad(router_side, ((0, 0), (0, LANES - router_side.shape[1])))

    x, out, pre, hidden = expert_forward(
        x_in, seq_n, slots, experts, pack, router_side, threshold, w_gate, w_up, w_down, hid_scale
    )
    out = to_owners(out)
    c, back, delta = expert_backward(
        c_in, seq_n, exp_n, slots, pack, x, pre, router_side, w_gate, w_up, w_down, hid_scale
    )
    back, out = lax.optimization_barrier((back, out))
    back = to_owners(back)
    down_grad = down_grads(c, hidden, pack, hidden_n)
    gate_grad, up_grad = side_grads(x, delta, pack, hidden_n)
    (mixture,) = scatter_rows(out, hot, seq_n)
    token_grad, router_grad, threshold_grad = scatter_rows(back, hot, seq_n, (features // everyone, experts))
    if extra:
        gate_grad, up_grad = gate_grad[:, :, :true_hidden], up_grad[:, :, :true_hidden]
        down_grad = down_grad[:, :true_hidden]
    return mixture, token_grad, router_grad.T, threshold_grad[0], gate_grad, up_grad, down_grad


def solution(mesh):
    by_owner = P(BOTH, None)
    columns = P("exp", None, "seq")
    down = P("exp", "seq", None)
    return jax.shard_map(
        on_device,
        mesh=mesh,
        in_specs=(
            by_owner,
            by_owner,
            P(),
            P(),
            columns,
            columns,
            down,
            P("exp", "seq"),
            P(BOTH, None, None),
            by_owner,
        ),
        out_specs=(by_owner, by_owner, by_owner, P(), columns, columns, down),
        check_vma=False,
    )
```

```python
import jax
import jax.numpy as jnp
from jax import lax
from jax.experimental import pallas as pl
from jax.experimental.pallas import tpu as pltpu
from jax.sharding import PartitionSpec as P

BOTH = ("seq", "exp")
F32 = jnp.float32
BF16 = jnp.bfloat16
ROWS = ((0,), (0,))
LAST = ((1,), (1,))
STEPS = 4
LANES = 128


def mm(a, b, dims=((1,), (0,))):
    return lax.dot_general(a, b, (dims, ((), ())), preferred_element_type=F32)


PARAMS = pltpu.CompilerParams(vmem_limit_bytes=56 * 2**20)
SMALL = pltpu.CompilerParams(vmem_limit_bytes=12 * 2**20)


def to_hbm(*arrays):
    return [pltpu.with_memory_space_constraint(x, pltpu.HBM) for x in arrays]


def cost(flops, moved):
    return pl.CostEstimate(flops=flops, bytes_accessed=moved, transcendentals=0)


def shape(dims, dtype=BF16):
    return jax.ShapeDtypeStruct(dims, dtype)


ANYWHERE = pl.BlockSpec(memory_space=pl.ANY)
IN_VMEM = pl.BlockSpec(memory_space=pltpu.VMEM)


def choose_rows(tokens, cotangent, picks, counts, pack):
    own, features = tokens.shape
    slots, experts = picks.shape
    group = pack * slots
    count = 2 * experts * group
    part = features // pack
    width = part // STEPS

    def body(picks_ref, counts_ref, c_ref, x_ref, out_ref, hot_ref, picks_s, counts_s, c_v, x_v, out_v, sems, out_sems):
        small = [
            pltpu.make_async_copy(picks_ref, picks_s, sems.at[STEPS, 0]),
            pltpu.make_async_copy(counts_ref, counts_s, sems.at[STEPS, 1]),
        ]
        for copy in small:
            copy.start()
        large = []
        for j in range(STEPS):
            for h in range(pack):
                now = pl.ds(h * part + j * width, width)
                for n, (ref, held) in enumerate(((x_ref, x_v), (c_ref, c_v))):
                    large.append(pltpu.make_async_copy(ref.at[:, now], held.at[:, now], sems.at[j, 2 * h + n]))
        for copy in large:
            copy.start()
        for copy in small:
            copy.wait()
        dims = (count, own)
        row = lax.broadcasted_iota(jnp.int32, dims, 0)
        token = lax.broadcasted_iota(jnp.int32, dims, 1)
        second = (row // group) % 2
        place = (row // (2 * group) * slots + row % slots) * 2 + second
        want = jnp.full(dims, -1, jnp.int32)
        for e in range(experts):
            for k in range(slots):
                index = (e * slots + k) * 2
                want = jnp.where(place == index, picks_s[k, e], want)
                live = jnp.where(k < counts_s[0, e], picks_s[k, e], -1)
                want = jnp.where(place == index + 1, live, want)
        found = (want == token) & (second == 0)
        found_live = (want == token) & (second == 1)
        part_of = (row // slots) % pack
        chosen = [jnp.where(found & (part_of == h), 1.0, 0.0).astype(BF16) for h in range(pack)]
        live = [jnp.where(found_live & (part_of == h), 1.0, 0.0) for h in range(pack)]
        for h in range(pack):
            hot_ref[h] = jnp.concatenate(
                [live[h][(2 * e + 1) * group : (2 * e + 2) * group] for e in range(experts)]
            ).astype(BF16)
        live = [value.astype(BF16) for value in live]
        leaving = []
        for j in range(STEPS):
            for copy in large[2 * pack * j : 2 * pack * (j + 1)]:
                copy.wait()
            total = 0.0
            for h in range(pack):
                now = slice(h * part + j * width, h * part + (j + 1) * width)
                total = total + mm(chosen[h], x_v[:, now]) + mm(live[h], c_v[:, now])
            out_v[:, j * width : (j + 1) * width] = total.astype(BF16)
            now = pl.ds(j * width, width)
            leaving.append(pltpu.make_async_copy(out_v.at[:, now], out_ref.at[:, now], out_sems.at[j]))
            leaving[-1].start()
        for copy in leaving:
            copy.wait()

    return pl.pallas_call(
        body,
        in_specs=[ANYWHERE] * 4,
        out_specs=[ANYWHERE, IN_VMEM],
        out_shape=[shape((count, part)), shape((pack, count // 2, own))],
        scratch_shapes=[
            pltpu.SMEM(picks.shape, jnp.int32),
            pltpu.SMEM(counts.shape, jnp.int32),
            pltpu.VMEM(tokens.shape, BF16),
            pltpu.VMEM(tokens.shape, BF16),
            pltpu.VMEM((count, part), BF16),
            pltpu.SemaphoreType.DMA((STEPS + 1, 2 * pack)),
            pltpu.SemaphoreType.DMA((STEPS,)),
        ],
        compiler_params=PARAMS,
        cost_estimate=cost(4 * count * own * features, 4 * features * own),
    )(*to_hbm(picks, counts, cotangent, tokens))


def scatter_rows(back, hot, seq_n, message=None):
    pack, count, own = hot.shape
    rows = back.shape[0]
    extra = 0 if message is None else riding(seq_n, count // message[1])
    part = back.shape[1] - extra
    width = part // STEPS

    def body(hot_ref, back_ref, *refs):
        hot_v, back_v, out_v, hot_sem, in_sems, out_sems = refs[-6:]
        out_ref = refs[0]
        hot_copy = pltpu.make_async_copy(hot_ref, hot_v, hot_sem)
        hot_copy.start()
        arriving = []
        for i in range(STEPS):
            now = pl.ds(i * width, width + (extra if i + 1 == STEPS else 0))
            arriving.append(pltpu.make_async_copy(back_ref.at[:, now], back_v.at[:, now], in_sems.at[i]))
            arriving[-1].start()
        hot_copy.wait()
        choosers = [jnp.concatenate([hot_v[h]] * seq_n, axis=0) for h in range(pack)]
        leaving = []
        for i in range(STEPS):
            arriving[i].wait()
            for h in range(pack):
                first = h * part + i * width
                rows_now = back_v[:, i * width : (i + 1) * width]
                out_v[:, first : first + width] = mm(choosers[h], rows_now, ROWS).astype(BF16)
                now = pl.ds(first, width)
                leaving.append(pltpu.make_async_copy(out_v.at[:, now], out_ref.at[:, now], out_sems.at[h, i]))
                leaving[-1].start()
        if message is not None:
            router_ref, total_ref = refs[1], refs[2]
            experts, per = router_ref.shape
            group = count // experts
            row = lax.broadcasted_iota(jnp.int32, (rows, experts), 0)
            expert = lax.broadcasted_iota(jnp.int32, (rows, experts), 1)
            mine = row % count // group == expert
            even = jnp.where(mine & (row % 2 == 0), 1.0, 0.0).astype(BF16)
            odd = jnp.where(mine & (row % 2 == 1), 1.0, 0.0).astype(BF16)
            rides = [back_v[:, part + t * LANES : part + (t + 1) * LANES] for t in range(extra // LANES)]
            router = sum(mm(even, ride, ROWS) for ride in rides)
            total = sum(mm(ride, odd, ROWS) for ride in rides)
            router_ref[...] = router[:, :per]
            total_ref[...] = jnp.sum(total[:3], axis=0, keepdims=True)
        for copy in leaving:
            copy.wait()

    out_specs = [ANYWHERE]
    out_shape = [shape((own, part * pack))]
    if message is not None:
        per, experts = message
        out_specs += [IN_VMEM] * 2
        out_shape += [shape((experts, per), F32), shape((1, experts), F32)]
    return pl.pallas_call(
        body,
        in_specs=[ANYWHERE] * 2,
        out_specs=out_specs,
        out_shape=out_shape,
        scratch_shapes=[
            pltpu.VMEM(hot.shape, BF16),
            pltpu.VMEM(back.shape, BF16),
            pltpu.VMEM((own, part * pack), BF16),
            pltpu.SemaphoreType.DMA,
            pltpu.SemaphoreType.DMA((STEPS,)),
            pltpu.SemaphoreType.DMA((pack, STEPS)),
        ],
        compiler_params=SMALL,
        cost_estimate=cost(2 * rows * own * part * pack, 2 * part * pack * own),
    )(*to_hbm(hot), back)


def first_part(rows, pack, slots):
    return (lax.broadcasted_iota(jnp.int32, (rows, 1), 0) // slots) % pack == 0


def fold(parts, slots):
    rows = parts[0].shape[0]
    total = parts[0]
    for h in range(1, len(parts)):
        total = total + pltpu.roll(parts[h], rows - h * slots, 0)
    return total


def spread(value, pack, slots):
    return [value if h == 0 else pltpu.roll(value, h * slots, 0) for h in range(pack)]


class Arrivals:
    def __init__(self, blocks, plan):
        self.blocks, self.plan = blocks, plan

    def near(self, step):
        return self.blocks[step], self.blocks[len(self.blocks) // 2 + step]

    def start(self, refs, places, sems):
        here = lax.axis_index("seq")
        for k, (a, b, t) in enumerate(self.plan):
            if a == b:
                pltpu.make_async_copy(refs[a], places[k], sems.at[k]).start()
            else:

                @pl.when(here >= t)
                def _():
                    pltpu.make_async_copy(refs[a], places[k], sems.at[k]).start()

                @pl.when(here < t)
                def _():
                    pltpu.make_async_copy(refs[b], places[k], sems.at[k]).start()

    def wait(self, refs, places, sems):
        for k, (a, _, _) in enumerate(self.plan):
            pltpu.make_async_copy(refs[a], places[k], sems.at[k]).wait()


def side_copies(gate_ref, up_ref, router_ref, side, sems, pack, j, width):
    part = side.shape[0]
    hidden_n = gate_ref.shape[2]
    rows = pl.ds(j * width, width)
    copies = []
    for h in range(pack):
        for n, ref in enumerate((gate_ref, up_ref)):
            columns = pl.ds((2 * h + n) * hidden_n, hidden_n)
            copies.append((ref.at[0, pl.ds(h * part + j * width, width), :], side.at[rows, columns]))
    copies.append((router_ref.at[rows, :], side.at[rows, pl.ds(2 * pack * hidden_n, LANES)]))
    return [pltpu.make_async_copy(a, b, sems.at[j, n]) for n, (a, b) in enumerate(copies)]


def down_copies(down_ref, stack, sems, pack):
    hidden_n = down_ref.shape[1]
    part = stack.shape[1]
    return [
        pltpu.make_async_copy(
            down_ref.at[0, :, pl.ds(h * part, part)], stack.at[pl.ds(h * hidden_n, hidden_n), :], sems.at[h]
        )
        for h in range(pack)
    ]


def put_blocks(out, target, columns):
    seq_n, rows, _ = target.shape
    here = lax.axis_index("seq")
    for k in range(seq_n):
        target[lax.rem(here - k + seq_n, seq_n), :, columns] = out[k * rows : (k + 1) * rows]


def expert_forward(arrivals, seq_n, slots, experts, pack, router_side, threshold, w_gate, w_up, w_down, hid_scale):
    block_rows, part = arrivals.blocks[0].shape
    rows = block_rows * seq_n
    hidden_n = w_gate.shape[2]
    both = 2 * hidden_n
    width = part // STEPS
    total = pack * both + LANES
    n_blocks = len(arrivals.blocks)

    def body(*refs):
        blocks = refs[:n_blocks]
        router_ref, gate_ref, up_ref, down_ref, threshold_ref, scale_ref = refs[n_blocks : n_blocks + 6]
        x_ref, out_ref, pre_ref, hidden_ref = refs[n_blocks + 6 : n_blocks + 10]
        pre_v, hidden_v, x_v, out_v, side, stack, x_sems, side_sems, stack_sems, out_sems = refs[n_blocks + 10 :]
        places = [x_v.at[pl.ds(k * block_rows, block_rows), :] for k in range(seq_n)]
        arrivals.start(blocks, places, x_sems)
        chunks = [side_copies(gate_ref, up_ref, router_ref, side, side_sems, pack, j, width) for j in range(STEPS)]
        downs = down_copies(down_ref, stack, stack_sems, pack)
        for copy in sum(chunks, []) + downs:
            copy.start()
        arrivals.wait(blocks, places, x_sems)
        leaving = [pltpu.make_async_copy(x_v, x_ref, out_sems.at[STEPS])]
        leaving[0].start()
        sums = [0.0] * (pack + 1)
        for j, chunk in enumerate(chunks):
            for copy in chunk:
                copy.wait()
            now = slice(j * width, (j + 1) * width)
            for n in range(pack + 1):
                sums[n] = sums[n] + mm(x_v[:, now], side[now, n * both : min((n + 1) * both, total)])
        gate = fold([y[:, :hidden_n] for y in sums[:pack]], slots)
        up = fold([y[:, hidden_n:] for y in sums[:pack]], slots)
        scores = sums[pack]
        lane = lax.broadcasted_iota(jnp.int32, scores.shape, 1)
        expert = lax.axis_index("exp")
        score = fold([jnp.where(lane == h * experts + expert, scores, 0.0) for h in range(pack)], slots)
        lane = lax.broadcasted_iota(jnp.int32, threshold_ref.shape, 1)
        cut = jnp.sum(jnp.where(lane == expert, threshold_ref[...], 0.0), axis=1, keepdims=True)
        g = jax.nn.sigmoid(jnp.sum(score, axis=1, keepdims=True) - cut)
        hidden = gate * jax.nn.sigmoid(gate) * up * scale_ref[...] * g
        hidden = jnp.where(first_part(rows, pack, slots), hidden, 0.0)
        for h, value in enumerate(spread(hidden, pack, slots)):
            now = slice(h * hidden_n, (h + 1) * hidden_n)
            hidden_v[:, now] = value.astype(BF16)
        pre_v[:, :hidden_n] = gate
        pre_v[:, hidden_n:both] = up
        pre_v[:, both:] = jnp.broadcast_to(g, (rows, LANES))
        leaving.append(pltpu.make_async_copy(pre_v, pre_ref, out_sems.at[STEPS + 1]))
        leaving.append(pltpu.make_async_copy(hidden_v, hidden_ref, out_sems.at[STEPS + 2]))
        for copy in leaving[1:]:
            copy.start()
        for copy in downs:
            copy.wait()
        for j in range(STEPS):
            now = slice(j * width, (j + 1) * width)
            put_blocks(mm(hidden_v[...], stack[:, now]).astype(BF16), out_v, now)
            columns = pl.ds(j * width, width)
            leaving.append(pltpu.make_async_copy(out_v.at[:, :, columns], out_ref.at[:, :, columns], out_sems.at[j]))
            leaving[-1].start()
        for copy in leaving:
            copy.wait()

    return pl.pallas_call(
        body,
        in_specs=[ANYWHERE] * (n_blocks + 4) + [IN_VMEM] * 2,
        out_specs=[ANYWHERE] * 4,
        out_shape=[
            shape((rows, part)),
            shape((seq_n, block_rows, part)),
            shape((rows, both + LANES), F32),
            shape((rows, pack * hidden_n)),
        ],
        scratch_shapes=[
            pltpu.VMEM((rows, both + LANES), F32),
            pltpu.VMEM((rows, pack * hidden_n), BF16),
            pltpu.VMEM((rows, part), BF16),
            pltpu.VMEM((seq_n, block_rows, part), BF16),
            pltpu.VMEM((part, total), BF16),
            pltpu.VMEM((pack * hidden_n, part), BF16),
            pltpu.SemaphoreType.DMA((seq_n,)),
            pltpu.SemaphoreType.DMA((STEPS, 2 * pack + 1)),
            pltpu.SemaphoreType.DMA((pack,)),
            pltpu.SemaphoreType.DMA((STEPS + 3,)),
        ],
        compiler_params=PARAMS,
        cost_estimate=cost(6 * rows * part * pack * hidden_n, 12 * part * pack * hidden_n),
    )(*to_hbm(*arrivals.blocks, router_side, w_gate, w_up, w_down), threshold.reshape(1, -1), hid_scale)


def split3(v):
    hi = v.astype(BF16)
    rest = v - hi.astype(F32)
    mid = rest.astype(BF16)
    return hi, mid, (rest - mid.astype(F32)).astype(BF16)


def riding(seq_n, group):
    return LANES * -(-2 * seq_n // group)


def expert_backward(arrivals, seq_n, exp_n, slots, pack, x, pre, router_side, w_gate, w_up, w_down, hid_scale):
    block_rows, part = arrivals.blocks[0].shape
    rows = block_rows * seq_n
    hidden_n = w_gate.shape[2]
    width = part // STEPS
    total = 2 * pack * hidden_n + LANES
    group = pack * slots
    extra = riding(seq_n, group)
    per = part * pack // (seq_n * exp_n)
    n_blocks = len(arrivals.blocks)

    def body(*refs):
        blocks = refs[:n_blocks]
        router_ref, gate_ref, up_ref, down_ref, x_ref, pre_ref, scale_ref = refs[n_blocks : n_blocks + 7]
        c_ref, out_ref, delta_ref = refs[n_blocks + 7 : n_blocks + 10]
        c_v, x_v, pre_v, out_v, side, stack, columns, c_sems, x_sems, side_sems, stack_sems, out_sems = refs[
            n_blocks + 10 :
        ]
        places = [c_v.at[pl.ds(k * block_rows, block_rows), :] for k in range(seq_n)]
        arrivals.start(blocks, places, c_sems)
        chunks = [side_copies(gate_ref, up_ref, router_ref, side, side_sems, pack, j, width) for j in range(STEPS)]
        downs = down_copies(down_ref, stack, stack_sems, pack)
        x_copy = pltpu.make_async_copy(x_ref, x_v, x_sems.at[0])
        pre_copy = pltpu.make_async_copy(pre_ref, pre_v, x_sems.at[1])
        for copy in downs + [pre_copy] + sum(chunks, []) + [x_copy]:
            copy.start()
        arrivals.wait(blocks, places, c_sems)
        leaving = [pltpu.make_async_copy(c_v, c_ref, out_sems.at[STEPS])]
        leaving[0].start()
        for copy in downs:
            copy.wait()
        both = mm(c_v[...], stack[...], LAST)
        parts = [both[:, h * hidden_n : (h + 1) * hidden_n] for h in range(pack)]
        pre_copy.wait()
        raw = jnp.where(first_part(rows, pack, slots), fold(parts, slots) * scale_ref[...], 0.0)
        gate = pre_v[:, :hidden_n]
        up = pre_v[:, hidden_n : 2 * hidden_n]
        g = pre_v[:, 2 * hidden_n : 2 * hidden_n + 1]
        sig = jax.nn.sigmoid(gate)
        act = gate * sig
        score = jnp.sum(act * up * raw, axis=1, keepdims=True) * g * (1.0 - g)
        grad = raw * g
        to_gate = spread(grad * up * sig * (1.0 + gate * (1.0 - sig)), pack, slots)
        to_up = spread(grad * act, pack, slots)
        expert = lax.axis_index("exp")
        lane = lax.broadcasted_iota(jnp.int32, (rows, LANES), 1)
        by_expert = jnp.zeros((rows, LANES), F32)
        by_split = jnp.zeros((rows, LANES), F32)
        for h, value in enumerate(spread(jnp.broadcast_to(score, (rows, LANES)), pack, slots)):
            delta_ref[:, 2 * h * hidden_n : (2 * h + 1) * hidden_n] = to_gate[h].astype(BF16)
            delta_ref[:, (2 * h + 1) * hidden_n : (2 * h + 2) * hidden_n] = to_up[h].astype(BF16)
            for n, piece in enumerate(split3(value)):
                piece = piece.astype(F32)
                by_split = jnp.where(lane == 3 * h + n, piece, by_split)
                if n < 2:
                    by_expert = jnp.where(lane == (n * pack + h) * exp_n + expert, piece, by_expert)
        columns[...] = by_split.astype(BF16)
        delta_ref[:, 2 * pack * hidden_n :] = by_expert.astype(BF16)
        for j, chunk in enumerate(chunks):
            for copy in chunk:
                copy.wait()
            now = slice(j * width, (j + 1) * width)
            put_blocks(mm(delta_ref[...], side[now, :], LAST).astype(BF16), out_v, now)
            if j + 1 < STEPS:
                now = pl.ds(j * width, width)
                leaving.append(pltpu.make_async_copy(out_v.at[:, :, now], out_ref.at[:, :, now], out_sems.at[j]))
                leaving[-1].start()

        here = lax.axis_index("seq")
        x_copy.wait()
        told = mm(columns[...], x_v[...], ROWS)
        sub = lax.broadcasted_iota(jnp.int32, (group, LANES), 0)
        lane = lax.broadcasted_iota(jnp.int32, (group, LANES), 1)
        minus = jnp.broadcast_to(-jnp.sum(score, axis=0, keepdims=True), (group, LANES))
        pieces = [piece.astype(F32) for piece in split3(minus)]
        threshold_row = jnp.zeros((group, LANES), F32)
        for n, piece in enumerate(pieces):
            threshold_row = jnp.where(lane == n, piece, threshold_row)
        for owner in range(seq_n * exp_n):
            h, first = divmod(owner * per, part)
            shift = first % LANES
            value = jnp.sum(told[3 * h : 3 * h + 3, first - shift : first - shift + LANES], axis=0, keepdims=True)
            value = jnp.broadcast_to(value, (group, LANES))
            if shift:
                value = pltpu.roll(value, LANES - shift, 1)
            if per < LANES:
                value = jnp.where(lane < per, value, 0.0)
            d, place = divmod(owner, exp_n)
            for t in range(extra // LANES):
                row = sub + t * group
                now = slice(part + t * LANES, part + (t + 1) * LANES)
                out_v[d, place * group : (place + 1) * group, now] = jnp.where(
                    row == 2 * here, value, jnp.where(row == 2 * here + 1, threshold_row, 0.0)
                ).astype(BF16)
        now = pl.ds((STEPS - 1) * width, width + extra)
        leaving.append(pltpu.make_async_copy(out_v.at[:, :, now], out_ref.at[:, :, now], out_sems.at[STEPS - 1]))
        leaving[-1].start()
        for copy in leaving:
            copy.wait()

    return pl.pallas_call(
        body,
        in_specs=[ANYWHERE] * (n_blocks + 6) + [IN_VMEM],
        out_specs=[ANYWHERE] * 2 + [IN_VMEM],
        out_shape=[
            shape((rows, part)),
            shape((seq_n, block_rows, part + extra)),
            shape((rows, total)),
        ],
        scratch_shapes=[
            pltpu.VMEM((rows, part), BF16),
            pltpu.VMEM((rows, part), BF16),
            pltpu.VMEM(pre.shape, F32),
            pltpu.VMEM((seq_n, block_rows, part + extra), BF16),
            pltpu.VMEM((part, total), BF16),
            pltpu.VMEM((pack * hidden_n, part), BF16),
            pltpu.VMEM((rows, LANES), BF16),
            pltpu.SemaphoreType.DMA((seq_n,)),
            pltpu.SemaphoreType.DMA((2,)),
            pltpu.SemaphoreType.DMA((STEPS, 2 * pack + 1)),
            pltpu.SemaphoreType.DMA((pack,)),
            pltpu.SemaphoreType.DMA((STEPS + 1,)),
        ],
        compiler_params=PARAMS,
        cost_estimate=cost(100 * rows * part * pack * hidden_n, 100 * part * pack * hidden_n),
    )(*to_hbm(*arrivals.blocks, router_side, w_gate, w_up, w_down, x, pre), hid_scale)


def side_grads(x, delta, pack, hidden_n):
    rows, part = x.shape
    width = part // STEPS

    def body(x_ref, delta_ref, gate_out, up_out):
        for h in range(pack):
            both = mm(x_ref[...], delta_ref[:, 2 * h * hidden_n : 2 * (h + 1) * hidden_n], ROWS)
            gate_out[h] = both[:, :hidden_n]
            up_out[h] = both[:, hidden_n:]

    tall = pl.BlockSpec((pack, width, hidden_n), lambda i: (0, i, 0))
    gate, up = pl.pallas_call(
        body,
        grid=(STEPS,),
        in_specs=[
            pl.BlockSpec((rows, width), lambda i: (0, i)),
            pl.BlockSpec(delta.shape, lambda i: (0, 0)),
        ],
        out_specs=[tall, tall],
        out_shape=[shape((pack, part, hidden_n), F32)] * 2,
        compiler_params=PARAMS,
        cost_estimate=cost(4 * rows * part * pack * hidden_n, 8 * part * pack * hidden_n),
    )(*to_hbm(x, delta))
    return gate.reshape(1, part * pack, hidden_n), up.reshape(1, part * pack, hidden_n)


def down_grads(c, hidden, pack, hidden_n):
    rows, part = c.shape
    width = part // 2

    def body(c_ref, hidden_ref, out):
        out[...] = mm(hidden_ref[...], c_ref[...], ROWS)

    return pl.pallas_call(
        body,
        grid=(pack, 2),
        in_specs=[
            pl.BlockSpec((rows, width), lambda h, i: (0, i)),
            pl.BlockSpec((rows, hidden_n), lambda h, i: (0, h)),
        ],
        out_specs=pl.BlockSpec((None, hidden_n, width), lambda h, i: (0, 0, h * 2 + i)),
        out_shape=shape((1, hidden_n, part * pack), F32),
        compiler_params=PARAMS,
        cost_estimate=cost(2 * rows * part * pack * hidden_n, 4 * part * pack * hidden_n),
    )(*to_hbm(c, hidden))


def up_line(block, n, first=0, last=None):
    last = n - 1 if last is None else last
    return lax.ppermute(block, "seq", [(s, s + 1) for s in range(first, last)])


def down_line(block, n, first=1, last=None):
    last = n if last is None else last
    return lax.ppermute(block, "seq", [(s, s - 1) for s in range(first, last)])


def line_gather(block, n, pause=None):
    ups, downs = [], []
    plan = [(0, 0, 0)] + [(k, 2 * n - 1 - k, k) for k in range(1, n)]

    def go(up, down, first, last):
        for j in range(first, last):
            up = up_line(up, n, j - 1)
            down = down_line(down, n, 1, n - j + 1)
            ups.append(up)
            downs.append(down)
        return Arrivals([block] + ups + downs, plan)

    if pause is None:
        return go(block, block, 1, n)

    def finish(value):
        return go(behind(ups[-1], value), behind(downs[-1], value), pause + 1, n)

    return go(block, block, 1, pause + 1), finish


def behind(value, *others):
    return lax.optimization_barrier((value, *others))[0]


def on_device(tokens, cotangent, router, threshold, w_gate, w_up, w_down, hid_scale, picks, counts):
    experts, slots = picks.shape[1:]
    features = tokens.shape[1]
    true_hidden = w_gate.shape[2]
    extra = -true_hidden % LANES
    if extra:
        w_gate, w_up = (jnp.pad(w, ((0, 0), (0, 0), (0, extra))) for w in (w_gate, w_up))
        w_down = jnp.pad(w_down, ((0, 0), (0, extra), (0, 0)))
        hid_scale = jnp.pad(hid_scale, ((0, 0), (0, extra)))
    hidden_n = true_hidden + extra
    seq_n = lax.axis_size("seq")
    exp_n = lax.axis_size("exp")
    everyone = seq_n * exp_n
    pack = max(1, 8 // slots)
    chosen = picks[0].T

    def to_owners(parts):
        parts = parts.reshape(everyone, -1, parts.shape[2])
        return lax.all_to_all(parts, BOTH, split_axis=0, concat_axis=0, tiled=True).reshape(-1, parts.shape[2])

    sent, hot = choose_rows(tokens, cotangent, chosen, counts, pack)
    sent = sent.reshape(experts, 2, -1, sent.shape[1])
    here = lax.all_to_all(sent, "exp", split_axis=0, concat_axis=0, tiled=True)
    x_rows, c_rows = (here[:, n].reshape(-1, here.shape[3]) for n in range(2))
    x_in = line_gather(x_rows, seq_n)
    c_rows = behind(c_rows, *(x_in.near(min(2, seq_n - 1))))
    c_in, finish = line_gather(c_rows, seq_n, seq_n - 2)
    halves = list(router.reshape(pack, features // pack, experts))
    router_side = jnp.concatenate(halves + halves, axis=1)
    router_side = jnp.pad(router_side, ((0, 0), (0, LANES - router_side.shape[1])))

    x_in.blocks[0] = behind(x_in.blocks[0], *c_in.near(1))
    x, out, pre, hidden = expert_forward(
        x_in, seq_n, slots, experts, pack, router_side, threshold, w_gate, w_up, w_down, hid_scale
    )
    c_in = finish(pre)
    out = to_owners(out)
    c, back, delta = expert_backward(
        c_in, seq_n, exp_n, slots, pack, x, pre, router_side, w_gate, w_up, w_down, hid_scale
    )
    back, out = lax.optimization_barrier((back, out))
    back = to_owners(back)
    down_grad = down_grads(c, hidden, pack, hidden_n)
    gate_grad, up_grad = side_grads(x, delta, pack, hidden_n)
    (mixture,) = scatter_rows(out, hot, seq_n)
    token_grad, router_grad, threshold_grad = scatter_rows(back, hot, seq_n, (features // everyone, experts))
    if extra:
        gate_grad, up_grad = gate_grad[:, :, :true_hidden], up_grad[:, :, :true_hidden]
        down_grad = down_grad[:, :true_hidden]
    return mixture, token_grad, router_grad.T, threshold_grad[0], gate_grad, up_grad, down_grad


def solution(mesh):
    by_owner = P(BOTH, None)
    columns = P("exp", None, "seq")
    down = P("exp", "seq", None)
    return jax.shard_map(
        on_device,
        mesh=mesh,
        in_specs=(
            by_owner,
            by_owner,
            P(),
            P(),
            columns,
            columns,
            down,
            P("exp", "seq"),
            P(BOTH, None, None),
            by_owner,
        ),
        out_specs=(by_owner, by_owner, by_owner, P(), columns, columns, down),
        check_vma=False,
    )
```

```python
import jax
import jax.numpy as jnp
from jax import lax
from jax.experimental import pallas as pl
from jax.experimental.pallas import tpu as pltpu
from jax.sharding import PartitionSpec as P

BOTH = ("seq", "exp")
F32 = jnp.float32
BF16 = jnp.bfloat16
ROWS = ((0,), (0,))
LAST = ((1,), (1,))
STEPS = 4
LANES = 128


def mm(a, b, dims=((1,), (0,))):
    return lax.dot_general(a, b, (dims, ((), ())), preferred_element_type=F32)


PARAMS = pltpu.CompilerParams(vmem_limit_bytes=56 * 2**20)
SMALL = pltpu.CompilerParams(vmem_limit_bytes=12 * 2**20)


def to_hbm(*arrays):
    return [pltpu.with_memory_space_constraint(x, pltpu.HBM) for x in arrays]


def cost(flops, moved):
    return pl.CostEstimate(flops=flops, bytes_accessed=moved, transcendentals=0)


def shape(dims, dtype=BF16):
    return jax.ShapeDtypeStruct(dims, dtype)


ANYWHERE = pl.BlockSpec(memory_space=pl.ANY)
IN_VMEM = pl.BlockSpec(memory_space=pltpu.VMEM)


def choose_rows(tokens, cotangent, picks, counts, pack):
    own, features = tokens.shape
    slots, experts = picks.shape
    group = pack * slots
    count = 2 * experts * group
    part = features // pack
    width = part // STEPS

    def body(picks_ref, counts_ref, c_ref, x_ref, out_ref, hot_ref, picks_s, counts_s, c_v, x_v, out_v, sems, out_sems):
        small = [
            pltpu.make_async_copy(picks_ref, picks_s, sems.at[STEPS, 0]),
            pltpu.make_async_copy(counts_ref, counts_s, sems.at[STEPS, 1]),
        ]
        for copy in small:
            copy.start()
        large = []
        for j in range(STEPS):
            for h in range(pack):
                now = pl.ds(h * part + j * width, width)
                for n, (ref, held) in enumerate(((x_ref, x_v), (c_ref, c_v))):
                    large.append(pltpu.make_async_copy(ref.at[:, now], held.at[:, now], sems.at[j, 2 * h + n]))
        for copy in large:
            copy.start()
        for copy in small:
            copy.wait()
        dims = (count, own)
        row = lax.broadcasted_iota(jnp.int32, dims, 0)
        token = lax.broadcasted_iota(jnp.int32, dims, 1)
        second = (row // group) % 2
        place = (row // (2 * group) * slots + row % slots) * 2 + second
        want = jnp.full(dims, -1, jnp.int32)
        for e in range(experts):
            for k in range(slots):
                index = (e * slots + k) * 2
                want = jnp.where(place == index, picks_s[k, e], want)
                live = jnp.where(k < counts_s[0, e], picks_s[k, e], -1)
                want = jnp.where(place == index + 1, live, want)
        found = (want == token) & (second == 0)
        found_live = (want == token) & (second == 1)
        part_of = (row // slots) % pack
        chosen = [jnp.where(found & (part_of == h), 1.0, 0.0).astype(BF16) for h in range(pack)]
        live = [jnp.where(found_live & (part_of == h), 1.0, 0.0) for h in range(pack)]
        for h in range(pack):
            hot_ref[h] = jnp.concatenate(
                [live[h][(2 * e + 1) * group : (2 * e + 2) * group] for e in range(experts)]
            ).astype(BF16)
        live = [value.astype(BF16) for value in live]
        leaving = []
        for j in range(STEPS):
            for copy in large[2 * pack * j : 2 * pack * (j + 1)]:
                copy.wait()
            total = 0.0
            for h in range(pack):
                now = slice(h * part + j * width, h * part + (j + 1) * width)
                total = total + mm(chosen[h], x_v[:, now]) + mm(live[h], c_v[:, now])
            out_v[:, j * width : (j + 1) * width] = total.astype(BF16)
            now = pl.ds(j * width, width)
            leaving.append(pltpu.make_async_copy(out_v.at[:, now], out_ref.at[:, now], out_sems.at[j]))
            leaving[-1].start()
        for copy in leaving:
            copy.wait()

    return pl.pallas_call(
        body,
        in_specs=[ANYWHERE] * 4,
        out_specs=[ANYWHERE, IN_VMEM],
        out_shape=[shape((count, part)), shape((pack, count // 2, own))],
        scratch_shapes=[
            pltpu.SMEM(picks.shape, jnp.int32),
            pltpu.SMEM(counts.shape, jnp.int32),
            pltpu.VMEM(tokens.shape, BF16),
            pltpu.VMEM(tokens.shape, BF16),
            pltpu.VMEM((count, part), BF16),
            pltpu.SemaphoreType.DMA((STEPS + 1, 2 * pack)),
            pltpu.SemaphoreType.DMA((STEPS,)),
        ],
        compiler_params=PARAMS,
        cost_estimate=cost(4 * count * own * features, 4 * features * own),
    )(*to_hbm(picks, counts, cotangent, tokens))


def scatter_rows(back, hot, seq_n, message=None):
    pack, count, own = hot.shape
    rows = back.shape[0]
    extra = 0 if message is None else riding(seq_n, count // message[1])
    part = back.shape[1] - extra
    width = part // STEPS

    def body(hot_ref, back_ref, *refs):
        hot_v, back_v, out_v, hot_sem, in_sems, out_sems = refs[-6:]
        out_ref = refs[0]
        hot_copy = pltpu.make_async_copy(hot_ref, hot_v, hot_sem)
        hot_copy.start()
        arriving = []
        for i in range(STEPS):
            now = pl.ds(i * width, width + (extra if i + 1 == STEPS else 0))
            arriving.append(pltpu.make_async_copy(back_ref.at[:, now], back_v.at[:, now], in_sems.at[i]))
            arriving[-1].start()
        hot_copy.wait()
        choosers = [jnp.concatenate([hot_v[h]] * seq_n, axis=0) for h in range(pack)]
        leaving = []
        for i in range(STEPS):
            arriving[i].wait()
            for h in range(pack):
                first = h * part + i * width
                rows_now = back_v[:, i * width : (i + 1) * width]
                out_v[:, first : first + width] = mm(choosers[h], rows_now, ROWS).astype(BF16)
                now = pl.ds(first, width)
                leaving.append(pltpu.make_async_copy(out_v.at[:, now], out_ref.at[:, now], out_sems.at[h, i]))
                leaving[-1].start()
        if message is not None:
            router_ref, total_ref = refs[1], refs[2]
            experts, per = router_ref.shape
            group = count // experts
            row = lax.broadcasted_iota(jnp.int32, (rows, experts), 0)
            expert = lax.broadcasted_iota(jnp.int32, (rows, experts), 1)
            mine = row % count // group == expert
            even = jnp.where(mine & (row % 2 == 0), 1.0, 0.0).astype(BF16)
            odd = jnp.where(mine & (row % 2 == 1), 1.0, 0.0).astype(BF16)
            rides = [back_v[:, part + t * LANES : part + (t + 1) * LANES] for t in range(extra // LANES)]
            router = sum(mm(even, ride, ROWS) for ride in rides)
            total = sum(mm(ride, odd, ROWS) for ride in rides)
            router_ref[...] = router[:, :per]
            total_ref[...] = jnp.sum(total[:3], axis=0, keepdims=True)
        for copy in leaving:
            copy.wait()

    out_specs = [ANYWHERE]
    out_shape = [shape((own, part * pack))]
    if message is not None:
        per, experts = message
        out_specs += [IN_VMEM] * 2
        out_shape += [shape((experts, per), F32), shape((1, experts), F32)]
    return pl.pallas_call(
        body,
        in_specs=[ANYWHERE] * 2,
        out_specs=out_specs,
        out_shape=out_shape,
        scratch_shapes=[
            pltpu.VMEM(hot.shape, BF16),
            pltpu.VMEM(back.shape, BF16),
            pltpu.VMEM((own, part * pack), BF16),
            pltpu.SemaphoreType.DMA,
            pltpu.SemaphoreType.DMA((STEPS,)),
            pltpu.SemaphoreType.DMA((pack, STEPS)),
        ],
        compiler_params=SMALL,
        cost_estimate=cost(2 * rows * own * part * pack, 2 * part * pack * own),
    )(*to_hbm(hot), back)


def first_part(rows, pack, slots):
    return (lax.broadcasted_iota(jnp.int32, (rows, 1), 0) // slots) % pack == 0


def fold(parts, slots):
    rows = parts[0].shape[0]
    total = parts[0]
    for h in range(1, len(parts)):
        total = total + pltpu.roll(parts[h], rows - h * slots, 0)
    return total


def spread(value, pack, slots):
    return [value if h == 0 else pltpu.roll(value, h * slots, 0) for h in range(pack)]


class Arrivals:
    def __init__(self, blocks, plan):
        self.blocks, self.plan = blocks, plan

    def start(self, refs, places, sems):
        here = lax.axis_index("seq")
        for k, (a, b, t) in enumerate(self.plan):
            if a == b:
                pltpu.make_async_copy(refs[a], places[k], sems.at[k]).start()
            else:

                @pl.when(here >= t)
                def _():
                    pltpu.make_async_copy(refs[a], places[k], sems.at[k]).start()

                @pl.when(here < t)
                def _():
                    pltpu.make_async_copy(refs[b], places[k], sems.at[k]).start()

    def wait(self, refs, places, sems):
        for k, (a, _, _) in enumerate(self.plan):
            pltpu.make_async_copy(refs[a], places[k], sems.at[k]).wait()


def side_copies(gate_ref, up_ref, router_ref, side, sems, pack, j, width):
    part = side.shape[0]
    hidden_n = gate_ref.shape[2]
    rows = pl.ds(j * width, width)
    copies = []
    for h in range(pack):
        for n, ref in enumerate((gate_ref, up_ref)):
            columns = pl.ds((2 * h + n) * hidden_n, hidden_n)
            copies.append((ref.at[0, pl.ds(h * part + j * width, width), :], side.at[rows, columns]))
    copies.append((router_ref.at[rows, :], side.at[rows, pl.ds(2 * pack * hidden_n, LANES)]))
    return [pltpu.make_async_copy(a, b, sems.at[j, n]) for n, (a, b) in enumerate(copies)]


def down_copies(down_ref, stack, sems, pack):
    hidden_n = down_ref.shape[1]
    part = stack.shape[1]
    return [
        pltpu.make_async_copy(
            down_ref.at[0, :, pl.ds(h * part, part)], stack.at[pl.ds(h * hidden_n, hidden_n), :], sems.at[h]
        )
        for h in range(pack)
    ]


def put_blocks(out, target, columns):
    seq_n, rows, _ = target.shape
    here = lax.axis_index("seq")
    for k in range(seq_n):
        target[lax.rem(here - k + seq_n, seq_n), :, columns] = out[k * rows : (k + 1) * rows]


def expert_forward(arrivals, seq_n, slots, experts, pack, router_side, threshold, w_gate, w_up, w_down, hid_scale):
    block_rows, part = arrivals.blocks[0].shape
    rows = block_rows * seq_n
    hidden_n = w_gate.shape[2]
    both = 2 * hidden_n
    width = part // STEPS
    total = pack * both + LANES
    n_blocks = len(arrivals.blocks)

    def body(*refs):
        blocks = refs[:n_blocks]
        router_ref, gate_ref, up_ref, down_ref, threshold_ref, scale_ref = refs[n_blocks : n_blocks + 6]
        x_ref, out_ref, pre_ref, hidden_ref = refs[n_blocks + 6 : n_blocks + 10]
        pre_v, hidden_v, x_v, out_v, side, stack, x_sems, side_sems, stack_sems, out_sems = refs[n_blocks + 10 :]
        places = [x_v.at[pl.ds(k * block_rows, block_rows), :] for k in range(seq_n)]
        arrivals.start(blocks, places, x_sems)
        chunks = [side_copies(gate_ref, up_ref, router_ref, side, side_sems, pack, j, width) for j in range(STEPS)]
        downs = down_copies(down_ref, stack, stack_sems, pack)
        for copy in sum(chunks, []) + downs:
            copy.start()
        arrivals.wait(blocks, places, x_sems)
        leaving = [pltpu.make_async_copy(x_v, x_ref, out_sems.at[STEPS])]
        leaving[0].start()
        sums = [0.0] * (pack + 1)
        for j, chunk in enumerate(chunks):
            for copy in chunk:
                copy.wait()
            now = slice(j * width, (j + 1) * width)
            for n in range(pack + 1):
                sums[n] = sums[n] + mm(x_v[:, now], side[now, n * both : min((n + 1) * both, total)])
        gate = fold([y[:, :hidden_n] for y in sums[:pack]], slots)
        up = fold([y[:, hidden_n:] for y in sums[:pack]], slots)
        scores = sums[pack]
        lane = lax.broadcasted_iota(jnp.int32, scores.shape, 1)
        expert = lax.axis_index("exp")
        score = fold([jnp.where(lane == h * experts + expert, scores, 0.0) for h in range(pack)], slots)
        lane = lax.broadcasted_iota(jnp.int32, threshold_ref.shape, 1)
        cut = jnp.sum(jnp.where(lane == expert, threshold_ref[...], 0.0), axis=1, keepdims=True)
        g = jax.nn.sigmoid(jnp.sum(score, axis=1, keepdims=True) - cut)
        hidden = gate * jax.nn.sigmoid(gate) * up * scale_ref[...] * g
        hidden = jnp.where(first_part(rows, pack, slots), hidden, 0.0)
        for h, value in enumerate(spread(hidden, pack, slots)):
            now = slice(h * hidden_n, (h + 1) * hidden_n)
            hidden_v[:, now] = value.astype(BF16)
        pre_v[:, :hidden_n] = gate
        pre_v[:, hidden_n:both] = up
        pre_v[:, both:] = jnp.broadcast_to(g, (rows, LANES))
        leaving.append(pltpu.make_async_copy(pre_v, pre_ref, out_sems.at[STEPS + 1]))
        leaving.append(pltpu.make_async_copy(hidden_v, hidden_ref, out_sems.at[STEPS + 2]))
        for copy in leaving[1:]:
            copy.start()
        for copy in downs:
            copy.wait()
        for j in range(STEPS):
            now = slice(j * width, (j + 1) * width)
            put_blocks(mm(hidden_v[...], stack[:, now]).astype(BF16), out_v, now)
            columns = pl.ds(j * width, width)
            leaving.append(pltpu.make_async_copy(out_v.at[:, :, columns], out_ref.at[:, :, columns], out_sems.at[j]))
            leaving[-1].start()
        for copy in leaving:
            copy.wait()

    return pl.pallas_call(
        body,
        in_specs=[ANYWHERE] * (n_blocks + 4) + [IN_VMEM] * 2,
        out_specs=[ANYWHERE] * 4,
        out_shape=[
            shape((rows, part)),
            shape((seq_n, block_rows, part)),
            shape((rows, both + LANES), F32),
            shape((rows, pack * hidden_n)),
        ],
        scratch_shapes=[
            pltpu.VMEM((rows, both + LANES), F32),
            pltpu.VMEM((rows, pack * hidden_n), BF16),
            pltpu.VMEM((rows, part), BF16),
            pltpu.VMEM((seq_n, block_rows, part), BF16),
            pltpu.VMEM((part, total), BF16),
            pltpu.VMEM((pack * hidden_n, part), BF16),
            pltpu.SemaphoreType.DMA((seq_n,)),
            pltpu.SemaphoreType.DMA((STEPS, 2 * pack + 1)),
            pltpu.SemaphoreType.DMA((pack,)),
            pltpu.SemaphoreType.DMA((STEPS + 3,)),
        ],
        compiler_params=PARAMS,
        cost_estimate=cost(6 * rows * part * pack * hidden_n, 12 * part * pack * hidden_n),
    )(*to_hbm(*arrivals.blocks, router_side, w_gate, w_up, w_down), threshold.reshape(1, -1), hid_scale)


def split3(v):
    hi = v.astype(BF16)
    rest = v - hi.astype(F32)
    mid = rest.astype(BF16)
    return hi, mid, (rest - mid.astype(F32)).astype(BF16)


def riding(seq_n, group):
    return LANES * -(-2 * seq_n // group)


def expert_backward(arrivals, seq_n, exp_n, slots, pack, x, pre, router_side, w_gate, w_up, w_down, hid_scale):
    block_rows, part = arrivals.blocks[0].shape
    rows = block_rows * seq_n
    hidden_n = w_gate.shape[2]
    width = part // STEPS
    total = 2 * pack * hidden_n + LANES
    group = pack * slots
    extra = riding(seq_n, group)
    per = part * pack // (seq_n * exp_n)
    n_blocks = len(arrivals.blocks)

    def body(*refs):
        blocks = refs[:n_blocks]
        router_ref, gate_ref, up_ref, down_ref, x_ref, pre_ref, scale_ref = refs[n_blocks : n_blocks + 7]
        c_ref, out_ref, delta_ref = refs[n_blocks + 7 : n_blocks + 10]
        c_v, x_v, pre_v, out_v, side, stack, columns, c_sems, x_sems, side_sems, stack_sems, out_sems = refs[
            n_blocks + 10 :
        ]
        places = [c_v.at[pl.ds(k * block_rows, block_rows), :] for k in range(seq_n)]
        arrivals.start(blocks, places, c_sems)
        chunks = [side_copies(gate_ref, up_ref, router_ref, side, side_sems, pack, j, width) for j in range(STEPS)]
        downs = down_copies(down_ref, stack, stack_sems, pack)
        x_copy = pltpu.make_async_copy(x_ref, x_v, x_sems.at[0])
        pre_copy = pltpu.make_async_copy(pre_ref, pre_v, x_sems.at[1])
        for copy in downs + [pre_copy] + sum(chunks, []) + [x_copy]:
            copy.start()
        arrivals.wait(blocks, places, c_sems)
        leaving = [pltpu.make_async_copy(c_v, c_ref, out_sems.at[STEPS])]
        leaving[0].start()
        for copy in downs:
            copy.wait()
        both = mm(c_v[...], stack[...], LAST)
        parts = [both[:, h * hidden_n : (h + 1) * hidden_n] for h in range(pack)]
        pre_copy.wait()
        raw = jnp.where(first_part(rows, pack, slots), fold(parts, slots) * scale_ref[...], 0.0)
        gate = pre_v[:, :hidden_n]
        up = pre_v[:, hidden_n : 2 * hidden_n]
        g = pre_v[:, 2 * hidden_n : 2 * hidden_n + 1]
        sig = jax.nn.sigmoid(gate)
        act = gate * sig
        score = jnp.sum(act * up * raw, axis=1, keepdims=True) * g * (1.0 - g)
        grad = raw * g
        to_gate = spread(grad * up * sig * (1.0 + gate * (1.0 - sig)), pack, slots)
        to_up = spread(grad * act, pack, slots)
        expert = lax.axis_index("exp")
        lane = lax.broadcasted_iota(jnp.int32, (rows, LANES), 1)
        by_expert = jnp.zeros((rows, LANES), F32)
        by_split = jnp.zeros((rows, LANES), F32)
        for h, value in enumerate(spread(jnp.broadcast_to(score, (rows, LANES)), pack, slots)):
            delta_ref[:, 2 * h * hidden_n : (2 * h + 1) * hidden_n] = to_gate[h].astype(BF16)
            delta_ref[:, (2 * h + 1) * hidden_n : (2 * h + 2) * hidden_n] = to_up[h].astype(BF16)
            for n, piece in enumerate(split3(value)):
                piece = piece.astype(F32)
                by_split = jnp.where(lane == 3 * h + n, piece, by_split)
                if n < 2:
                    by_expert = jnp.where(lane == (n * pack + h) * exp_n + expert, piece, by_expert)
        columns[...] = by_split.astype(BF16)
        delta_ref[:, 2 * pack * hidden_n :] = by_expert.astype(BF16)
        for j, chunk in enumerate(chunks):
            for copy in chunk:
                copy.wait()
            now = slice(j * width, (j + 1) * width)
            put_blocks(mm(delta_ref[...], side[now, :], LAST).astype(BF16), out_v, now)
            if j + 1 < STEPS:
                now = pl.ds(j * width, width)
                leaving.append(pltpu.make_async_copy(out_v.at[:, :, now], out_ref.at[:, :, now], out_sems.at[j]))
                leaving[-1].start()

        here = lax.axis_index("seq")
        x_copy.wait()
        told = mm(columns[...], x_v[...], ROWS)
        sub = lax.broadcasted_iota(jnp.int32, (group, LANES), 0)
        lane = lax.broadcasted_iota(jnp.int32, (group, LANES), 1)
        minus = jnp.broadcast_to(-jnp.sum(score, axis=0, keepdims=True), (group, LANES))
        pieces = [piece.astype(F32) for piece in split3(minus)]
        threshold_row = jnp.zeros((group, LANES), F32)
        for n, piece in enumerate(pieces):
            threshold_row = jnp.where(lane == n, piece, threshold_row)
        for owner in range(seq_n * exp_n):
            h, first = divmod(owner * per, part)
            shift = first % LANES
            value = jnp.sum(told[3 * h : 3 * h + 3, first - shift : first - shift + LANES], axis=0, keepdims=True)
            value = jnp.broadcast_to(value, (group, LANES))
            if shift:
                value = pltpu.roll(value, LANES - shift, 1)
            if per < LANES:
                value = jnp.where(lane < per, value, 0.0)
            d, place = divmod(owner, exp_n)
            for t in range(extra // LANES):
                row = sub + t * group
                now = slice(part + t * LANES, part + (t + 1) * LANES)
                out_v[d, place * group : (place + 1) * group, now] = jnp.where(
                    row == 2 * here, value, jnp.where(row == 2 * here + 1, threshold_row, 0.0)
                ).astype(BF16)
        now = pl.ds((STEPS - 1) * width, width + extra)
        leaving.append(pltpu.make_async_copy(out_v.at[:, :, now], out_ref.at[:, :, now], out_sems.at[STEPS - 1]))
        leaving[-1].start()
        for copy in leaving:
            copy.wait()

    return pl.pallas_call(
        body,
        in_specs=[ANYWHERE] * (n_blocks + 6) + [IN_VMEM],
        out_specs=[ANYWHERE] * 2 + [IN_VMEM],
        out_shape=[
            shape((rows, part)),
            shape((seq_n, block_rows, part + extra)),
            shape((rows, total)),
        ],
        scratch_shapes=[
            pltpu.VMEM((rows, part), BF16),
            pltpu.VMEM((rows, part), BF16),
            pltpu.VMEM(pre.shape, F32),
            pltpu.VMEM((seq_n, block_rows, part + extra), BF16),
            pltpu.VMEM((part, total), BF16),
            pltpu.VMEM((pack * hidden_n, part), BF16),
            pltpu.VMEM((rows, LANES), BF16),
            pltpu.SemaphoreType.DMA((seq_n,)),
            pltpu.SemaphoreType.DMA((2,)),
            pltpu.SemaphoreType.DMA((STEPS, 2 * pack + 1)),
            pltpu.SemaphoreType.DMA((pack,)),
            pltpu.SemaphoreType.DMA((STEPS + 1,)),
        ],
        compiler_params=PARAMS,
        cost_estimate=cost(100 * rows * part * pack * hidden_n, 100 * part * pack * hidden_n),
    )(*to_hbm(*arrivals.blocks, router_side, w_gate, w_up, w_down, x, pre), hid_scale)


def side_grads(x, delta, pack, hidden_n):
    rows, part = x.shape
    width = part // STEPS

    def body(x_ref, delta_ref, gate_out, up_out):
        for h in range(pack):
            both = mm(x_ref[...], delta_ref[:, 2 * h * hidden_n : 2 * (h + 1) * hidden_n], ROWS)
            gate_out[h] = both[:, :hidden_n]
            up_out[h] = both[:, hidden_n:]

    tall = pl.BlockSpec((pack, width, hidden_n), lambda i: (0, i, 0))
    gate, up = pl.pallas_call(
        body,
        grid=(STEPS,),
        in_specs=[
            pl.BlockSpec((rows, width), lambda i: (0, i)),
            pl.BlockSpec(delta.shape, lambda i: (0, 0)),
        ],
        out_specs=[tall, tall],
        out_shape=[shape((pack, part, hidden_n), F32)] * 2,
        compiler_params=PARAMS,
        cost_estimate=cost(4 * rows * part * pack * hidden_n, 8 * part * pack * hidden_n),
    )(*to_hbm(x, delta))
    return gate.reshape(1, part * pack, hidden_n), up.reshape(1, part * pack, hidden_n)


def down_grads(c, hidden, pack, hidden_n):
    rows, part = c.shape
    width = part // 2

    def body(c_ref, hidden_ref, out):
        out[...] = mm(hidden_ref[...], c_ref[...], ROWS)

    return pl.pallas_call(
        body,
        grid=(pack, 2),
        in_specs=[
            pl.BlockSpec((rows, width), lambda h, i: (0, i)),
            pl.BlockSpec((rows, hidden_n), lambda h, i: (0, h)),
        ],
        out_specs=pl.BlockSpec((None, hidden_n, width), lambda h, i: (0, 0, h * 2 + i)),
        out_shape=shape((1, hidden_n, part * pack), F32),
        compiler_params=PARAMS,
        cost_estimate=cost(2 * rows * part * pack * hidden_n, 4 * part * pack * hidden_n),
    )(*to_hbm(c, hidden))


def up_line(block, n, first=0, last=None):
    last = n - 1 if last is None else last
    return lax.ppermute(block, "seq", [(s, s + 1) for s in range(first, last)])


def down_line(block, n, first=1, last=None):
    last = n if last is None else last
    return lax.ppermute(block, "seq", [(s, s - 1) for s in range(first, last)])


def cyclic_gather(block, n):
    shifts = [lax.ppermute(block, "seq", [(s, (s + k) % n) for s in range(n)]) for k in range(1, n)]
    return Arrivals([block] + shifts, [(k, k, 0) for k in range(n)])


def line_gather(block, n):
    ups, downs = [], []
    up = down = block
    for j in range(1, n):
        up = up_line(up, n, j - 1)
        down = down_line(down, n, 1, n - j + 1)
        ups.append(up)
        downs.append(down)
    plan = [(0, 0, 0)] + [(k, 2 * n - 1 - k, k) for k in range(1, n)]
    return Arrivals([block] + ups + downs, plan)


def on_device(tokens, cotangent, router, threshold, w_gate, w_up, w_down, hid_scale, picks, counts):
    experts, slots = picks.shape[1:]
    features = tokens.shape[1]
    true_hidden = w_gate.shape[2]
    extra = -true_hidden % LANES
    if extra:
        w_gate, w_up = (jnp.pad(w, ((0, 0), (0, 0), (0, extra))) for w in (w_gate, w_up))
        w_down = jnp.pad(w_down, ((0, 0), (0, extra), (0, 0)))
        hid_scale = jnp.pad(hid_scale, ((0, 0), (0, extra)))
    hidden_n = true_hidden + extra
    seq_n = lax.axis_size("seq")
    exp_n = lax.axis_size("exp")
    everyone = seq_n * exp_n
    pack = max(1, 8 // slots)
    chosen = picks[0].T

    def to_owners(parts):
        parts = parts.reshape(everyone, -1, parts.shape[2])
        return lax.all_to_all(parts, BOTH, split_axis=0, concat_axis=0, tiled=True).reshape(-1, parts.shape[2])

    sent, hot = choose_rows(tokens, cotangent, chosen, counts, pack)
    sent = sent.reshape(experts, 2, -1, sent.shape[1])
    here = lax.all_to_all(sent, "exp", split_axis=0, concat_axis=0, tiled=True)
    x_rows, c_rows = (here[:, n].reshape(-1, here.shape[3]) for n in range(2))
    x_in = cyclic_gather(x_rows, seq_n)
    c_in = line_gather(c_rows, seq_n)
    halves = list(router.reshape(pack, features // pack, experts))
    router_side = jnp.concatenate(halves + halves, axis=1)
    router_side = jnp.pad(router_side, ((0, 0), (0, LANES - router_side.shape[1])))

    x, out, pre, hidden = expert_forward(
        x_in, seq_n, slots, experts, pack, router_side, threshold, w_gate, w_up, w_down, hid_scale
    )
    out = to_owners(out)
    c, back, delta = expert_backward(
        c_in, seq_n, exp_n, slots, pack, x, pre, router_side, w_gate, w_up, w_down, hid_scale
    )
    back, out = lax.optimization_barrier((back, out))
    back = to_owners(back)
    down_grad = down_grads(c, hidden, pack, hidden_n)
    gate_grad, up_grad = side_grads(x, delta, pack, hidden_n)
    (mixture,) = scatter_rows(out, hot, seq_n)
    token_grad, router_grad, threshold_grad = scatter_rows(back, hot, seq_n, (features // everyone, experts))
    if extra:
        gate_grad, up_grad = gate_grad[:, :, :true_hidden], up_grad[:, :, :true_hidden]
        down_grad = down_grad[:, :true_hidden]
    return mixture, token_grad, router_grad.T, threshold_grad[0], gate_grad, up_grad, down_grad


def solution(mesh):
    by_owner = P(BOTH, None)
    columns = P("exp", None, "seq")
    down = P("exp", "seq", None)
    return jax.shard_map(
        on_device,
        mesh=mesh,
        in_specs=(
            by_owner,
            by_owner,
            P(),
            P(),
            columns,
            columns,
            down,
            P("exp", "seq"),
            P(BOTH, None, None),
            by_owner,
        ),
        out_specs=(by_owner, by_owner, by_owner, P(), columns, columns, down),
        check_vma=False,
    )
```

```python
import jax
import jax.numpy as jnp
from jax import lax
from jax.experimental import pallas as pl
from jax.experimental.pallas import tpu as pltpu
from jax.sharding import PartitionSpec as P

BOTH = ("seq", "exp")
F32 = jnp.float32
BF16 = jnp.bfloat16
ROWS = ((0,), (0,))
LAST = ((1,), (1,))
STEPS = 4
LANES = 128


def mm(a, b, dims=((1,), (0,))):
    return lax.dot_general(a, b, (dims, ((), ())), preferred_element_type=F32)


PARAMS = pltpu.CompilerParams(vmem_limit_bytes=32 * 2**20)
SMALL = pltpu.CompilerParams(vmem_limit_bytes=12 * 2**20)


def to_hbm(*arrays):
    return [pltpu.with_memory_space_constraint(x, pltpu.HBM) for x in arrays]


def cost(flops, moved):
    return pl.CostEstimate(flops=flops, bytes_accessed=moved, transcendentals=0)


def shape(dims, dtype=BF16):
    return pltpu.HBM(dims, dtype)


ANYWHERE = pl.BlockSpec(memory_space=pl.ANY)
IN_VMEM = pl.BlockSpec(memory_space=pltpu.VMEM)


def choose_rows(tokens, cotangent, picks, counts, pack):
    own, features = tokens.shape
    slots, experts = picks.shape
    group = pack * slots
    count = 2 * experts * group
    part = features // pack
    width = part // STEPS

    def body(picks_ref, counts_ref, c_ref, x_ref, out_ref, hot_ref, picks_s, counts_s, c_v, x_v, out_v, sems, out_sems):
        small = [
            pltpu.make_async_copy(picks_ref, picks_s, sems.at[STEPS, 0]),
            pltpu.make_async_copy(counts_ref, counts_s, sems.at[STEPS, 1]),
        ]
        for copy in small:
            copy.start()
        large = []
        for j in range(STEPS):
            for h in range(pack):
                now = pl.ds(h * part + j * width, width)
                for n, (ref, held) in enumerate(((x_ref, x_v), (c_ref, c_v))):
                    large.append(pltpu.make_async_copy(ref.at[:, now], held.at[:, now], sems.at[j, 2 * h + n]))
        for copy in large:
            copy.start()
        for copy in small:
            copy.wait()
        dims = (count, own)
        row = lax.broadcasted_iota(jnp.int32, dims, 0)
        token = lax.broadcasted_iota(jnp.int32, dims, 1)
        second = (row // group) % 2
        place = (row // (2 * group) * slots + row % slots) * 2 + second
        want = jnp.full(dims, -1, jnp.int32)
        for e in range(experts):
            for k in range(slots):
                index = (e * slots + k) * 2
                want = jnp.where(place == index, picks_s[k, e], want)
                live = jnp.where(k < counts_s[0, e], picks_s[k, e], -1)
                want = jnp.where(place == index + 1, live, want)
        found = (want == token) & (second == 0)
        found_live = (want == token) & (second == 1)
        part_of = (row // slots) % pack
        chosen = [jnp.where(found & (part_of == h), 1.0, 0.0).astype(BF16) for h in range(pack)]
        live = [jnp.where(found_live & (part_of == h), 1.0, 0.0) for h in range(pack)]
        for h in range(pack):
            hot_ref[h] = jnp.concatenate(
                [live[h][(2 * e + 1) * group : (2 * e + 2) * group] for e in range(experts)]
            ).astype(BF16)
        live = [value.astype(BF16) for value in live]
        leaving = []
        for j in range(STEPS):
            for copy in large[2 * pack * j : 2 * pack * (j + 1)]:
                copy.wait()
            total = 0.0
            for h in range(pack):
                now = slice(h * part + j * width, h * part + (j + 1) * width)
                total = total + mm(chosen[h], x_v[:, now]) + mm(live[h], c_v[:, now])
            out_v[:, j * width : (j + 1) * width] = total.astype(BF16)
            now = pl.ds(j * width, width)
            leaving.append(pltpu.make_async_copy(out_v.at[:, now], out_ref.at[:, now], out_sems.at[j]))
            leaving[-1].start()
        for copy in leaving:
            copy.wait()

    return pl.pallas_call(
        body,
        in_specs=[ANYWHERE] * 4,
        out_specs=[ANYWHERE, IN_VMEM],
        out_shape=[shape((count, part)), shape((pack, count // 2, own))],
        scratch_shapes=[
            pltpu.SMEM(picks.shape, jnp.int32),
            pltpu.SMEM(counts.shape, jnp.int32),
            pltpu.VMEM(tokens.shape, BF16),
            pltpu.VMEM(tokens.shape, BF16),
            pltpu.VMEM((count, part), BF16),
            pltpu.SemaphoreType.DMA((STEPS + 1, 2 * pack)),
            pltpu.SemaphoreType.DMA((STEPS,)),
        ],
        compiler_params=PARAMS,
        cost_estimate=cost(4 * count * own * features, 4 * features * own),
    )(*to_hbm(picks, counts, cotangent, tokens))


def scatter_rows(back, hot, seq_n, message=None):
    pack, count, own = hot.shape
    rows = back.shape[0]
    extra = 0 if message is None else riding(seq_n, count // message[1])
    part = back.shape[1] - extra
    width = part // STEPS

    def body(hot_ref, back_ref, *refs):
        hot_v, back_v, out_v, hot_sem, in_sems, out_sems = refs[-6:]
        out_ref = refs[0]
        hot_copy = pltpu.make_async_copy(hot_ref, hot_v, hot_sem)
        hot_copy.start()
        arriving = []
        for i in range(STEPS):
            now = pl.ds(i * width, width + (extra if i + 1 == STEPS else 0))
            arriving.append(pltpu.make_async_copy(back_ref.at[:, now], back_v.at[:, now], in_sems.at[i]))
            arriving[-1].start()
        hot_copy.wait()
        choosers = [jnp.concatenate([hot_v[h]] * seq_n, axis=0) for h in range(pack)]
        leaving = []
        for i in range(STEPS):
            arriving[i].wait()
            for h in range(pack):
                first = h * part + i * width
                rows_now = back_v[:, i * width : (i + 1) * width]
                out_v[:, first : first + width] = mm(choosers[h], rows_now, ROWS).astype(BF16)
                now = pl.ds(first, width)
                leaving.append(pltpu.make_async_copy(out_v.at[:, now], out_ref.at[:, now], out_sems.at[h, i]))
                leaving[-1].start()
        if message is not None:
            router_ref, total_ref = refs[1], refs[2]
            experts, per = router_ref.shape
            group = count // experts
            row = lax.broadcasted_iota(jnp.int32, (rows, experts), 0)
            expert = lax.broadcasted_iota(jnp.int32, (rows, experts), 1)
            mine = row % count // group == expert
            even = jnp.where(mine & (row % 2 == 0), 1.0, 0.0).astype(BF16)
            odd = jnp.where(mine & (row % 2 == 1), 1.0, 0.0).astype(BF16)
            rides = [back_v[:, part + t * LANES : part + (t + 1) * LANES] for t in range(extra // LANES)]
            router = sum(mm(even, ride, ROWS) for ride in rides)
            total = sum(mm(ride, odd, ROWS) for ride in rides)
            router_ref[...] = router[:, :per]
            total_ref[...] = jnp.sum(total[:3], axis=0, keepdims=True)
        for copy in leaving:
            copy.wait()

    out_specs = [ANYWHERE]
    out_shape = [shape((own, part * pack))]
    if message is not None:
        per, experts = message
        out_specs += [IN_VMEM] * 2
        out_shape += [shape((experts, per), F32), shape((1, experts), F32)]
    return pl.pallas_call(
        body,
        in_specs=[ANYWHERE] * 2,
        out_specs=out_specs,
        out_shape=out_shape,
        scratch_shapes=[
            pltpu.VMEM(hot.shape, BF16),
            pltpu.VMEM(back.shape, BF16),
            pltpu.VMEM((own, part * pack), BF16),
            pltpu.SemaphoreType.DMA,
            pltpu.SemaphoreType.DMA((STEPS,)),
            pltpu.SemaphoreType.DMA((pack, STEPS)),
        ],
        compiler_params=SMALL,
        cost_estimate=cost(2 * rows * own * part * pack, 2 * part * pack * own),
    )(*to_hbm(hot), back)


def first_part(rows, pack, slots):
    return (lax.broadcasted_iota(jnp.int32, (rows, 1), 0) // slots) % pack == 0


def fold(parts, slots):
    rows = parts[0].shape[0]
    total = parts[0]
    for h in range(1, len(parts)):
        total = total + pltpu.roll(parts[h], rows - h * slots, 0)
    return total


def spread(value, pack, slots):
    return [value if h == 0 else pltpu.roll(value, h * slots, 0) for h in range(pack)]


class Arrivals:
    def __init__(self, blocks, plan):
        self.blocks, self.plan = blocks, plan

    def start(self, refs, places, sems):
        here = lax.axis_index("seq")
        for k, (a, b, t) in enumerate(self.plan):
            if a == b:
                pltpu.make_async_copy(refs[a], places[k], sems.at[k]).start()
            else:

                @pl.when(here >= t)
                def _():
                    pltpu.make_async_copy(refs[a], places[k], sems.at[k]).start()

                @pl.when(here < t)
                def _():
                    pltpu.make_async_copy(refs[b], places[k], sems.at[k]).start()

    def wait(self, refs, places, sems):
        for k, (a, _, _) in enumerate(self.plan):
            pltpu.make_async_copy(refs[a], places[k], sems.at[k]).wait()


def side_copies(gate_ref, up_ref, router_ref, side, sems, pack, j, width):
    part = side.shape[0]
    hidden_n = gate_ref.shape[2]
    rows = pl.ds(j * width, width)
    copies = []
    for h in range(pack):
        for n, ref in enumerate((gate_ref, up_ref)):
            columns = pl.ds((2 * h + n) * hidden_n, hidden_n)
            copies.append((ref.at[0, pl.ds(h * part + j * width, width), :], side.at[rows, columns]))
    copies.append((router_ref.at[rows, :], side.at[rows, pl.ds(2 * pack * hidden_n, LANES)]))
    return [pltpu.make_async_copy(a, b, sems.at[j, n]) for n, (a, b) in enumerate(copies)]


def down_copies(down_ref, stack, sems, pack):
    hidden_n = down_ref.shape[1]
    part = stack.shape[1]
    return [
        pltpu.make_async_copy(
            down_ref.at[0, :, pl.ds(h * part, part)], stack.at[pl.ds(h * hidden_n, hidden_n), :], sems.at[h]
        )
        for h in range(pack)
    ]


def put_blocks(out, target, columns):
    seq_n, rows, _ = target.shape
    here = lax.axis_index("seq")
    for k in range(seq_n):
        target[lax.rem(here - k + seq_n, seq_n), :, columns] = out[k * rows : (k + 1) * rows]


def expert_forward(arrivals, seq_n, slots, experts, pack, router_side, threshold, w_gate, w_up, w_down, hid_scale):
    block_rows, part = arrivals.blocks[0].shape
    rows = block_rows * seq_n
    hidden_n = w_gate.shape[2]
    both = 2 * hidden_n
    width = part // STEPS
    total = pack * both + LANES
    n_blocks = len(arrivals.blocks)

    def body(*refs):
        blocks = refs[:n_blocks]
        router_ref, gate_ref, up_ref, down_ref, threshold_ref, scale_ref = refs[n_blocks : n_blocks + 6]
        x_ref, out_ref, pre_ref, hidden_ref = refs[n_blocks + 6 : n_blocks + 10]
        pre_v, hidden_v, x_v, out_v, side, stack, x_sems, side_sems, stack_sems, out_sems = refs[n_blocks + 10 :]
        places = [x_v.at[pl.ds(k * block_rows, block_rows), :] for k in range(seq_n)]
        arrivals.start(blocks, places, x_sems)
        chunks = [side_copies(gate_ref, up_ref, router_ref, side, side_sems, pack, j, width) for j in range(STEPS)]
        downs = down_copies(down_ref, stack, stack_sems, pack)
        for copy in sum(chunks, []) + downs:
            copy.start()
        arrivals.wait(blocks, places, x_sems)
        leaving = [pltpu.make_async_copy(x_v, x_ref, out_sems.at[STEPS])]
        leaving[0].start()
        sums = [0.0] * (pack + 1)
        for j, chunk in enumerate(chunks):
            for copy in chunk:
                copy.wait()
            now = slice(j * width, (j + 1) * width)
            for n in range(pack + 1):
                sums[n] = sums[n] + mm(x_v[:, now], side[now, n * both : min((n + 1) * both, total)])
        gate = fold([y[:, :hidden_n] for y in sums[:pack]], slots)
        up = fold([y[:, hidden_n:] for y in sums[:pack]], slots)
        scores = sums[pack]
        lane = lax.broadcasted_iota(jnp.int32, scores.shape, 1)
        expert = lax.axis_index("exp")
        score = fold([jnp.where(lane == h * experts + expert, scores, 0.0) for h in range(pack)], slots)
        lane = lax.broadcasted_iota(jnp.int32, threshold_ref.shape, 1)
        cut = jnp.sum(jnp.where(lane == expert, threshold_ref[...], 0.0), axis=1, keepdims=True)
        g = jax.nn.sigmoid(jnp.sum(score, axis=1, keepdims=True) - cut)
        hidden = gate * jax.nn.sigmoid(gate) * up * scale_ref[...] * g
        hidden = jnp.where(first_part(rows, pack, slots), hidden, 0.0)
        for h, value in enumerate(spread(hidden, pack, slots)):
            now = slice(h * hidden_n, (h + 1) * hidden_n)
            hidden_v[:, now] = value.astype(BF16)
        pre_v[:, :hidden_n] = gate
        pre_v[:, hidden_n:both] = up
        pre_v[:, both:] = jnp.broadcast_to(g, (rows, LANES))
        leaving.append(pltpu.make_async_copy(pre_v, pre_ref, out_sems.at[STEPS + 1]))
        leaving.append(pltpu.make_async_copy(hidden_v, hidden_ref, out_sems.at[STEPS + 2]))
        for copy in leaving[1:]:
            copy.start()
        for copy in downs:
            copy.wait()
        for j in range(STEPS):
            now = slice(j * width, (j + 1) * width)
            put_blocks(mm(hidden_v[...], stack[:, now]).astype(BF16), out_v, now)
            columns = pl.ds(j * width, width)
            leaving.append(pltpu.make_async_copy(out_v.at[:, :, columns], out_ref.at[:, :, columns], out_sems.at[j]))
            leaving[-1].start()
        for copy in leaving:
            copy.wait()

    return pl.pallas_call(
        body,
        in_specs=[ANYWHERE] * (n_blocks + 4) + [IN_VMEM] * 2,
        out_specs=[ANYWHERE] * 4,
        out_shape=[
            shape((rows, part)),
            shape((seq_n, block_rows, part)),
            shape((rows, both + LANES), F32),
            shape((rows, pack * hidden_n)),
        ],
        scratch_shapes=[
            pltpu.VMEM((rows, both + LANES), F32),
            pltpu.VMEM((rows, pack * hidden_n), BF16),
            pltpu.VMEM((rows, part), BF16),
            pltpu.VMEM((seq_n, block_rows, part), BF16),
            pltpu.VMEM((part, total), BF16),
            pltpu.VMEM((pack * hidden_n, part), BF16),
            pltpu.SemaphoreType.DMA((seq_n,)),
            pltpu.SemaphoreType.DMA((STEPS, 2 * pack + 1)),
            pltpu.SemaphoreType.DMA((pack,)),
            pltpu.SemaphoreType.DMA((STEPS + 3,)),
        ],
        compiler_params=PARAMS,
        cost_estimate=cost(6 * rows * part * pack * hidden_n, 12 * part * pack * hidden_n),
    )(*to_hbm(*arrivals.blocks, router_side), w_gate, w_up, *to_hbm(w_down), threshold.reshape(1, -1), hid_scale)


def split3(v):
    hi = v.astype(BF16)
    rest = v - hi.astype(F32)
    mid = rest.astype(BF16)
    return hi, mid, (rest - mid.astype(F32)).astype(BF16)


def riding(seq_n, group):
    return LANES * -(-2 * seq_n // group)


def expert_backward(arrivals, seq_n, exp_n, slots, pack, x, pre, router_side, w_gate, w_up, w_down, hid_scale):
    block_rows, part = arrivals.blocks[0].shape
    rows = block_rows * seq_n
    hidden_n = w_gate.shape[2]
    width = part // STEPS
    total = 2 * pack * hidden_n + LANES
    group = pack * slots
    extra = riding(seq_n, group)
    per = part * pack // (seq_n * exp_n)
    n_blocks = len(arrivals.blocks)

    def body(*refs):
        blocks = refs[:n_blocks]
        router_ref, gate_ref, up_ref, down_ref, x_ref, pre_ref, scale_ref = refs[n_blocks : n_blocks + 7]
        c_ref, out_ref, delta_ref = refs[n_blocks + 7 : n_blocks + 10]
        c_v, x_v, pre_v, out_v, side, stack, columns, c_sems, x_sems, side_sems, stack_sems, out_sems = refs[
            n_blocks + 10 :
        ]
        places = [c_v.at[pl.ds(k * block_rows, block_rows), :] for k in range(seq_n)]
        arrivals.start(blocks, places, c_sems)
        chunks = [side_copies(gate_ref, up_ref, router_ref, side, side_sems, pack, j, width) for j in range(STEPS)]
        downs = down_copies(down_ref, stack, stack_sems, pack)
        x_copy = pltpu.make_async_copy(x_ref, x_v, x_sems.at[0])
        pre_copy = pltpu.make_async_copy(pre_ref, pre_v, x_sems.at[1])
        for copy in downs + [pre_copy] + sum(chunks, []) + [x_copy]:
            copy.start()
        arrivals.wait(blocks, places, c_sems)
        leaving = [pltpu.make_async_copy(c_v, c_ref, out_sems.at[STEPS])]
        leaving[0].start()
        for copy in downs:
            copy.wait()
        both = mm(c_v[...], stack[...], LAST)
        parts = [both[:, h * hidden_n : (h + 1) * hidden_n] for h in range(pack)]
        pre_copy.wait()
        raw = jnp.where(first_part(rows, pack, slots), fold(parts, slots) * scale_ref[...], 0.0)
        gate = pre_v[:, :hidden_n]
        up = pre_v[:, hidden_n : 2 * hidden_n]
        g = pre_v[:, 2 * hidden_n : 2 * hidden_n + 1]
        sig = jax.nn.sigmoid(gate)
        act = gate * sig
        score = jnp.sum(act * up * raw, axis=1, keepdims=True) * g * (1.0 - g)
        grad = raw * g
        to_gate = spread(grad * up * sig * (1.0 + gate * (1.0 - sig)), pack, slots)
        to_up = spread(grad * act, pack, slots)
        expert = lax.axis_index("exp")
        lane = lax.broadcasted_iota(jnp.int32, (rows, LANES), 1)
        by_expert = jnp.zeros((rows, LANES), F32)
        by_split = jnp.zeros((rows, LANES), F32)
        for h, value in enumerate(spread(jnp.broadcast_to(score, (rows, LANES)), pack, slots)):
            delta_ref[:, 2 * h * hidden_n : (2 * h + 1) * hidden_n] = to_gate[h].astype(BF16)
            delta_ref[:, (2 * h + 1) * hidden_n : (2 * h + 2) * hidden_n] = to_up[h].astype(BF16)
            for n, piece in enumerate(split3(value)):
                piece = piece.astype(F32)
                by_split = jnp.where(lane == 3 * h + n, piece, by_split)
                if n < 2:
                    by_expert = jnp.where(lane == (n * pack + h) * exp_n + expert, piece, by_expert)
        columns[...] = by_split.astype(BF16)
        delta_ref[:, 2 * pack * hidden_n :] = by_expert.astype(BF16)
        for j, chunk in enumerate(chunks):
            for copy in chunk:
                copy.wait()
            now = slice(j * width, (j + 1) * width)
            put_blocks(mm(delta_ref[...], side[now, :], LAST).astype(BF16), out_v, now)
            if j + 1 < STEPS:
                now = pl.ds(j * width, width)
                leaving.append(pltpu.make_async_copy(out_v.at[:, :, now], out_ref.at[:, :, now], out_sems.at[j]))
                leaving[-1].start()

        here = lax.axis_index("seq")
        x_copy.wait()
        told = mm(columns[...], x_v[...], ROWS)
        sub = lax.broadcasted_iota(jnp.int32, (group, LANES), 0)
        lane = lax.broadcasted_iota(jnp.int32, (group, LANES), 1)
        minus = jnp.broadcast_to(-jnp.sum(score, axis=0, keepdims=True), (group, LANES))
        pieces = [piece.astype(F32) for piece in split3(minus)]
        threshold_row = jnp.zeros((group, LANES), F32)
        for n, piece in enumerate(pieces):
            threshold_row = jnp.where(lane == n, piece, threshold_row)
        for owner in range(seq_n * exp_n):
            h, first = divmod(owner * per, part)
            shift = first % LANES
            value = jnp.sum(told[3 * h : 3 * h + 3, first - shift : first - shift + LANES], axis=0, keepdims=True)
            value = jnp.broadcast_to(value, (group, LANES))
            if shift:
                value = pltpu.roll(value, LANES - shift, 1)
            if per < LANES:
                value = jnp.where(lane < per, value, 0.0)
            d, place = divmod(owner, exp_n)
            for t in range(extra // LANES):
                row = sub + t * group
                now = slice(part + t * LANES, part + (t + 1) * LANES)
                out_v[d, place * group : (place + 1) * group, now] = jnp.where(
                    row == 2 * here, value, jnp.where(row == 2 * here + 1, threshold_row, 0.0)
                ).astype(BF16)
        now = pl.ds((STEPS - 1) * width, width + extra)
        leaving.append(pltpu.make_async_copy(out_v.at[:, :, now], out_ref.at[:, :, now], out_sems.at[STEPS - 1]))
        leaving[-1].start()
        for copy in leaving:
            copy.wait()

    return pl.pallas_call(
        body,
        in_specs=[ANYWHERE] * (n_blocks + 6) + [IN_VMEM],
        out_specs=[ANYWHERE] * 2 + [IN_VMEM],
        out_shape=[
            shape((rows, part)),
            shape((seq_n, block_rows, part + extra)),
            shape((rows, total)),
        ],
        scratch_shapes=[
            pltpu.VMEM((rows, part), BF16),
            pltpu.VMEM((rows, part), BF16),
            pltpu.VMEM(pre.shape, F32),
            pltpu.VMEM((seq_n, block_rows, part + extra), BF16),
            pltpu.VMEM((part, total), BF16),
            pltpu.VMEM((pack * hidden_n, part), BF16),
            pltpu.VMEM((rows, LANES), BF16),
            pltpu.SemaphoreType.DMA((seq_n,)),
            pltpu.SemaphoreType.DMA((2,)),
            pltpu.SemaphoreType.DMA((STEPS, 2 * pack + 1)),
            pltpu.SemaphoreType.DMA((pack,)),
            pltpu.SemaphoreType.DMA((STEPS + 1,)),
        ],
        compiler_params=PARAMS,
        cost_estimate=cost(100 * rows * part * pack * hidden_n, 100 * part * pack * hidden_n),
    )(*to_hbm(*arrivals.blocks, router_side, w_gate, w_up, w_down, x, pre), hid_scale)


def side_grads(x, delta, pack, hidden_n):
    rows, part = x.shape
    width = part // STEPS

    def body(x_ref, delta_ref, gate_out, up_out):
        for h in range(pack):
            both = mm(x_ref[...], delta_ref[:, 2 * h * hidden_n : 2 * (h + 1) * hidden_n], ROWS)
            gate_out[h] = both[:, :hidden_n]
            up_out[h] = both[:, hidden_n:]

    tall = pl.BlockSpec((pack, width, hidden_n), lambda i: (0, i, 0))
    gate, up = pl.pallas_call(
        body,
        grid=(STEPS,),
        in_specs=[
            pl.BlockSpec((rows, width), lambda i: (0, i)),
            pl.BlockSpec(delta.shape, lambda i: (0, 0)),
        ],
        out_specs=[tall, tall],
        out_shape=[shape((pack, part, hidden_n), F32)] * 2,
        compiler_params=PARAMS,
        cost_estimate=cost(4 * rows * part * pack * hidden_n, 8 * part * pack * hidden_n),
    )(*to_hbm(x, delta))
    return gate.reshape(1, part * pack, hidden_n), up.reshape(1, part * pack, hidden_n)


def down_grads(c, hidden, pack, hidden_n):
    rows, part = c.shape
    width = part // 2

    def body(c_ref, hidden_ref, out):
        out[...] = mm(hidden_ref[...], c_ref[...], ROWS)

    return pl.pallas_call(
        body,
        grid=(pack, 2),
        in_specs=[
            pl.BlockSpec((rows, width), lambda h, i: (0, i)),
            pl.BlockSpec((rows, hidden_n), lambda h, i: (0, h)),
        ],
        out_specs=pl.BlockSpec((None, hidden_n, width), lambda h, i: (0, 0, h * 2 + i)),
        out_shape=shape((1, hidden_n, part * pack), F32),
        compiler_params=PARAMS,
        cost_estimate=cost(2 * rows * part * pack * hidden_n, 4 * part * pack * hidden_n),
    )(*to_hbm(c, hidden))


def up_line(block, n, first=0, last=None):
    last = n - 1 if last is None else last
    return lax.ppermute(block, "seq", [(s, s + 1) for s in range(first, last)])


def down_line(block, n, first=1, last=None):
    last = n if last is None else last
    return lax.ppermute(block, "seq", [(s, s - 1) for s in range(first, last)])


def line_gather(block, n):
    ups, downs = [], []
    up = down = block
    for j in range(1, n):
        up = up_line(up, n, j - 1)
        down = down_line(down, n, 1, n - j + 1)
        ups.append(up)
        downs.append(down)
    plan = [(0, 0, 0)] + [(k, 2 * n - 1 - k, k) for k in range(1, n)]
    return Arrivals([block] + ups + downs, plan)


def on_device(tokens, cotangent, router, threshold, w_gate, w_up, w_down, hid_scale, picks, counts):
    experts, slots = picks.shape[1:]
    features = tokens.shape[1]
    true_hidden = w_gate.shape[2]
    extra = -true_hidden % LANES
    if extra:
        w_gate, w_up = (jnp.pad(w, ((0, 0), (0, 0), (0, extra))) for w in (w_gate, w_up))
        w_down = jnp.pad(w_down, ((0, 0), (0, extra), (0, 0)))
        hid_scale = jnp.pad(hid_scale, ((0, 0), (0, extra)))
    hidden_n = true_hidden + extra
    seq_n = lax.axis_size("seq")
    exp_n = lax.axis_size("exp")
    everyone = seq_n * exp_n
    pack = max(1, 8 // slots)
    chosen = picks[0].T

    def to_owners(parts):
        parts = parts.reshape(everyone, -1, parts.shape[2])
        return lax.all_to_all(parts, BOTH, split_axis=0, concat_axis=0, tiled=True).reshape(-1, parts.shape[2])

    sent, hot = choose_rows(tokens, cotangent, chosen, counts, pack)
    sent = sent.reshape(experts, 2, -1, sent.shape[1])
    here = lax.all_to_all(sent, "exp", split_axis=0, concat_axis=0, tiled=True)
    x_in, c_in = (line_gather(here[:, n].reshape(-1, here.shape[3]), seq_n) for n in range(2))
    halves = list(router.reshape(pack, features // pack, experts))
    router_side = jnp.concatenate(halves + halves, axis=1)
    router_side = jnp.pad(router_side, ((0, 0), (0, LANES - router_side.shape[1])))

    x, out, pre, hidden = expert_forward(
        x_in, seq_n, slots, experts, pack, router_side, threshold, w_gate, w_up, w_down, hid_scale
    )
    out = to_owners(out)
    c, back, delta = expert_backward(
        c_in, seq_n, exp_n, slots, pack, x, pre, router_side, w_gate, w_up, w_down, hid_scale
    )
    back, out = lax.optimization_barrier((back, out))
    back = to_owners(back)
    down_grad = down_grads(c, hidden, pack, hidden_n)
    gate_grad, up_grad = side_grads(x, delta, pack, hidden_n)
    (mixture,) = scatter_rows(out, hot, seq_n)
    token_grad, router_grad, threshold_grad = scatter_rows(back, hot, seq_n, (features // everyone, experts))
    if extra:
        gate_grad, up_grad = gate_grad[:, :, :true_hidden], up_grad[:, :, :true_hidden]
        down_grad = down_grad[:, :true_hidden]
    return mixture, token_grad, router_grad.T, threshold_grad[0], gate_grad, up_grad, down_grad


def solution(mesh):
    by_owner = P(BOTH, None)
    columns = P("exp", None, "seq")
    down = P("exp", "seq", None)
    return jax.shard_map(
        on_device,
        mesh=mesh,
        in_specs=(
            by_owner,
            by_owner,
            P(),
            P(),
            columns,
            columns,
            down,
            P("exp", "seq"),
            P(BOTH, None, None),
            by_owner,
        ),
        out_specs=(by_owner, by_owner, by_owner, P(), columns, columns, down),
        check_vma=False,
    )
```

```python
import jax
import jax.numpy as jnp
from jax import lax
from jax.experimental import pallas as pl
from jax.experimental.pallas import tpu as pltpu
from jax.sharding import PartitionSpec as P

BOTH = ("seq", "exp")
F32 = jnp.float32
BF16 = jnp.bfloat16
ROWS = ((0,), (0,))
LAST = ((1,), (1,))
STEPS = 4
LANES = 128


def mm(a, b, dims=((1,), (0,))):
    return lax.dot_general(a, b, (dims, ((), ())), preferred_element_type=F32)


PARAMS = pltpu.CompilerParams(vmem_limit_bytes=32 * 2**20)
SMALL = pltpu.CompilerParams(vmem_limit_bytes=12 * 2**20)


def to_hbm(*arrays):
    return [pltpu.with_memory_space_constraint(x, pltpu.HBM) for x in arrays]


def cost(flops, moved):
    return pl.CostEstimate(flops=flops, bytes_accessed=moved, transcendentals=0)


def shape(dims, dtype=BF16):
    return pltpu.HBM(dims, dtype)


ANYWHERE = pl.BlockSpec(memory_space=pl.ANY)
IN_VMEM = pl.BlockSpec(memory_space=pltpu.VMEM)


def choose_rows(tokens, cotangent, picks, counts, pack):
    own, features = tokens.shape
    slots, experts = picks.shape
    group = pack * slots
    count = 2 * experts * group
    part = features // pack
    width = part // STEPS

    def body(picks_ref, counts_ref, c_ref, x_ref, out_ref, hot_ref, picks_s, counts_s, c_v, x_v, out_v, sems, out_sems):
        small = [
            pltpu.make_async_copy(picks_ref, picks_s, sems.at[STEPS, 0]),
            pltpu.make_async_copy(counts_ref, counts_s, sems.at[STEPS, 1]),
        ]
        for copy in small:
            copy.start()
        large = []
        for j in range(STEPS):
            for h in range(pack):
                now = pl.ds(h * part + j * width, width)
                for n, (ref, held) in enumerate(((x_ref, x_v), (c_ref, c_v))):
                    large.append(pltpu.make_async_copy(ref.at[:, now], held.at[:, now], sems.at[j, 2 * h + n]))
        for copy in large:
            copy.start()
        for copy in small:
            copy.wait()
        dims = (count, own)
        row = lax.broadcasted_iota(jnp.int32, dims, 0)
        token = lax.broadcasted_iota(jnp.int32, dims, 1)
        second = (row // group) % 2
        place = (row // (2 * group) * slots + row % slots) * 2 + second
        want = jnp.full(dims, -1, jnp.int32)
        for e in range(experts):
            for k in range(slots):
                index = (e * slots + k) * 2
                want = jnp.where(place == index, picks_s[k, e], want)
                live = jnp.where(k < counts_s[0, e], picks_s[k, e], -1)
                want = jnp.where(place == index + 1, live, want)
        found = (want == token) & (second == 0)
        found_live = (want == token) & (second == 1)
        part_of = (row // slots) % pack
        chosen = [jnp.where(found & (part_of == h), 1.0, 0.0).astype(BF16) for h in range(pack)]
        live = [jnp.where(found_live & (part_of == h), 1.0, 0.0) for h in range(pack)]
        for h in range(pack):
            hot_ref[h] = jnp.concatenate(
                [live[h][(2 * e + 1) * group : (2 * e + 2) * group] for e in range(experts)]
            ).astype(BF16)
        live = [value.astype(BF16) for value in live]
        leaving = []
        for j in range(STEPS):
            for copy in large[2 * pack * j : 2 * pack * (j + 1)]:
                copy.wait()
            total = 0.0
            for h in range(pack):
                now = slice(h * part + j * width, h * part + (j + 1) * width)
                total = total + mm(chosen[h], x_v[:, now]) + mm(live[h], c_v[:, now])
            out_v[:, j * width : (j + 1) * width] = total.astype(BF16)
            now = pl.ds(j * width, width)
            leaving.append(pltpu.make_async_copy(out_v.at[:, now], out_ref.at[:, now], out_sems.at[j]))
            leaving[-1].start()
        for copy in leaving:
            copy.wait()

    return pl.pallas_call(
        body,
        in_specs=[ANYWHERE] * 4,
        out_specs=[ANYWHERE, IN_VMEM],
        out_shape=[shape((count, part)), shape((pack, count // 2, own))],
        scratch_shapes=[
            pltpu.SMEM(picks.shape, jnp.int32),
            pltpu.SMEM(counts.shape, jnp.int32),
            pltpu.VMEM(tokens.shape, BF16),
            pltpu.VMEM(tokens.shape, BF16),
            pltpu.VMEM((count, part), BF16),
            pltpu.SemaphoreType.DMA((STEPS + 1, 2 * pack)),
            pltpu.SemaphoreType.DMA((STEPS,)),
        ],
        compiler_params=PARAMS,
        cost_estimate=cost(4 * count * own * features, 4 * features * own),
    )(*to_hbm(picks, counts, cotangent, tokens))


def scatter_rows(back, hot, seq_n, message=None):
    pack, count, own = hot.shape
    rows = back.shape[0]
    extra = 0 if message is None else riding(seq_n, count // message[1])
    part = back.shape[1] - extra
    width = part // STEPS

    def body(hot_ref, back_ref, *refs):
        hot_v, back_v, out_v, hot_sem, in_sems, out_sems = refs[-6:]
        out_ref = refs[0]
        hot_copy = pltpu.make_async_copy(hot_ref, hot_v, hot_sem)
        hot_copy.start()
        arriving = []
        for i in range(STEPS):
            now = pl.ds(i * width, width + (extra if i + 1 == STEPS else 0))
            arriving.append(pltpu.make_async_copy(back_ref.at[:, now], back_v.at[:, now], in_sems.at[i]))
            arriving[-1].start()
        hot_copy.wait()
        choosers = [jnp.concatenate([hot_v[h]] * seq_n, axis=0) for h in range(pack)]
        leaving = []
        for i in range(STEPS):
            arriving[i].wait()
            for h in range(pack):
                first = h * part + i * width
                rows_now = back_v[:, i * width : (i + 1) * width]
                out_v[:, first : first + width] = mm(choosers[h], rows_now, ROWS).astype(BF16)
                now = pl.ds(first, width)
                leaving.append(pltpu.make_async_copy(out_v.at[:, now], out_ref.at[:, now], out_sems.at[h, i]))
                leaving[-1].start()
        if message is not None:
            router_ref, total_ref = refs[1], refs[2]
            experts, per = router_ref.shape
            group = count // experts
            row = lax.broadcasted_iota(jnp.int32, (rows, experts), 0)
            expert = lax.broadcasted_iota(jnp.int32, (rows, experts), 1)
            mine = row % count // group == expert
            even = jnp.where(mine & (row % 2 == 0), 1.0, 0.0).astype(BF16)
            odd = jnp.where(mine & (row % 2 == 1), 1.0, 0.0).astype(BF16)
            rides = [back_v[:, part + t * LANES : part + (t + 1) * LANES] for t in range(extra // LANES)]
            router = sum(mm(even, ride, ROWS) for ride in rides)
            total = sum(mm(ride, odd, ROWS) for ride in rides)
            router_ref[...] = router[:, :per]
            total_ref[...] = jnp.sum(total[:3], axis=0, keepdims=True)
        for copy in leaving:
            copy.wait()

    out_specs = [ANYWHERE]
    out_shape = [shape((own, part * pack))]
    if message is not None:
        per, experts = message
        out_specs += [IN_VMEM] * 2
        out_shape += [shape((experts, per), F32), shape((1, experts), F32)]
    return pl.pallas_call(
        body,
        in_specs=[ANYWHERE] * 2,
        out_specs=out_specs,
        out_shape=out_shape,
        scratch_shapes=[
            pltpu.VMEM(hot.shape, BF16),
            pltpu.VMEM(back.shape, BF16),
            pltpu.VMEM((own, part * pack), BF16),
            pltpu.SemaphoreType.DMA,
            pltpu.SemaphoreType.DMA((STEPS,)),
            pltpu.SemaphoreType.DMA((pack, STEPS)),
        ],
        compiler_params=SMALL,
        cost_estimate=cost(2 * rows * own * part * pack, 2 * part * pack * own),
    )(*to_hbm(hot), back)


def first_part(rows, pack, slots):
    return (lax.broadcasted_iota(jnp.int32, (rows, 1), 0) // slots) % pack == 0


def fold(parts, slots):
    rows = parts[0].shape[0]
    total = parts[0]
    for h in range(1, len(parts)):
        total = total + pltpu.roll(parts[h], rows - h * slots, 0)
    return total


def spread(value, pack, slots):
    return [value if h == 0 else pltpu.roll(value, h * slots, 0) for h in range(pack)]


class Arrivals:
    def __init__(self, blocks, plan):
        self.blocks, self.plan = blocks, plan

    def start(self, refs, places, sems):
        here = lax.axis_index("seq")
        for k, (a, b, t) in enumerate(self.plan):
            if a == b:
                pltpu.make_async_copy(refs[a], places[k], sems.at[k]).start()
            else:

                @pl.when(here >= t)
                def _():
                    pltpu.make_async_copy(refs[a], places[k], sems.at[k]).start()

                @pl.when(here < t)
                def _():
                    pltpu.make_async_copy(refs[b], places[k], sems.at[k]).start()

    def wait(self, refs, places, sems):
        for k, (a, _, _) in enumerate(self.plan):
            pltpu.make_async_copy(refs[a], places[k], sems.at[k]).wait()


def router_rows(ref, pack, copies, rows):
    part = ref.shape[1] // pack
    wide = ref[...].astype(F32)
    pieces = [wide[:, h * part : (h + 1) * part] for h in range(pack)] * copies
    left = rows - len(pieces) * ref.shape[0]
    if left:
        pieces.append(jnp.zeros((left, part), F32))
    return jnp.concatenate(pieces).astype(BF16)


def side_copies(gate_ref, up_ref, side, sems, pack, j, width):
    part = side.shape[0]
    hidden_n = gate_ref.shape[2]
    rows = pl.ds(j * width, width)
    copies = []
    for h in range(pack):
        for n, ref in enumerate((gate_ref, up_ref)):
            columns = pl.ds((2 * h + n) * hidden_n, hidden_n)
            copies.append((ref.at[0, pl.ds(h * part + j * width, width), :], side.at[rows, columns]))
    return [pltpu.make_async_copy(a, b, sems.at[j, n]) for n, (a, b) in enumerate(copies)]


def down_copies(down_ref, stack, sems, pack):
    hidden_n = down_ref.shape[1]
    part = stack.shape[1]
    return [
        pltpu.make_async_copy(
            down_ref.at[0, :, pl.ds(h * part, part)], stack.at[pl.ds(h * hidden_n, hidden_n), :], sems.at[h]
        )
        for h in range(pack)
    ]


def put_blocks(out, target, columns):
    seq_n, rows, _ = target.shape
    here = lax.axis_index("seq")
    for k in range(seq_n):
        target[lax.rem(here - k + seq_n, seq_n), :, columns] = out[k * rows : (k + 1) * rows]


def expert_forward(arrivals, seq_n, slots, experts, pack, router_t, threshold, w_gate, w_up, w_down, hid_scale):
    block_rows, part = arrivals.blocks[0].shape
    rows = block_rows * seq_n
    hidden_n = w_gate.shape[2]
    both = 2 * hidden_n
    width = part // STEPS
    total = pack * both
    n_blocks = len(arrivals.blocks)

    def body(*refs):
        blocks = refs[:n_blocks]
        gate_ref, up_ref, down_ref, router_ref, threshold_ref, scale_ref = refs[n_blocks : n_blocks + 6]
        x_ref, out_ref, pre_ref, hidden_ref = refs[n_blocks + 6 : n_blocks + 10]
        pre_v, hidden_v, x_v, out_v, side, stack, x_sems, side_sems, stack_sems, out_sems = refs[n_blocks + 10 :]
        places = [x_v.at[pl.ds(k * block_rows, block_rows), :] for k in range(seq_n)]
        arrivals.start(blocks, places, x_sems)
        chunks = [side_copies(gate_ref, up_ref, side, side_sems, pack, j, width) for j in range(STEPS)]
        downs = down_copies(down_ref, stack, stack_sems, pack)
        for copy in sum(chunks, []) + downs:
            copy.start()
        arrivals.wait(blocks, places, x_sems)
        leaving = [pltpu.make_async_copy(x_v, x_ref, out_sems.at[STEPS])]
        leaving[0].start()
        sums = [0.0] * pack
        scores = mm(x_v[...], router_rows(router_ref, pack, 1, pack * experts), LAST)
        for j, chunk in enumerate(chunks):
            for copy in chunk:
                copy.wait()
            now = slice(j * width, (j + 1) * width)
            for n in range(pack):
                sums[n] = sums[n] + mm(x_v[:, now], side[now, n * both : (n + 1) * both])
        gate = fold([y[:, :hidden_n] for y in sums], slots)
        up = fold([y[:, hidden_n:] for y in sums], slots)
        lane = lax.broadcasted_iota(jnp.int32, scores.shape, 1)
        expert = lax.axis_index("exp")
        score = fold([jnp.where(lane == h * experts + expert, scores, 0.0) for h in range(pack)], slots)
        lane = lax.broadcasted_iota(jnp.int32, threshold_ref.shape, 1)
        cut = jnp.sum(jnp.where(lane == expert, threshold_ref[...], 0.0), axis=1, keepdims=True)
        g = jax.nn.sigmoid(jnp.sum(score, axis=1, keepdims=True) - cut)
        hidden = gate * jax.nn.sigmoid(gate) * up * scale_ref[...] * g
        hidden = jnp.where(first_part(rows, pack, slots), hidden, 0.0)
        for h, value in enumerate(spread(hidden, pack, slots)):
            now = slice(h * hidden_n, (h + 1) * hidden_n)
            hidden_v[:, now] = value.astype(BF16)
        pre_v[:, :hidden_n] = gate
        pre_v[:, hidden_n:both] = up
        pre_v[:, both:] = jnp.broadcast_to(g, (rows, LANES))
        leaving.append(pltpu.make_async_copy(pre_v, pre_ref, out_sems.at[STEPS + 1]))
        leaving.append(pltpu.make_async_copy(hidden_v, hidden_ref, out_sems.at[STEPS + 2]))
        for copy in leaving[1:]:
            copy.start()
        for copy in downs:
            copy.wait()
        for j in range(STEPS):
            now = slice(j * width, (j + 1) * width)
            put_blocks(mm(hidden_v[...], stack[:, now]).astype(BF16), out_v, now)
            columns = pl.ds(j * width, width)
            leaving.append(pltpu.make_async_copy(out_v.at[:, :, columns], out_ref.at[:, :, columns], out_sems.at[j]))
            leaving[-1].start()
        for copy in leaving:
            copy.wait()

    return pl.pallas_call(
        body,
        in_specs=[ANYWHERE] * (n_blocks + 3) + [IN_VMEM] * 3,
        out_specs=[ANYWHERE] * 4,
        out_shape=[
            shape((rows, part)),
            shape((seq_n, block_rows, part)),
            shape((rows, both + LANES), F32),
            shape((rows, pack * hidden_n)),
        ],
        scratch_shapes=[
            pltpu.VMEM((rows, both + LANES), F32),
            pltpu.VMEM((rows, pack * hidden_n), BF16),
            pltpu.VMEM((rows, part), BF16),
            pltpu.VMEM((seq_n, block_rows, part), BF16),
            pltpu.VMEM((part, total), BF16),
            pltpu.VMEM((pack * hidden_n, part), BF16),
            pltpu.SemaphoreType.DMA((seq_n,)),
            pltpu.SemaphoreType.DMA((STEPS, 2 * pack)),
            pltpu.SemaphoreType.DMA((pack,)),
            pltpu.SemaphoreType.DMA((STEPS + 3,)),
        ],
        compiler_params=PARAMS,
        cost_estimate=cost(6 * rows * part * pack * hidden_n, 12 * part * pack * hidden_n),
    )(
        *to_hbm(*arrivals.blocks),
        w_gate,
        *to_hbm(w_up, w_down),
        router_t,
        threshold.reshape(1, -1),
        hid_scale,
    )


def split3(v):
    hi = v.astype(BF16)
    rest = v - hi.astype(F32)
    mid = rest.astype(BF16)
    return hi, mid, (rest - mid.astype(F32)).astype(BF16)


def riding(seq_n, group):
    return LANES * -(-2 * seq_n // group)


def expert_backward(arrivals, seq_n, exp_n, slots, pack, x, pre, router_t, w_gate, w_up, w_down, hid_scale):
    block_rows, part = arrivals.blocks[0].shape
    rows = block_rows * seq_n
    hidden_n = w_gate.shape[2]
    width = part // STEPS
    total = 2 * pack * hidden_n
    group = pack * slots
    extra = riding(seq_n, group)
    per = part * pack // (seq_n * exp_n)
    n_blocks = len(arrivals.blocks)

    def body(*refs):
        blocks = refs[:n_blocks]
        gate_ref, up_ref, down_ref, x_ref, pre_ref, router_ref, scale_ref = refs[n_blocks : n_blocks + 7]
        c_ref, out_ref, delta_ref = refs[n_blocks + 7 : n_blocks + 10]
        c_v, x_v, pre_v, out_v, side, stack, columns, router_v, c_sems, x_sems, side_sems, stack_sems, out_sems = refs[
            n_blocks + 10 :
        ]
        places = [c_v.at[pl.ds(k * block_rows, block_rows), :] for k in range(seq_n)]
        arrivals.start(blocks, places, c_sems)
        chunks = [side_copies(gate_ref, up_ref, side, side_sems, pack, j, width) for j in range(STEPS)]
        downs = down_copies(down_ref, stack, stack_sems, pack)
        x_copy = pltpu.make_async_copy(x_ref, x_v, x_sems.at[0])
        pre_copy = pltpu.make_async_copy(pre_ref, pre_v, x_sems.at[1])
        for copy in downs + [pre_copy] + sum(chunks, []) + [x_copy]:
            copy.start()
        arrivals.wait(blocks, places, c_sems)
        leaving = [pltpu.make_async_copy(c_v, c_ref, out_sems.at[STEPS])]
        leaving[0].start()
        for copy in downs:
            copy.wait()
        both = mm(c_v[...], stack[...], LAST)
        parts = [both[:, h * hidden_n : (h + 1) * hidden_n] for h in range(pack)]
        pre_copy.wait()
        raw = jnp.where(first_part(rows, pack, slots), fold(parts, slots) * scale_ref[...], 0.0)
        gate = pre_v[:, :hidden_n]
        up = pre_v[:, hidden_n : 2 * hidden_n]
        g = pre_v[:, 2 * hidden_n : 2 * hidden_n + 1]
        sig = jax.nn.sigmoid(gate)
        act = gate * sig
        score = jnp.sum(act * up * raw, axis=1, keepdims=True) * g * (1.0 - g)
        grad = raw * g
        to_gate = spread(grad * up * sig * (1.0 + gate * (1.0 - sig)), pack, slots)
        to_up = spread(grad * act, pack, slots)
        expert = lax.axis_index("exp")
        lane = lax.broadcasted_iota(jnp.int32, (rows, LANES), 1)
        by_expert = jnp.zeros((rows, LANES), F32)
        by_split = jnp.zeros((rows, LANES), F32)
        for h, value in enumerate(spread(jnp.broadcast_to(score, (rows, LANES)), pack, slots)):
            delta_ref[:, 2 * h * hidden_n : (2 * h + 1) * hidden_n] = to_gate[h].astype(BF16)
            delta_ref[:, (2 * h + 1) * hidden_n : (2 * h + 2) * hidden_n] = to_up[h].astype(BF16)
            for n, piece in enumerate(split3(value)):
                piece = piece.astype(F32)
                by_split = jnp.where(lane == 3 * h + n, piece, by_split)
                if n < 2:
                    by_expert = jnp.where(lane == (n * pack + h) * exp_n + expert, piece, by_expert)
        columns[...] = by_split.astype(BF16)
        by_expert = by_expert.astype(BF16)
        router_v[...] = router_rows(router_ref, pack, 2, LANES)
        for j, chunk in enumerate(chunks):
            for copy in chunk:
                copy.wait()
            now = slice(j * width, (j + 1) * width)
            put_blocks((mm(delta_ref[...], side[now, :], LAST) + mm(by_expert, router_v[:, now])).astype(BF16), out_v, now)
            if j + 1 < STEPS:
                now = pl.ds(j * width, width)
                leaving.append(pltpu.make_async_copy(out_v.at[:, :, now], out_ref.at[:, :, now], out_sems.at[j]))
                leaving[-1].start()

        here = lax.axis_index("seq")
        x_copy.wait()
        told = mm(columns[...], x_v[...], ROWS)
        sub = lax.broadcasted_iota(jnp.int32, (group, LANES), 0)
        lane = lax.broadcasted_iota(jnp.int32, (group, LANES), 1)
        minus = jnp.broadcast_to(-jnp.sum(score, axis=0, keepdims=True), (group, LANES))
        pieces = [piece.astype(F32) for piece in split3(minus)]
        threshold_row = jnp.zeros((group, LANES), F32)
        for n, piece in enumerate(pieces):
            threshold_row = jnp.where(lane == n, piece, threshold_row)
        for owner in range(seq_n * exp_n):
            h, first = divmod(owner * per, part)
            shift = first % LANES
            value = jnp.sum(told[3 * h : 3 * h + 3, first - shift : first - shift + LANES], axis=0, keepdims=True)
            value = jnp.broadcast_to(value, (group, LANES))
            if shift:
                value = pltpu.roll(value, LANES - shift, 1)
            if per < LANES:
                value = jnp.where(lane < per, value, 0.0)
            d, place = divmod(owner, exp_n)
            for t in range(extra // LANES):
                row = sub + t * group
                now = slice(part + t * LANES, part + (t + 1) * LANES)
                out_v[d, place * group : (place + 1) * group, now] = jnp.where(
                    row == 2 * here, value, jnp.where(row == 2 * here + 1, threshold_row, 0.0)
                ).astype(BF16)
        now = pl.ds((STEPS - 1) * width, width + extra)
        leaving.append(pltpu.make_async_copy(out_v.at[:, :, now], out_ref.at[:, :, now], out_sems.at[STEPS - 1]))
        leaving[-1].start()
        for copy in leaving:
            copy.wait()

    return pl.pallas_call(
        body,
        in_specs=[ANYWHERE] * (n_blocks + 5) + [IN_VMEM] * 2,
        out_specs=[ANYWHERE] * 2 + [IN_VMEM],
        out_shape=[
            shape((rows, part)),
            shape((seq_n, block_rows, part + extra)),
            shape((rows, total)),
        ],
        scratch_shapes=[
            pltpu.VMEM((rows, part), BF16),
            pltpu.VMEM((rows, part), BF16),
            pltpu.VMEM(pre.shape, F32),
            pltpu.VMEM((seq_n, block_rows, part + extra), BF16),
            pltpu.VMEM((part, total), BF16),
            pltpu.VMEM((pack * hidden_n, part), BF16),
            pltpu.VMEM((rows, LANES), BF16),
            pltpu.VMEM((LANES, part), BF16),
            pltpu.SemaphoreType.DMA((seq_n,)),
            pltpu.SemaphoreType.DMA((2,)),
            pltpu.SemaphoreType.DMA((STEPS, 2 * pack)),
            pltpu.SemaphoreType.DMA((pack,)),
            pltpu.SemaphoreType.DMA((STEPS + 1,)),
        ],
        compiler_params=PARAMS,
        cost_estimate=cost(100 * rows * part * pack * hidden_n, 100 * part * pack * hidden_n),
    )(*to_hbm(*arrivals.blocks, w_gate, w_up, w_down, x, pre), router_t, hid_scale)


def side_grads(x, delta, pack, hidden_n):
    rows, part = x.shape
    width = part // STEPS

    def body(x_ref, delta_ref, gate_out, up_out):
        for h in range(pack):
            both = mm(x_ref[...], delta_ref[:, 2 * h * hidden_n : 2 * (h + 1) * hidden_n], ROWS)
            gate_out[h] = both[:, :hidden_n]
            up_out[h] = both[:, hidden_n:]

    tall = pl.BlockSpec((pack, width, hidden_n), lambda i: (0, i, 0))
    gate, up = pl.pallas_call(
        body,
        grid=(STEPS,),
        in_specs=[
            pl.BlockSpec((rows, width), lambda i: (0, i)),
            pl.BlockSpec(delta.shape, lambda i: (0, 0)),
        ],
        out_specs=[tall, tall],
        out_shape=[shape((pack, part, hidden_n), F32)] * 2,
        compiler_params=PARAMS,
        cost_estimate=cost(4 * rows * part * pack * hidden_n, 8 * part * pack * hidden_n),
    )(*to_hbm(x, delta))
    return gate.reshape(1, part * pack, hidden_n), up.reshape(1, part * pack, hidden_n)


def down_grads(c, hidden, pack, hidden_n):
    rows, part = c.shape
    width = part // 2

    def body(c_ref, hidden_ref, out):
        out[...] = mm(hidden_ref[...], c_ref[...], ROWS)

    return pl.pallas_call(
        body,
        grid=(pack, 2),
        in_specs=[
            pl.BlockSpec((rows, width), lambda h, i: (0, i)),
            pl.BlockSpec((rows, hidden_n), lambda h, i: (0, h)),
        ],
        out_specs=pl.BlockSpec((None, hidden_n, width), lambda h, i: (0, 0, h * 2 + i)),
        out_shape=shape((1, hidden_n, part * pack), F32),
        compiler_params=PARAMS,
        cost_estimate=cost(2 * rows * part * pack * hidden_n, 4 * part * pack * hidden_n),
    )(*to_hbm(c, hidden))


def up_line(block, n, first=0, last=None):
    last = n - 1 if last is None else last
    return lax.ppermute(block, "seq", [(s, s + 1) for s in range(first, last)])


def down_line(block, n, first=1, last=None):
    last = n if last is None else last
    return lax.ppermute(block, "seq", [(s, s - 1) for s in range(first, last)])


def line_gather(block, n):
    ups, downs = [], []
    up = down = block
    for j in range(1, n):
        up = up_line(up, n, j - 1)
        down = down_line(down, n, 1, n - j + 1)
        ups.append(up)
        downs.append(down)
    plan = [(0, 0, 0)] + [(k, 2 * n - 1 - k, k) for k in range(1, n)]
    return Arrivals([block] + ups + downs, plan)


def on_device(tokens, cotangent, router, threshold, w_gate, w_up, w_down, hid_scale, picks, counts):
    experts, slots = picks.shape[1:]
    features = tokens.shape[1]
    true_hidden = w_gate.shape[2]
    extra = -true_hidden % LANES
    if extra:
        w_gate, w_up = (jnp.pad(w, ((0, 0), (0, 0), (0, extra))) for w in (w_gate, w_up))
        w_down = jnp.pad(w_down, ((0, 0), (0, extra), (0, 0)))
        hid_scale = jnp.pad(hid_scale, ((0, 0), (0, extra)))
    hidden_n = true_hidden + extra
    seq_n = lax.axis_size("seq")
    exp_n = lax.axis_size("exp")
    everyone = seq_n * exp_n
    pack = max(1, 8 // slots)
    chosen = picks[0].T

    def to_owners(parts):
        parts = parts.reshape(everyone, -1, parts.shape[2])
        return lax.all_to_all(parts, BOTH, split_axis=0, concat_axis=0, tiled=True).reshape(-1, parts.shape[2])

    sent, hot = choose_rows(tokens, cotangent, chosen, counts, pack)
    sent = sent.reshape(experts, 2, -1, sent.shape[1])
    here = lax.all_to_all(sent, "exp", split_axis=0, concat_axis=0, tiled=True)
    x_in, c_in = (line_gather(here[:, n].reshape(-1, here.shape[3]), seq_n) for n in range(2))
    router_t = router.T

    x, out, pre, hidden = expert_forward(
        x_in, seq_n, slots, experts, pack, router_t, threshold, w_gate, w_up, w_down, hid_scale
    )
    out = to_owners(out)
    c, back, delta = expert_backward(
        c_in, seq_n, exp_n, slots, pack, x, pre, router_t, w_gate, w_up, w_down, hid_scale
    )
    back, out = lax.optimization_barrier((back, out))
    back = to_owners(back)
    down_grad = down_grads(c, hidden, pack, hidden_n)
    gate_grad, up_grad = side_grads(x, delta, pack, hidden_n)
    (mixture,) = scatter_rows(out, hot, seq_n)
    token_grad, router_grad, threshold_grad = scatter_rows(back, hot, seq_n, (features // everyone, experts))
    if extra:
        gate_grad, up_grad = gate_grad[:, :, :true_hidden], up_grad[:, :, :true_hidden]
        down_grad = down_grad[:, :true_hidden]
    return mixture, token_grad, router_grad.T, threshold_grad[0], gate_grad, up_grad, down_grad


def solution(mesh):
    by_owner = P(BOTH, None)
    columns = P("exp", None, "seq")
    down = P("exp", "seq", None)
    return jax.shard_map(
        on_device,
        mesh=mesh,
        in_specs=(
            by_owner,
            by_owner,
            P(),
            P(),
            columns,
            columns,
            down,
            P("exp", "seq"),
            P(BOTH, None, None),
            by_owner,
        ),
        out_specs=(by_owner, by_owner, by_owner, P(), columns, columns, down),
        check_vma=False,
    )
```

```python
import jax
import jax.numpy as jnp
from jax import lax
from jax.experimental import pallas as pl
from jax.experimental.pallas import tpu as pltpu
from jax.sharding import PartitionSpec as P

BOTH = ("seq", "exp")
F32 = jnp.float32
BF16 = jnp.bfloat16
ROWS = ((0,), (0,))
LAST = ((1,), (1,))
STEPS = 4
LANES = 128


def mm(a, b, dims=((1,), (0,))):
    return lax.dot_general(a, b, (dims, ((), ())), preferred_element_type=F32)


PARAMS = pltpu.CompilerParams(vmem_limit_bytes=32 * 2**20)
SMALL = pltpu.CompilerParams(vmem_limit_bytes=12 * 2**20)


def to_hbm(*arrays):
    return [pltpu.with_memory_space_constraint(x, pltpu.HBM) for x in arrays]


def cost(flops, moved):
    return pl.CostEstimate(flops=flops, bytes_accessed=moved, transcendentals=0)


def shape(dims, dtype=BF16):
    return pltpu.HBM(dims, dtype)


ANYWHERE = pl.BlockSpec(memory_space=pl.ANY)
IN_VMEM = pl.BlockSpec(memory_space=pltpu.VMEM)


def choose_rows(tokens, cotangent, picks, counts, pack):
    own, features = tokens.shape
    slots, experts = picks.shape
    group = pack * slots
    count = 2 * experts * group
    part = features // pack
    width = part // STEPS

    def body(picks_ref, counts_ref, c_ref, x_ref, out_ref, hot_ref, picks_s, counts_s, c_v, x_v, out_v, sems, out_sems):
        small = [
            pltpu.make_async_copy(picks_ref, picks_s, sems.at[STEPS, 0]),
            pltpu.make_async_copy(counts_ref, counts_s, sems.at[STEPS, 1]),
        ]
        for copy in small:
            copy.start()
        large = []
        for j in range(STEPS):
            for h in range(pack):
                now = pl.ds(h * part + j * width, width)
                for n, (ref, held) in enumerate(((x_ref, x_v), (c_ref, c_v))):
                    large.append(pltpu.make_async_copy(ref.at[:, now], held.at[:, now], sems.at[j, 2 * h + n]))
        for copy in large:
            copy.start()
        for copy in small:
            copy.wait()
        dims = (count, own)
        row = lax.broadcasted_iota(jnp.int32, dims, 0)
        token = lax.broadcasted_iota(jnp.int32, dims, 1)
        second = (row // group) % 2
        place = (row // (2 * group) * slots + row % slots) * 2 + second
        want = jnp.full(dims, -1, jnp.int32)
        for e in range(experts):
            for k in range(slots):
                index = (e * slots + k) * 2
                want = jnp.where(place == index, picks_s[k, e], want)
                live = jnp.where(k < counts_s[0, e], picks_s[k, e], -1)
                want = jnp.where(place == index + 1, live, want)
        found = (want == token) & (second == 0)
        found_live = (want == token) & (second == 1)
        part_of = (row // slots) % pack
        chosen = [jnp.where(found & (part_of == h), 1.0, 0.0).astype(BF16) for h in range(pack)]
        live = [jnp.where(found_live & (part_of == h), 1.0, 0.0) for h in range(pack)]
        for h in range(pack):
            hot_ref[h] = jnp.concatenate(
                [live[h][(2 * e + 1) * group : (2 * e + 2) * group] for e in range(experts)]
            ).astype(BF16)
        live = [value.astype(BF16) for value in live]
        leaving = []
        for j in range(STEPS):
            for copy in large[2 * pack * j : 2 * pack * (j + 1)]:
                copy.wait()
            total = 0.0
            for h in range(pack):
                now = slice(h * part + j * width, h * part + (j + 1) * width)
                total = total + mm(chosen[h], x_v[:, now]) + mm(live[h], c_v[:, now])
            out_v[:, j * width : (j + 1) * width] = total.astype(BF16)
            now = pl.ds(j * width, width)
            leaving.append(pltpu.make_async_copy(out_v.at[:, now], out_ref.at[:, now], out_sems.at[j]))
            leaving[-1].start()
        for copy in leaving:
            copy.wait()

    return pl.pallas_call(
        body,
        in_specs=[ANYWHERE] * 4,
        out_specs=[ANYWHERE, IN_VMEM],
        out_shape=[shape((count, part)), shape((pack, count // 2, own))],
        scratch_shapes=[
            pltpu.SMEM(picks.shape, jnp.int32),
            pltpu.SMEM(counts.shape, jnp.int32),
            pltpu.VMEM(tokens.shape, BF16),
            pltpu.VMEM(tokens.shape, BF16),
            pltpu.VMEM((count, part), BF16),
            pltpu.SemaphoreType.DMA((STEPS + 1, 2 * pack)),
            pltpu.SemaphoreType.DMA((STEPS,)),
        ],
        compiler_params=PARAMS,
        cost_estimate=cost(4 * count * own * features, 4 * features * own),
    )(*to_hbm(picks, counts, cotangent, tokens))


def scatter_rows(back, hot, seq_n, message=None):
    pack, count, own = hot.shape
    rows = back.shape[0]
    extra = 0 if message is None else riding(seq_n, count // message[1])
    part = back.shape[1] - extra
    width = part // STEPS

    def body(hot_ref, back_ref, *refs):
        hot_v, back_v, out_v, hot_sem, in_sems, out_sems = refs[-6:]
        out_ref = refs[0]
        hot_copy = pltpu.make_async_copy(hot_ref, hot_v, hot_sem)
        hot_copy.start()
        arriving = []
        for i in range(STEPS):
            now = pl.ds(i * width, width + (extra if i + 1 == STEPS else 0))
            arriving.append(pltpu.make_async_copy(back_ref.at[:, now], back_v.at[:, now], in_sems.at[i]))
            arriving[-1].start()
        hot_copy.wait()
        choosers = [jnp.concatenate([hot_v[h]] * seq_n, axis=0) for h in range(pack)]
        leaving = []
        for i in range(STEPS):
            arriving[i].wait()
            for h in range(pack):
                first = h * part + i * width
                rows_now = back_v[:, i * width : (i + 1) * width]
                out_v[:, first : first + width] = mm(choosers[h], rows_now, ROWS).astype(BF16)
                now = pl.ds(first, width)
                leaving.append(pltpu.make_async_copy(out_v.at[:, now], out_ref.at[:, now], out_sems.at[h, i]))
                leaving[-1].start()
        if message is not None:
            router_ref, total_ref = refs[1], refs[2]
            experts, per = router_ref.shape
            group = count // experts
            row = lax.broadcasted_iota(jnp.int32, (rows, experts), 0)
            expert = lax.broadcasted_iota(jnp.int32, (rows, experts), 1)
            mine = row % count // group == expert
            even = jnp.where(mine & (row % 2 == 0), 1.0, 0.0).astype(BF16)
            odd = jnp.where(mine & (row % 2 == 1), 1.0, 0.0).astype(BF16)
            rides = [back_v[:, part + t * LANES : part + (t + 1) * LANES] for t in range(extra // LANES)]
            router = sum(mm(even, ride, ROWS) for ride in rides)
            total = sum(mm(ride, odd, ROWS) for ride in rides)
            router_ref[...] = router[:, :per]
            total_ref[...] = jnp.sum(total[:3], axis=0, keepdims=True)
        for copy in leaving:
            copy.wait()

    out_specs = [ANYWHERE]
    out_shape = [shape((own, part * pack))]
    if message is not None:
        per, experts = message
        out_specs += [IN_VMEM] * 2
        out_shape += [shape((experts, per), F32), shape((1, experts), F32)]
    return pl.pallas_call(
        body,
        in_specs=[ANYWHERE] * 2,
        out_specs=out_specs,
        out_shape=out_shape,
        scratch_shapes=[
            pltpu.VMEM(hot.shape, BF16),
            pltpu.VMEM(back.shape, BF16),
            pltpu.VMEM((own, part * pack), BF16),
            pltpu.SemaphoreType.DMA,
            pltpu.SemaphoreType.DMA((STEPS,)),
            pltpu.SemaphoreType.DMA((pack, STEPS)),
        ],
        compiler_params=SMALL,
        cost_estimate=cost(2 * rows * own * part * pack, 2 * part * pack * own),
    )(*to_hbm(hot), back)


def first_part(rows, pack, slots):
    return (lax.broadcasted_iota(jnp.int32, (rows, 1), 0) // slots) % pack == 0


def fold(parts, slots):
    rows = parts[0].shape[0]
    total = parts[0]
    for h in range(1, len(parts)):
        total = total + pltpu.roll(parts[h], rows - h * slots, 0)
    return total


def spread(value, pack, slots):
    return [value if h == 0 else pltpu.roll(value, h * slots, 0) for h in range(pack)]


class Arrivals:
    def __init__(self, blocks, plan):
        self.blocks, self.plan = blocks, plan

    def start(self, refs, places, sems):
        here = lax.axis_index("seq")
        for k, (a, b, t) in enumerate(self.plan):
            if a == b:
                pltpu.make_async_copy(refs[a], places[k], sems.at[k]).start()
            else:

                @pl.when(here >= t)
                def _():
                    pltpu.make_async_copy(refs[a], places[k], sems.at[k]).start()

                @pl.when(here < t)
                def _():
                    pltpu.make_async_copy(refs[b], places[k], sems.at[k]).start()

    def wait(self, refs, places, sems):
        for k, (a, _, _) in enumerate(self.plan):
            pltpu.make_async_copy(refs[a], places[k], sems.at[k]).wait()


def router_rows(ref, pack, copies, rows):
    part = ref.shape[1] // pack
    wide = ref[...].astype(F32)
    pieces = [wide[:, h * part : (h + 1) * part] for h in range(pack)] * copies
    left = rows - len(pieces) * ref.shape[0]
    if left:
        pieces.append(jnp.zeros((left, part), F32))
    return jnp.concatenate(pieces).astype(BF16)


def side_copies(gate_ref, up_ref, side, sems, pack, j, width):
    part = side.shape[0]
    hidden_n = gate_ref.shape[2]
    rows = pl.ds(j * width, width)
    copies = []
    for h in range(pack):
        for n, ref in enumerate((gate_ref, up_ref)):
            columns = pl.ds((2 * h + n) * hidden_n, hidden_n)
            copies.append((ref.at[0, pl.ds(h * part + j * width, width), :], side.at[rows, columns]))
    return [pltpu.make_async_copy(a, b, sems.at[j, n]) for n, (a, b) in enumerate(copies)]


def down_copies(down_ref, stack, sems, pack):
    hidden_n = down_ref.shape[1]
    part = stack.shape[1]
    return [
        pltpu.make_async_copy(
            down_ref.at[0, :, pl.ds(h * part, part)], stack.at[pl.ds(h * hidden_n, hidden_n), :], sems.at[h]
        )
        for h in range(pack)
    ]


def put_blocks(out, target, columns):
    seq_n, rows, _ = target.shape
    here = lax.axis_index("seq")
    for k in range(seq_n):
        target[lax.rem(here - k + seq_n, seq_n), :, columns] = out[k * rows : (k + 1) * rows]


def expert_forward(arrivals, seq_n, slots, experts, pack, router_t, threshold, w_gate, w_up, w_down, hid_scale):
    block_rows, part = arrivals.blocks[0].shape
    rows = block_rows * seq_n
    hidden_n = w_gate.shape[2]
    both = 2 * hidden_n
    width = part // STEPS
    total = pack * both
    n_blocks = len(arrivals.blocks)

    def body(*refs):
        blocks = refs[:n_blocks]
        gate_ref, up_ref, down_ref, router_ref, threshold_ref, scale_ref = refs[n_blocks : n_blocks + 6]
        x_ref, out_ref, pre_ref, hidden_ref = refs[n_blocks + 6 : n_blocks + 10]
        pre_v, hidden_v, x_v, out_v, side, stack, x_sems, side_sems, stack_sems, out_sems = refs[n_blocks + 10 :]
        places = [x_v.at[pl.ds(k * block_rows, block_rows), :] for k in range(seq_n)]
        arrivals.start(blocks, places, x_sems)
        chunks = [side_copies(gate_ref, up_ref, side, side_sems, pack, j, width) for j in range(STEPS)]
        downs = down_copies(down_ref, stack, stack_sems, pack)
        for copy in sum(chunks, []) + downs:
            copy.start()
        arrivals.wait(blocks, places, x_sems)
        leaving = [pltpu.make_async_copy(x_v, x_ref, out_sems.at[STEPS])]
        leaving[0].start()
        sums = [0.0] * pack
        scores = mm(x_v[...], router_rows(router_ref, pack, 1, pack * experts), LAST)
        for j, chunk in enumerate(chunks):
            for copy in chunk:
                copy.wait()
            now = slice(j * width, (j + 1) * width)
            for n in range(pack):
                sums[n] = sums[n] + mm(x_v[:, now], side[now, n * both : (n + 1) * both])
        gate = fold([y[:, :hidden_n] for y in sums], slots)
        up = fold([y[:, hidden_n:] for y in sums], slots)
        lane = lax.broadcasted_iota(jnp.int32, scores.shape, 1)
        expert = lax.axis_index("exp")
        score = fold([jnp.where(lane == h * experts + expert, scores, 0.0) for h in range(pack)], slots)
        lane = lax.broadcasted_iota(jnp.int32, threshold_ref.shape, 1)
        cut = jnp.sum(jnp.where(lane == expert, threshold_ref[...], 0.0), axis=1, keepdims=True)
        g = jax.nn.sigmoid(jnp.sum(score, axis=1, keepdims=True) - cut)
        hidden = gate * jax.nn.sigmoid(gate) * up * scale_ref[...] * g
        hidden = jnp.where(first_part(rows, pack, slots), hidden, 0.0)
        for h, value in enumerate(spread(hidden, pack, slots)):
            now = slice(h * hidden_n, (h + 1) * hidden_n)
            hidden_v[:, now] = value.astype(BF16)
        pre_v[:, :hidden_n] = gate
        pre_v[:, hidden_n:both] = up
        pre_v[:, both:] = jnp.broadcast_to(g, (rows, LANES))
        leaving.append(pltpu.make_async_copy(pre_v, pre_ref, out_sems.at[STEPS + 1]))
        leaving.append(pltpu.make_async_copy(hidden_v, hidden_ref, out_sems.at[STEPS + 2]))
        for copy in leaving[1:]:
            copy.start()
        for copy in downs:
            copy.wait()
        for j in range(STEPS):
            now = slice(j * width, (j + 1) * width)
            put_blocks(mm(hidden_v[...], stack[:, now]).astype(BF16), out_v, now)
            columns = pl.ds(j * width, width)
            leaving.append(pltpu.make_async_copy(out_v.at[:, :, columns], out_ref.at[:, :, columns], out_sems.at[j]))
            leaving[-1].start()
        for copy in leaving:
            copy.wait()

    return pl.pallas_call(
        body,
        in_specs=[ANYWHERE] * (n_blocks + 3) + [IN_VMEM] * 3,
        out_specs=[ANYWHERE] * 4,
        out_shape=[
            shape((rows, part)),
            shape((seq_n, block_rows, part)),
            shape((rows, both + LANES), F32),
            shape((rows, pack * hidden_n)),
        ],
        scratch_shapes=[
            pltpu.VMEM((rows, both + LANES), F32),
            pltpu.VMEM((rows, pack * hidden_n), BF16),
            pltpu.VMEM((rows, part), BF16),
            pltpu.VMEM((seq_n, block_rows, part), BF16),
            pltpu.VMEM((part, total), BF16),
            pltpu.VMEM((pack * hidden_n, part), BF16),
            pltpu.SemaphoreType.DMA((seq_n,)),
            pltpu.SemaphoreType.DMA((STEPS, 2 * pack)),
            pltpu.SemaphoreType.DMA((pack,)),
            pltpu.SemaphoreType.DMA((STEPS + 3,)),
        ],
        compiler_params=PARAMS,
        cost_estimate=cost(6 * rows * part * pack * hidden_n, 12 * part * pack * hidden_n),
    )(
        *to_hbm(*arrivals.blocks),
        w_gate,
        *to_hbm(w_up, w_down),
        router_t,
        threshold.reshape(1, -1),
        hid_scale,
    )


def split3(v):
    hi = v.astype(BF16)
    rest = v - hi.astype(F32)
    mid = rest.astype(BF16)
    return hi, mid, (rest - mid.astype(F32)).astype(BF16)


def riding(seq_n, group):
    return LANES * -(-2 * seq_n // group)


def expert_backward(arrivals, seq_n, exp_n, slots, pack, x, pre, router_t, w_gate, w_up, w_down, hid_scale):
    block_rows, part = arrivals.blocks[0].shape
    rows = block_rows * seq_n
    hidden_n = w_gate.shape[2]
    width = part // STEPS
    total = 2 * pack * hidden_n
    group = pack * slots
    extra = riding(seq_n, group)
    per = part * pack // (seq_n * exp_n)
    n_blocks = len(arrivals.blocks)

    def body(*refs):
        blocks = refs[:n_blocks]
        gate_ref, up_ref, down_ref, x_ref, pre_ref, router_ref, scale_ref = refs[n_blocks : n_blocks + 7]
        c_ref, out_ref, delta_ref = refs[n_blocks + 7 : n_blocks + 10]
        c_v, x_v, pre_v, out_v, side, stack, columns, router_v, c_sems, x_sems, side_sems, stack_sems, out_sems = refs[
            n_blocks + 10 :
        ]
        places = [c_v.at[pl.ds(k * block_rows, block_rows), :] for k in range(seq_n)]
        arrivals.start(blocks, places, c_sems)
        chunks = [side_copies(gate_ref, up_ref, side, side_sems, pack, j, width) for j in range(STEPS)]
        downs = down_copies(down_ref, stack, stack_sems, pack)
        x_copy = pltpu.make_async_copy(x_ref, x_v, x_sems.at[0])
        pre_copy = pltpu.make_async_copy(pre_ref, pre_v, x_sems.at[1])
        for copy in downs + [pre_copy] + sum(chunks, []) + [x_copy]:
            copy.start()
        arrivals.wait(blocks, places, c_sems)
        leaving = [pltpu.make_async_copy(c_v, c_ref, out_sems.at[STEPS])]
        leaving[0].start()
        for copy in downs:
            copy.wait()
        both = mm(c_v[...], stack[...], LAST)
        parts = [both[:, h * hidden_n : (h + 1) * hidden_n] for h in range(pack)]
        pre_copy.wait()
        raw = jnp.where(first_part(rows, pack, slots), fold(parts, slots) * scale_ref[...], 0.0)
        gate = pre_v[:, :hidden_n]
        up = pre_v[:, hidden_n : 2 * hidden_n]
        g = pre_v[:, 2 * hidden_n : 2 * hidden_n + 1]
        sig = jax.nn.sigmoid(gate)
        act = gate * sig
        score = jnp.sum(act * up * raw, axis=1, keepdims=True) * g * (1.0 - g)
        grad = raw * g
        to_gate = spread(grad * up * sig * (1.0 + gate * (1.0 - sig)), pack, slots)
        to_up = spread(grad * act, pack, slots)
        expert = lax.axis_index("exp")
        lane = lax.broadcasted_iota(jnp.int32, (rows, LANES), 1)
        by_expert = jnp.zeros((rows, LANES), F32)
        by_split = jnp.zeros((rows, LANES), F32)
        for h, value in enumerate(spread(jnp.broadcast_to(score, (rows, LANES)), pack, slots)):
            delta_ref[:, 2 * h * hidden_n : (2 * h + 1) * hidden_n] = to_gate[h].astype(BF16)
            delta_ref[:, (2 * h + 1) * hidden_n : (2 * h + 2) * hidden_n] = to_up[h].astype(BF16)
            for n, piece in enumerate(split3(value)):
                piece = piece.astype(F32)
                by_split = jnp.where(lane == 3 * h + n, piece, by_split)
                if n < 2:
                    by_expert = jnp.where(lane == (n * pack + h) * exp_n + expert, piece, by_expert)
        columns[...] = by_split.astype(BF16)
        by_expert = by_expert.astype(BF16)
        router_v[...] = router_rows(router_ref, pack, 2, LANES)
        for j, chunk in enumerate(chunks):
            for copy in chunk:
                copy.wait()
            now = slice(j * width, (j + 1) * width)
            put_blocks((mm(delta_ref[...], side[now, :], LAST) + mm(by_expert, router_v[:, now])).astype(BF16), out_v, now)
            if j + 1 < STEPS:
                now = pl.ds(j * width, width)
                leaving.append(pltpu.make_async_copy(out_v.at[:, :, now], out_ref.at[:, :, now], out_sems.at[j]))
                leaving[-1].start()

        here = lax.axis_index("seq")
        x_copy.wait()
        told = mm(columns[...], x_v[...], ROWS)
        sub = lax.broadcasted_iota(jnp.int32, (group, LANES), 0)
        lane = lax.broadcasted_iota(jnp.int32, (group, LANES), 1)
        minus = jnp.broadcast_to(-jnp.sum(score, axis=0, keepdims=True), (group, LANES))
        pieces = [piece.astype(F32) for piece in split3(minus)]
        threshold_row = jnp.zeros((group, LANES), F32)
        for n, piece in enumerate(pieces):
            threshold_row = jnp.where(lane == n, piece, threshold_row)
        for owner in range(seq_n * exp_n):
            h, first = divmod(owner * per, part)
            shift = first % LANES
            value = jnp.sum(told[3 * h : 3 * h + 3, first - shift : first - shift + LANES], axis=0, keepdims=True)
            value = jnp.broadcast_to(value, (group, LANES))
            if shift:
                value = pltpu.roll(value, LANES - shift, 1)
            if per < LANES:
                value = jnp.where(lane < per, value, 0.0)
            d, place = divmod(owner, exp_n)
            for t in range(extra // LANES):
                row = sub + t * group
                now = slice(part + t * LANES, part + (t + 1) * LANES)
                out_v[d, place * group : (place + 1) * group, now] = jnp.where(
                    row == 2 * here, value, jnp.where(row == 2 * here + 1, threshold_row, 0.0)
                ).astype(BF16)
        now = pl.ds((STEPS - 1) * width, width + extra)
        leaving.append(pltpu.make_async_copy(out_v.at[:, :, now], out_ref.at[:, :, now], out_sems.at[STEPS - 1]))
        leaving[-1].start()
        for copy in leaving:
            copy.wait()

    return pl.pallas_call(
        body,
        in_specs=[ANYWHERE] * (n_blocks + 5) + [IN_VMEM] * 2,
        out_specs=[ANYWHERE] * 2 + [IN_VMEM],
        out_shape=[
            shape((rows, part)),
            shape((seq_n, block_rows, part + extra)),
            shape((rows, total)),
        ],
        scratch_shapes=[
            pltpu.VMEM((rows, part), BF16),
            pltpu.VMEM((rows, part), BF16),
            pltpu.VMEM(pre.shape, F32),
            pltpu.VMEM((seq_n, block_rows, part + extra), BF16),
            pltpu.VMEM((part, total), BF16),
            pltpu.VMEM((pack * hidden_n, part), BF16),
            pltpu.VMEM((rows, LANES), BF16),
            pltpu.VMEM((LANES, part), BF16),
            pltpu.SemaphoreType.DMA((seq_n,)),
            pltpu.SemaphoreType.DMA((2,)),
            pltpu.SemaphoreType.DMA((STEPS, 2 * pack)),
            pltpu.SemaphoreType.DMA((pack,)),
            pltpu.SemaphoreType.DMA((STEPS + 1,)),
        ],
        compiler_params=PARAMS,
        cost_estimate=cost(100 * rows * part * pack * hidden_n, 100 * part * pack * hidden_n),
    )(*to_hbm(*arrivals.blocks, w_gate, w_up, w_down, x, pre), router_t, hid_scale)


def side_grads(x, delta, pack, hidden_n):
    rows, part = x.shape
    width = part // STEPS

    def body(x_ref, delta_ref, gate_out, up_out):
        for h in range(pack):
            both = mm(x_ref[...], delta_ref[:, 2 * h * hidden_n : 2 * (h + 1) * hidden_n], ROWS)
            gate_out[h] = both[:, :hidden_n]
            up_out[h] = both[:, hidden_n:]

    tall = pl.BlockSpec((pack, width, hidden_n), lambda i: (0, i, 0))
    gate, up = pl.pallas_call(
        body,
        grid=(STEPS,),
        in_specs=[
            pl.BlockSpec((rows, width), lambda i: (0, i)),
            pl.BlockSpec(delta.shape, lambda i: (0, 0)),
        ],
        out_specs=[tall, tall],
        out_shape=[shape((pack, part, hidden_n), F32)] * 2,
        compiler_params=PARAMS,
        cost_estimate=cost(4 * rows * part * pack * hidden_n, 8 * part * pack * hidden_n),
    )(*to_hbm(x, delta))
    return gate.reshape(1, part * pack, hidden_n), up.reshape(1, part * pack, hidden_n)


def down_grads(c, hidden, pack, hidden_n):
    rows, part = c.shape
    width = part // 2

    def body(c_ref, hidden_ref, out):
        out[...] = mm(hidden_ref[...], c_ref[...], ROWS)

    return pl.pallas_call(
        body,
        grid=(pack, 2),
        in_specs=[
            pl.BlockSpec((rows, width), lambda h, i: (0, i)),
            pl.BlockSpec((rows, hidden_n), lambda h, i: (0, h)),
        ],
        out_specs=pl.BlockSpec((None, hidden_n, width), lambda h, i: (0, 0, h * 2 + i)),
        out_shape=shape((1, hidden_n, part * pack), F32),
        compiler_params=PARAMS,
        cost_estimate=cost(2 * rows * part * pack * hidden_n, 4 * part * pack * hidden_n),
    )(*to_hbm(c, hidden))


def up_line(block, n, first=0, last=None):
    last = n - 1 if last is None else last
    return lax.ppermute(block, "seq", [(s, s + 1) for s in range(first, last)])


def down_line(block, n, first=1, last=None):
    last = n if last is None else last
    return lax.ppermute(block, "seq", [(s, s - 1) for s in range(first, last)])


def line_gather(block, n, hold=()):
    ups, downs = [], []
    up = down = block
    for j in range(1, n):
        if hold and j == n - 1:
            up, down = lax.optimization_barrier((up, down, *hold))[:2]
        up = up_line(up, n, j - 1)
        down = down_line(down, n, 1, n - j + 1)
        ups.append(up)
        downs.append(down)
    plan = [(0, 0, 0)] + [(k, 2 * n - 1 - k, k) for k in range(1, n)]
    return Arrivals([block] + ups + downs, plan)


def on_device(tokens, cotangent, router, threshold, w_gate, w_up, w_down, hid_scale, picks, counts):
    experts, slots = picks.shape[1:]
    features = tokens.shape[1]
    true_hidden = w_gate.shape[2]
    extra = -true_hidden % LANES
    if extra:
        w_gate, w_up = (jnp.pad(w, ((0, 0), (0, 0), (0, extra))) for w in (w_gate, w_up))
        w_down = jnp.pad(w_down, ((0, 0), (0, extra), (0, 0)))
        hid_scale = jnp.pad(hid_scale, ((0, 0), (0, extra)))
    hidden_n = true_hidden + extra
    seq_n = lax.axis_size("seq")
    exp_n = lax.axis_size("exp")
    everyone = seq_n * exp_n
    pack = max(1, 8 // slots)
    chosen = picks[0].T

    def to_owners(parts):
        parts = parts.reshape(everyone, -1, parts.shape[2])
        return lax.all_to_all(parts, BOTH, split_axis=0, concat_axis=0, tiled=True).reshape(-1, parts.shape[2])

    sent, hot = choose_rows(tokens, cotangent, chosen, counts, pack)
    sent = sent.reshape(experts, 2, -1, sent.shape[1])
    here = lax.all_to_all(sent, "exp", split_axis=0, concat_axis=0, tiled=True)
    x_rows, c_rows = (here[:, n].reshape(-1, here.shape[3]) for n in range(2))
    x_in = line_gather(x_rows, seq_n)
    c_in = line_gather(c_rows, seq_n, (x_in.blocks[seq_n - 1], x_in.blocks[-1]))
    router_t = router.T

    x, out, pre, hidden = expert_forward(
        x_in, seq_n, slots, experts, pack, router_t, threshold, w_gate, w_up, w_down, hid_scale
    )
    out = to_owners(out)
    c, back, delta = expert_backward(
        c_in, seq_n, exp_n, slots, pack, x, pre, router_t, w_gate, w_up, w_down, hid_scale
    )
    back, out = lax.optimization_barrier((back, out))
    back = to_owners(back)
    down_grad = down_grads(c, hidden, pack, hidden_n)
    gate_grad, up_grad = side_grads(x, delta, pack, hidden_n)
    (mixture,) = scatter_rows(out, hot, seq_n)
    token_grad, router_grad, threshold_grad = scatter_rows(back, hot, seq_n, (features // everyone, experts))
    if extra:
        gate_grad, up_grad = gate_grad[:, :, :true_hidden], up_grad[:, :, :true_hidden]
        down_grad = down_grad[:, :true_hidden]
    return mixture, token_grad, router_grad.T, threshold_grad[0], gate_grad, up_grad, down_grad


def solution(mesh):
    by_owner = P(BOTH, None)
    columns = P("exp", None, "seq")
    down = P("exp", "seq", None)
    return jax.shard_map(
        on_device,
        mesh=mesh,
        in_specs=(
            by_owner,
            by_owner,
            P(),
            P(),
            columns,
            columns,
            down,
            P("exp", "seq"),
            P(BOTH, None, None),
            by_owner,
        ),
        out_specs=(by_owner, by_owner, by_owner, P(), columns, columns, down),
        check_vma=False,
    )
```

```python
import jax
import jax.numpy as jnp
from jax import lax
from jax.experimental import pallas as pl
from jax.experimental.pallas import tpu as pltpu
from jax.sharding import PartitionSpec as P

BOTH = ("seq", "exp")
F32 = jnp.float32
BF16 = jnp.bfloat16
ROWS = ((0,), (0,))
LAST = ((1,), (1,))
STEPS = 4
LANES = 128


def mm(a, b, dims=((1,), (0,))):
    return lax.dot_general(a, b, (dims, ((), ())), preferred_element_type=F32)


PARAMS = pltpu.CompilerParams(vmem_limit_bytes=32 * 2**20)
SMALL = pltpu.CompilerParams(vmem_limit_bytes=12 * 2**20)


def to_hbm(*arrays):
    return [pltpu.with_memory_space_constraint(x, pltpu.HBM) for x in arrays]


def cost(flops, moved):
    return pl.CostEstimate(flops=flops, bytes_accessed=moved, transcendentals=0)


def shape(dims, dtype=BF16):
    return pltpu.HBM(dims, dtype)


ANYWHERE = pl.BlockSpec(memory_space=pl.ANY)
IN_VMEM = pl.BlockSpec(memory_space=pltpu.VMEM)


def choose_rows(tokens, cotangent, picks, counts, pack):
    own, features = tokens.shape
    slots, experts = picks.shape
    group = pack * slots
    count = 2 * experts * group
    part = features // pack
    width = part // STEPS

    def body(picks_ref, counts_ref, c_ref, x_ref, out_ref, hot_ref, picks_s, counts_s, c_v, x_v, out_v, sems, out_sems):
        small = [
            pltpu.make_async_copy(picks_ref, picks_s, sems.at[STEPS, 0]),
            pltpu.make_async_copy(counts_ref, counts_s, sems.at[STEPS, 1]),
        ]
        for copy in small:
            copy.start()
        large = []
        for j in range(STEPS):
            for h in range(pack):
                now = pl.ds(h * part + j * width, width)
                for n, (ref, held) in enumerate(((x_ref, x_v), (c_ref, c_v))):
                    large.append(pltpu.make_async_copy(ref.at[:, now], held.at[:, now], sems.at[j, 2 * h + n]))
        for copy in large:
            copy.start()
        for copy in small:
            copy.wait()
        dims = (count, own)
        row = lax.broadcasted_iota(jnp.int32, dims, 0)
        token = lax.broadcasted_iota(jnp.int32, dims, 1)
        second = (row // group) % 2
        place = (row // (2 * group) * slots + row % slots) * 2 + second
        want = jnp.full(dims, -1, jnp.int32)
        for e in range(experts):
            for k in range(slots):
                index = (e * slots + k) * 2
                want = jnp.where(place == index, picks_s[k, e], want)
                live = jnp.where(k < counts_s[0, e], picks_s[k, e], -1)
                want = jnp.where(place == index + 1, live, want)
        found = (want == token) & (second == 0)
        found_live = (want == token) & (second == 1)
        part_of = (row // slots) % pack
        chosen = [jnp.where(found & (part_of == h), 1.0, 0.0).astype(BF16) for h in range(pack)]
        live = [jnp.where(found_live & (part_of == h), 1.0, 0.0) for h in range(pack)]
        for h in range(pack):
            hot_ref[h] = jnp.concatenate(
                [live[h][(2 * e + 1) * group : (2 * e + 2) * group] for e in range(experts)]
            ).astype(BF16)
        live = [value.astype(BF16) for value in live]
        leaving = []
        for j in range(STEPS):
            for copy in large[2 * pack * j : 2 * pack * (j + 1)]:
                copy.wait()
            total = 0.0
            for h in range(pack):
                now = slice(h * part + j * width, h * part + (j + 1) * width)
                total = total + mm(chosen[h], x_v[:, now]) + mm(live[h], c_v[:, now])
            out_v[:, j * width : (j + 1) * width] = total.astype(BF16)
            now = pl.ds(j * width, width)
            leaving.append(pltpu.make_async_copy(out_v.at[:, now], out_ref.at[:, now], out_sems.at[j]))
            leaving[-1].start()
        for copy in leaving:
            copy.wait()

    return pl.pallas_call(
        body,
        in_specs=[ANYWHERE] * 4,
        out_specs=[ANYWHERE, IN_VMEM],
        out_shape=[shape((count, part)), shape((pack, count // 2, own))],
        scratch_shapes=[
            pltpu.SMEM(picks.shape, jnp.int32),
            pltpu.SMEM(counts.shape, jnp.int32),
            pltpu.VMEM(tokens.shape, BF16),
            pltpu.VMEM(tokens.shape, BF16),
            pltpu.VMEM((count, part), BF16),
            pltpu.SemaphoreType.DMA((STEPS + 1, 2 * pack)),
            pltpu.SemaphoreType.DMA((STEPS,)),
        ],
        compiler_params=PARAMS,
        cost_estimate=cost(4 * count * own * features, 4 * features * own),
    )(*to_hbm(picks, counts, cotangent, tokens))


def scatter_rows(back, hot, seq_n, message=None):
    pack, count, own = hot.shape
    rows = back.shape[0]
    extra = 0 if message is None else riding(seq_n, count // message[1])
    part = back.shape[1] - extra
    width = part // STEPS

    def body(hot_ref, back_ref, *refs):
        hot_v, back_v, out_v, hot_sem, in_sems, out_sems = refs[-6:]
        out_ref = refs[0]
        hot_copy = pltpu.make_async_copy(hot_ref, hot_v, hot_sem)
        hot_copy.start()
        arriving = []
        for i in range(STEPS):
            now = pl.ds(i * width, width + (extra if i + 1 == STEPS else 0))
            arriving.append(pltpu.make_async_copy(back_ref.at[:, now], back_v.at[:, now], in_sems.at[i]))
            arriving[-1].start()
        hot_copy.wait()
        choosers = [jnp.concatenate([hot_v[h]] * seq_n, axis=0) for h in range(pack)]
        leaving = []
        for i in range(STEPS):
            arriving[i].wait()
            for h in range(pack):
                first = h * part + i * width
                rows_now = back_v[:, i * width : (i + 1) * width]
                out_v[:, first : first + width] = mm(choosers[h], rows_now, ROWS).astype(BF16)
                now = pl.ds(first, width)
                leaving.append(pltpu.make_async_copy(out_v.at[:, now], out_ref.at[:, now], out_sems.at[h, i]))
                leaving[-1].start()
        if message is not None:
            router_ref, total_ref = refs[1], refs[2]
            experts, per = router_ref.shape
            group = count // experts
            row = lax.broadcasted_iota(jnp.int32, (rows, experts), 0)
            expert = lax.broadcasted_iota(jnp.int32, (rows, experts), 1)
            mine = row % count // group == expert
            even = jnp.where(mine & (row % 2 == 0), 1.0, 0.0).astype(BF16)
            odd = jnp.where(mine & (row % 2 == 1), 1.0, 0.0).astype(BF16)
            rides = [back_v[:, part + t * LANES : part + (t + 1) * LANES] for t in range(extra // LANES)]
            router = sum(mm(even, ride, ROWS) for ride in rides)
            total = sum(mm(ride, odd, ROWS) for ride in rides)
            router_ref[...] = router[:, :per]
            total_ref[...] = jnp.sum(total[:3], axis=0, keepdims=True)
        for copy in leaving:
            copy.wait()

    out_specs = [ANYWHERE]
    out_shape = [shape((own, part * pack))]
    if message is not None:
        per, experts = message
        out_specs += [IN_VMEM] * 2
        out_shape += [shape((experts, per), F32), shape((1, experts), F32)]
    return pl.pallas_call(
        body,
        in_specs=[ANYWHERE] * 2,
        out_specs=out_specs,
        out_shape=out_shape,
        scratch_shapes=[
            pltpu.VMEM(hot.shape, BF16),
            pltpu.VMEM(back.shape, BF16),
            pltpu.VMEM((own, part * pack), BF16),
            pltpu.SemaphoreType.DMA,
            pltpu.SemaphoreType.DMA((STEPS,)),
            pltpu.SemaphoreType.DMA((pack, STEPS)),
        ],
        compiler_params=SMALL,
        cost_estimate=cost(2 * rows * own * part * pack, 2 * part * pack * own),
    )(*to_hbm(hot), back)


def first_part(rows, pack, slots):
    return (lax.broadcasted_iota(jnp.int32, (rows, 1), 0) // slots) % pack == 0


def fold(parts, slots):
    rows = parts[0].shape[0]
    total = parts[0]
    for h in range(1, len(parts)):
        total = total + pltpu.roll(parts[h], rows - h * slots, 0)
    return total


def spread(value, pack, slots):
    return [value if h == 0 else pltpu.roll(value, h * slots, 0) for h in range(pack)]


class Arrivals:
    def __init__(self, blocks, plan):
        self.blocks, self.plan = blocks, plan

    def start(self, refs, places, sems):
        here = lax.axis_index("seq")
        for k, (a, b, t) in enumerate(self.plan):
            if a == b:
                pltpu.make_async_copy(refs[a], places[k], sems.at[k]).start()
            else:

                @pl.when(here >= t)
                def _():
                    pltpu.make_async_copy(refs[a], places[k], sems.at[k]).start()

                @pl.when(here < t)
                def _():
                    pltpu.make_async_copy(refs[b], places[k], sems.at[k]).start()

    def wait(self, refs, places, sems):
        for k, (a, _, _) in enumerate(self.plan):
            pltpu.make_async_copy(refs[a], places[k], sems.at[k]).wait()


def router_rows(ref, pack, copies, rows):
    part = ref.shape[1] // pack
    wide = ref[...].astype(F32)
    pieces = [wide[:, h * part : (h + 1) * part] for h in range(pack)] * copies
    left = rows - len(pieces) * ref.shape[0]
    if left:
        pieces.append(jnp.zeros((left, part), F32))
    return jnp.concatenate(pieces).astype(BF16)


def side_copies(gate_ref, up_ref, side, sems, pack, j, width):
    part = side.shape[0]
    hidden_n = gate_ref.shape[2]
    rows = pl.ds(j * width, width)
    copies = []
    for h in range(pack):
        for n, ref in enumerate((gate_ref, up_ref)):
            columns = pl.ds((2 * h + n) * hidden_n, hidden_n)
            copies.append((ref.at[0, pl.ds(h * part + j * width, width), :], side.at[rows, columns]))
    return [pltpu.make_async_copy(a, b, sems.at[j, n]) for n, (a, b) in enumerate(copies)]


def down_copies(down_ref, stack, sems, pack):
    hidden_n = down_ref.shape[1]
    part = stack.shape[1]
    return [
        pltpu.make_async_copy(
            down_ref.at[0, :, pl.ds(h * part, part)], stack.at[pl.ds(h * hidden_n, hidden_n), :], sems.at[h]
        )
        for h in range(pack)
    ]


def put_blocks(out, target, columns):
    seq_n, rows, _ = target.shape
    here = lax.axis_index("seq")
    for k in range(seq_n):
        target[lax.rem(here - k + seq_n, seq_n), :, columns] = out[k * rows : (k + 1) * rows]


def expert_forward(arrivals, seq_n, slots, experts, pack, router_t, threshold, w_gate, w_up, w_down, hid_scale):
    block_rows, part = arrivals.blocks[0].shape
    rows = block_rows * seq_n
    hidden_n = w_gate.shape[2]
    both = 2 * hidden_n
    width = part // STEPS
    total = pack * both
    n_blocks = len(arrivals.blocks)

    def body(*refs):
        blocks = refs[:n_blocks]
        gate_ref, up_ref, down_ref, router_ref, threshold_ref, scale_ref = refs[n_blocks : n_blocks + 6]
        x_ref, out_ref, pre_ref, hidden_ref = refs[n_blocks + 6 : n_blocks + 10]
        pre_v, hidden_v, x_v, out_v, side, stack, x_sems, side_sems, stack_sems, out_sems = refs[n_blocks + 10 :]
        places = [x_v.at[pl.ds(k * block_rows, block_rows), :] for k in range(seq_n)]
        arrivals.start(blocks, places, x_sems)
        chunks = [side_copies(gate_ref, up_ref, side, side_sems, pack, j, width) for j in range(STEPS)]
        downs = down_copies(down_ref, stack, stack_sems, pack)
        for copy in sum(chunks, []) + downs:
            copy.start()
        arrivals.wait(blocks, places, x_sems)
        leaving = [pltpu.make_async_copy(x_v, x_ref, out_sems.at[STEPS])]
        leaving[0].start()
        sums = [0.0] * pack
        scores = mm(x_v[...], router_rows(router_ref, pack, 1, pack * experts), LAST)
        for j, chunk in enumerate(chunks):
            for copy in chunk:
                copy.wait()
            now = slice(j * width, (j + 1) * width)
            for n in range(pack):
                sums[n] = sums[n] + mm(x_v[:, now], side[now, n * both : (n + 1) * both])
        gate = fold([y[:, :hidden_n] for y in sums], slots)
        up = fold([y[:, hidden_n:] for y in sums], slots)
        lane = lax.broadcasted_iota(jnp.int32, scores.shape, 1)
        expert = lax.axis_index("exp")
        score = fold([jnp.where(lane == h * experts + expert, scores, 0.0) for h in range(pack)], slots)
        lane = lax.broadcasted_iota(jnp.int32, threshold_ref.shape, 1)
        cut = jnp.sum(jnp.where(lane == expert, threshold_ref[...], 0.0), axis=1, keepdims=True)
        g = jax.nn.sigmoid(jnp.sum(score, axis=1, keepdims=True) - cut)
        hidden = gate * jax.nn.sigmoid(gate) * up * scale_ref[...] * g
        hidden = jnp.where(first_part(rows, pack, slots), hidden, 0.0)
        for h, value in enumerate(spread(hidden, pack, slots)):
            now = slice(h * hidden_n, (h + 1) * hidden_n)
            hidden_v[:, now] = value.astype(BF16)
        pre_v[:, :hidden_n] = gate
        pre_v[:, hidden_n:both] = up
        pre_v[:, both:] = jnp.broadcast_to(g, (rows, LANES))
        leaving.append(pltpu.make_async_copy(pre_v, pre_ref, out_sems.at[STEPS + 1]))
        leaving.append(pltpu.make_async_copy(hidden_v, hidden_ref, out_sems.at[STEPS + 2]))
        for copy in leaving[1:]:
            copy.start()
        for copy in downs:
            copy.wait()
        for j in range(STEPS):
            now = slice(j * width, (j + 1) * width)
            put_blocks(mm(hidden_v[...], stack[:, now]).astype(BF16), out_v, now)
            columns = pl.ds(j * width, width)
            leaving.append(pltpu.make_async_copy(out_v.at[:, :, columns], out_ref.at[:, :, columns], out_sems.at[j]))
            leaving[-1].start()
        for copy in leaving:
            copy.wait()

    return pl.pallas_call(
        body,
        in_specs=[ANYWHERE] * (n_blocks + 3) + [IN_VMEM] * 3,
        out_specs=[ANYWHERE] * 4,
        out_shape=[
            shape((rows, part)),
            shape((seq_n, block_rows, part)),
            shape((rows, both + LANES), F32),
            shape((rows, pack * hidden_n)),
        ],
        scratch_shapes=[
            pltpu.VMEM((rows, both + LANES), F32),
            pltpu.VMEM((rows, pack * hidden_n), BF16),
            pltpu.VMEM((rows, part), BF16),
            pltpu.VMEM((seq_n, block_rows, part), BF16),
            pltpu.VMEM((part, total), BF16),
            pltpu.VMEM((pack * hidden_n, part), BF16),
            pltpu.SemaphoreType.DMA((seq_n,)),
            pltpu.SemaphoreType.DMA((STEPS, 2 * pack)),
            pltpu.SemaphoreType.DMA((pack,)),
            pltpu.SemaphoreType.DMA((STEPS + 3,)),
        ],
        compiler_params=PARAMS,
        cost_estimate=cost(6 * rows * part * pack * hidden_n, 12 * part * pack * hidden_n),
    )(
        *to_hbm(*arrivals.blocks),
        w_gate,
        *to_hbm(w_up, w_down),
        router_t,
        threshold.reshape(1, -1),
        hid_scale,
    )


def split3(v):
    hi = v.astype(BF16)
    rest = v - hi.astype(F32)
    mid = rest.astype(BF16)
    return hi, mid, (rest - mid.astype(F32)).astype(BF16)


def riding(seq_n, group):
    return LANES * -(-2 * seq_n // group)


def expert_backward(arrivals, seq_n, exp_n, slots, pack, x, pre, router_t, w_gate, w_up, w_down, hid_scale):
    block_rows, part = arrivals.blocks[0].shape
    rows = block_rows * seq_n
    hidden_n = w_gate.shape[2]
    width = part // STEPS
    total = 2 * pack * hidden_n
    group = pack * slots
    extra = riding(seq_n, group)
    per = part * pack // (seq_n * exp_n)
    n_blocks = len(arrivals.blocks)

    def body(*refs):
        blocks = refs[:n_blocks]
        gate_ref, up_ref, down_ref, x_ref, pre_ref, router_ref, scale_ref = refs[n_blocks : n_blocks + 7]
        c_ref, out_ref, delta_ref = refs[n_blocks + 7 : n_blocks + 10]
        c_v, x_v, pre_v, out_v, side, stack, columns, router_v, c_sems, x_sems, side_sems, stack_sems, out_sems = refs[
            n_blocks + 10 :
        ]
        places = [c_v.at[pl.ds(k * block_rows, block_rows), :] for k in range(seq_n)]
        arrivals.start(blocks, places, c_sems)
        chunks = [side_copies(gate_ref, up_ref, side, side_sems, pack, j, width) for j in range(STEPS)]
        downs = down_copies(down_ref, stack, stack_sems, pack)
        x_copy = pltpu.make_async_copy(x_ref, x_v, x_sems.at[0])
        pre_copy = pltpu.make_async_copy(pre_ref, pre_v, x_sems.at[1])
        for copy in downs + [pre_copy] + sum(chunks, []) + [x_copy]:
            copy.start()
        arrivals.wait(blocks, places, c_sems)
        leaving = [pltpu.make_async_copy(c_v, c_ref, out_sems.at[STEPS])]
        leaving[0].start()
        for copy in downs:
            copy.wait()
        both = mm(c_v[...], stack[...], LAST)
        parts = [both[:, h * hidden_n : (h + 1) * hidden_n] for h in range(pack)]
        pre_copy.wait()
        raw = jnp.where(first_part(rows, pack, slots), fold(parts, slots) * scale_ref[...], 0.0)
        gate = pre_v[:, :hidden_n]
        up = pre_v[:, hidden_n : 2 * hidden_n]
        g = pre_v[:, 2 * hidden_n : 2 * hidden_n + 1]
        sig = jax.nn.sigmoid(gate)
        act = gate * sig
        score = jnp.sum(act * up * raw, axis=1, keepdims=True) * g * (1.0 - g)
        grad = raw * g
        to_gate = spread(grad * up * sig * (1.0 + gate * (1.0 - sig)), pack, slots)
        to_up = spread(grad * act, pack, slots)
        expert = lax.axis_index("exp")
        lane = lax.broadcasted_iota(jnp.int32, (rows, LANES), 1)
        by_expert = jnp.zeros((rows, LANES), F32)
        by_split = jnp.zeros((rows, LANES), F32)
        for h, value in enumerate(spread(jnp.broadcast_to(score, (rows, LANES)), pack, slots)):
            delta_ref[:, 2 * h * hidden_n : (2 * h + 1) * hidden_n] = to_gate[h].astype(BF16)
            delta_ref[:, (2 * h + 1) * hidden_n : (2 * h + 2) * hidden_n] = to_up[h].astype(BF16)
            for n, piece in enumerate(split3(value)):
                piece = piece.astype(F32)
                by_split = jnp.where(lane == 3 * h + n, piece, by_split)
                if n < 2:
                    by_expert = jnp.where(lane == (n * pack + h) * exp_n + expert, piece, by_expert)
        columns[...] = by_split.astype(BF16)
        by_expert = by_expert.astype(BF16)
        router_v[...] = router_rows(router_ref, pack, 2, LANES)
        for j, chunk in enumerate(chunks):
            for copy in chunk:
                copy.wait()
            now = slice(j * width, (j + 1) * width)
            put_blocks((mm(delta_ref[...], side[now, :], LAST) + mm(by_expert, router_v[:, now])).astype(BF16), out_v, now)
            if j + 1 < STEPS:
                now = pl.ds(j * width, width)
                leaving.append(pltpu.make_async_copy(out_v.at[:, :, now], out_ref.at[:, :, now], out_sems.at[j]))
                leaving[-1].start()

        here = lax.axis_index("seq")
        x_copy.wait()
        told = mm(columns[...], x_v[...], ROWS)
        sub = lax.broadcasted_iota(jnp.int32, (group, LANES), 0)
        lane = lax.broadcasted_iota(jnp.int32, (group, LANES), 1)
        minus = jnp.broadcast_to(-jnp.sum(score, axis=0, keepdims=True), (group, LANES))
        pieces = [piece.astype(F32) for piece in split3(minus)]
        threshold_row = jnp.zeros((group, LANES), F32)
        for n, piece in enumerate(pieces):
            threshold_row = jnp.where(lane == n, piece, threshold_row)
        rides = {}
        for owner in range(seq_n * exp_n):
            h, first = divmod(owner * per, part)
            shift = first % LANES
            value = jnp.sum(told[3 * h : 3 * h + 3, first - shift : first - shift + LANES], axis=0, keepdims=True)
            value = jnp.broadcast_to(value, (group, LANES))
            if shift:
                value = pltpu.roll(value, LANES - shift, 1)
            if per < LANES:
                value = jnp.where(lane < per, value, 0.0)
            d, place = divmod(owner, exp_n)
            for t in range(extra // LANES):
                row = sub + t * group
                pieces = rides.setdefault((d, t), [])
                pieces.append(jnp.where(row == 2 * here, value, jnp.where(row == 2 * here + 1, threshold_row, 0.0)))
                if place == exp_n - 1:
                    now = slice(part + t * LANES, part + (t + 1) * LANES)
                    out_v[d, :, now] = jnp.concatenate(pieces).astype(BF16)
        now = pl.ds((STEPS - 1) * width, width + extra)
        leaving.append(pltpu.make_async_copy(out_v.at[:, :, now], out_ref.at[:, :, now], out_sems.at[STEPS - 1]))
        leaving[-1].start()
        for copy in leaving:
            copy.wait()

    return pl.pallas_call(
        body,
        in_specs=[ANYWHERE] * (n_blocks + 5) + [IN_VMEM] * 2,
        out_specs=[ANYWHERE] * 2 + [IN_VMEM],
        out_shape=[
            shape((rows, part)),
            shape((seq_n, block_rows, part + extra)),
            shape((rows, total)),
        ],
        scratch_shapes=[
            pltpu.VMEM((rows, part), BF16),
            pltpu.VMEM((rows, part), BF16),
            pltpu.VMEM(pre.shape, F32),
            pltpu.VMEM((seq_n, block_rows, part + extra), BF16),
            pltpu.VMEM((part, total), BF16),
            pltpu.VMEM((pack * hidden_n, part), BF16),
            pltpu.VMEM((rows, LANES), BF16),
            pltpu.VMEM((LANES, part), BF16),
            pltpu.SemaphoreType.DMA((seq_n,)),
            pltpu.SemaphoreType.DMA((2,)),
            pltpu.SemaphoreType.DMA((STEPS, 2 * pack)),
            pltpu.SemaphoreType.DMA((pack,)),
            pltpu.SemaphoreType.DMA((STEPS + 1,)),
        ],
        compiler_params=PARAMS,
        cost_estimate=cost(100 * rows * part * pack * hidden_n, 100 * part * pack * hidden_n),
    )(*to_hbm(*arrivals.blocks, w_gate, w_up, w_down, x, pre), router_t, hid_scale)


def side_grads(x, delta, pack, hidden_n):
    rows, part = x.shape
    width = part // STEPS

    def body(x_ref, delta_ref, gate_out, up_out):
        for h in range(pack):
            both = mm(x_ref[...], delta_ref[:, 2 * h * hidden_n : 2 * (h + 1) * hidden_n], ROWS)
            gate_out[h] = both[:, :hidden_n]
            up_out[h] = both[:, hidden_n:]

    tall = pl.BlockSpec((pack, width, hidden_n), lambda i: (0, i, 0))
    gate, up = pl.pallas_call(
        body,
        grid=(STEPS,),
        in_specs=[
            pl.BlockSpec((rows, width), lambda i: (0, i)),
            pl.BlockSpec(delta.shape, lambda i: (0, 0)),
        ],
        out_specs=[tall, tall],
        out_shape=[shape((pack, part, hidden_n), F32)] * 2,
        compiler_params=PARAMS,
        cost_estimate=cost(4 * rows * part * pack * hidden_n, 8 * part * pack * hidden_n),
    )(*to_hbm(x, delta))
    return gate.reshape(1, part * pack, hidden_n), up.reshape(1, part * pack, hidden_n)


def down_grads(c, hidden, pack, hidden_n):
    rows, part = c.shape
    width = part // 2

    def body(c_ref, hidden_ref, out):
        out[...] = mm(hidden_ref[...], c_ref[...], ROWS)

    return pl.pallas_call(
        body,
        grid=(pack, 2),
        in_specs=[
            pl.BlockSpec((rows, width), lambda h, i: (0, i)),
            pl.BlockSpec((rows, hidden_n), lambda h, i: (0, h)),
        ],
        out_specs=pl.BlockSpec((None, hidden_n, width), lambda h, i: (0, 0, h * 2 + i)),
        out_shape=shape((1, hidden_n, part * pack), F32),
        compiler_params=PARAMS,
        cost_estimate=cost(2 * rows * part * pack * hidden_n, 4 * part * pack * hidden_n),
    )(*to_hbm(c, hidden))


def up_line(block, n, first=0, last=None):
    last = n - 1 if last is None else last
    return lax.ppermute(block, "seq", [(s, s + 1) for s in range(first, last)])


def down_line(block, n, first=1, last=None):
    last = n if last is None else last
    return lax.ppermute(block, "seq", [(s, s - 1) for s in range(first, last)])


def line_gather(block, n):
    ups, downs = [], []
    up = down = block
    for j in range(1, n):
        up = up_line(up, n, j - 1)
        down = down_line(down, n, 1, n - j + 1)
        ups.append(up)
        downs.append(down)
    plan = [(0, 0, 0)] + [(k, 2 * n - 1 - k, k) for k in range(1, n)]
    return Arrivals([block] + ups + downs, plan)


def on_device(tokens, cotangent, router, threshold, w_gate, w_up, w_down, hid_scale, picks, counts):
    experts, slots = picks.shape[1:]
    features = tokens.shape[1]
    true_hidden = w_gate.shape[2]
    extra = -true_hidden % LANES
    if extra:
        w_gate, w_up = (jnp.pad(w, ((0, 0), (0, 0), (0, extra))) for w in (w_gate, w_up))
        w_down = jnp.pad(w_down, ((0, 0), (0, extra), (0, 0)))
        hid_scale = jnp.pad(hid_scale, ((0, 0), (0, extra)))
    hidden_n = true_hidden + extra
    seq_n = lax.axis_size("seq")
    exp_n = lax.axis_size("exp")
    everyone = seq_n * exp_n
    pack = max(1, 8 // slots)
    chosen = picks[0].T

    def to_owners(parts):
        parts = parts.reshape(everyone, -1, parts.shape[2])
        return lax.all_to_all(parts, BOTH, split_axis=0, concat_axis=0, tiled=True).reshape(-1, parts.shape[2])

    sent, hot = choose_rows(tokens, cotangent, chosen, counts, pack)
    sent = sent.reshape(experts, 2, -1, sent.shape[1])
    here = lax.all_to_all(sent, "exp", split_axis=0, concat_axis=0, tiled=True)
    x_in, c_in = (line_gather(here[:, n].reshape(-1, here.shape[3]), seq_n) for n in range(2))
    router_t = router.T

    x, out, pre, hidden = expert_forward(
        x_in, seq_n, slots, experts, pack, router_t, threshold, w_gate, w_up, w_down, hid_scale
    )
    out = to_owners(out)
    c, back, delta = expert_backward(
        c_in, seq_n, exp_n, slots, pack, x, pre, router_t, w_gate, w_up, w_down, hid_scale
    )
    back, out = lax.optimization_barrier((back, out))
    back = to_owners(back)
    down_grad = down_grads(c, hidden, pack, hidden_n)
    gate_grad, up_grad = side_grads(x, delta, pack, hidden_n)
    (mixture,) = scatter_rows(out, hot, seq_n)
    token_grad, router_grad, threshold_grad = scatter_rows(back, hot, seq_n, (features // everyone, experts))
    if extra:
        gate_grad, up_grad = gate_grad[:, :, :true_hidden], up_grad[:, :, :true_hidden]
        down_grad = down_grad[:, :true_hidden]
    return mixture, token_grad, router_grad.T, threshold_grad[0], gate_grad, up_grad, down_grad


def solution(mesh):
    by_owner = P(BOTH, None)
    columns = P("exp", None, "seq")
    down = P("exp", "seq", None)
    return jax.shard_map(
        on_device,
        mesh=mesh,
        in_specs=(
            by_owner,
            by_owner,
            P(),
            P(),
            columns,
            columns,
            down,
            P("exp", "seq"),
            P(BOTH, None, None),
            by_owner,
        ),
        out_specs=(by_owner, by_owner, by_owner, P(), columns, columns, down),
        check_vma=False,
    )
```
